32 devices in a mesh: dp: 16 (over z, x, core), tensor: 2 (over y).
Axes of the slice: x: 2, y: 2, z: 4, core: 2. Of those that a mesh axis runs over, the one named last changes fastest.
Arguments:
- tokens_in: bfloat16 [16, 256, 2048], P('dp'), may hold values from -6 to 6
- segment_ids: int32 [16, 256], P('dp'), may hold values from 0 to 3, never falling along the last dimension, each value on 1 to 128 neighbouring positions
- d_out: bfloat16 [16, 256, 2048], P('dp'), may hold values from -6 to 6
- qkv_weight: float32 [2048, 3, 2048], P('dp', None, 'tensor'), may hold values from -0.125 to 0.125
- qkv_bias: float32 [2, 3072], P('tensor', 'dp'), may hold values from -1.8 to 1.8
- out_weight: float32 [2048, 2048], P('tensor', 'dp'), may hold values from -0.5 to 0.5
- gating_weight: float32 [2048, 2, 5632], P('dp', None, 'tensor'), may hold values from -0.125 to 0.125
- down_weight: float32 [5632, 2048], P('tensor', 'dp'), may hold values from -0.078125 to 0.078125
- norm_params: float32 [4, 2048], P(None, 'dp'), may hold values from -1.2 to 1.5, as said below
- qkv_first: float32 [2048, 3, 2048], P('dp', None, 'tensor'), may hold values from -80 to 80
- qkv_second: float32 [2048, 3, 2048], P('dp', None, 'tensor'), may hold values from 860.16 to 3440.64
- bias_first: float32 [2, 3072], P('tensor', 'dp'), may hold values from -80 to 80
- bias_second: float32 [2, 3072], P('tensor', 'dp'), may hold values from 860.16 to 3440.64
- out_first: float32 [2048, 2048], P('tensor', 'dp'), may hold values from -16 to 16
- out_second: float32 [2048, 2048], P('tensor', 'dp'), may hold values from 34.4064 to 139.264
- gating_first: float32 [2048, 2, 5632], P('dp', None, 'tensor'), may hold values from -16 to 16
- gating_second: float32 [2048, 2, 5632], P('dp', None, 'tensor'), may hold values from 26.2144 to 106.496
- down_first: float32 [5632, 2048], P('tensor', 'dp'), may hold values from -24 to 24
- down_second: float32 [5632, 2048], P('tensor', 'dp'), may hold values from 77.824 to 311.296
- norm_first: float32 [4, 2048], P(None, 'dp'), may hold values from -64 to 64
- norm_second: float32 [4, 2048], P(None, 'dp'), may hold values from 491.52 to 1925.12
Outputs:
- block_out: float32 [16, 256, 2048], P('dp')
- input_grad: float32 [16, 256, 2048], P('dp')
- qkv_updated: float32 [2048, 3, 2048], P('dp', None, 'tensor')
- qkv_mean: float32 [2048, 3, 2048], P('dp', None, 'tensor')
- qkv_square: float32 [2048, 3, 2048], P('dp', None, 'tensor')
- bias_updated: float32 [2, 3072], P('tensor', 'dp')
- bias_mean: float32 [2, 3072], P('tensor', 'dp')
- bias_square: float32 [2, 3072], P('tensor', 'dp')
- out_updated: float32 [2048, 2048], P('tensor', 'dp')
- out_mean: float32 [2048, 2048], P('tensor', 'dp')
- out_square: float32 [2048, 2048], P('tensor', 'dp')
- gating_updated: float32 [2048, 2, 5632], P('dp', None, 'tensor')
- gating_mean: float32 [2048, 2, 5632], P('dp', None, 'tensor')
- gating_square: float32 [2048, 2, 5632], P('dp', None, 'tensor')
- down_updated: float32 [5632, 2048], P('tensor', 'dp')
- down_mean: float32 [5632, 2048], P('tensor', 'dp')
- down_square: float32 [5632, 2048], P('tensor', 'dp')
- norm_updated: float32 [4, 2048], P(None, 'dp')
- norm_mean: float32 [4, 2048], P(None, 'dp')
- norm_square: float32 [4, 2048], P(None, 'dp')
The draws below stay inside these ranges and needn't reach their ends.
Inputs may be any that keep to these rules, and one draw needn't show every extreme that they name: `segment_ids`: along each sequence the ids never fall; a document holds 1 to 128 tokens, and some document holds exactly 128. `norm_params`: rows 0 and 2 lie between 0.5 and 1.5, rows 1 and 3 between -1.2 and 1.2.
All inputs are finite; a program needn't handle non-finite values.
Results may differ from the reference program's by a relative error of at most 0.014.
Values may be sent and summed in bfloat16 or wider, within the bound.
A program may use at most 320 MiB of HBM per device.

```python
import math
import jax
import jax.numpy as jnp
import numpy as np
from jax import lax

D = 2048
H = 32
HD = 64
ROT = 16
FF = 5632
SEQ = 256
STEP = 10
SEQS = 16
QKVB = 3072
N_TENSOR = 2


def draw_norm_params(key, part):
    key = jax.random.fold_in(key, 11)
    gain_key, shift_key = jax.random.split(key)
    gains = jax.random.uniform(gain_key, (2, D), jnp.float32, 0.5, 1.5)
    shifts = jnp.clip(0.3 * jax.random.normal(shift_key, (2, D), jnp.float32), -1.2, 1.2)
    return jnp.stack([gains[0], shifts[0], gains[1], shifts[1]])


def shard_levels(rng, extent, cuts, smallest, largest):
    loudness, own = 1.0, jax.random.fold_in(rng, 6)
    for dim, blocks in cuts:
        draws = jnp.exp(jax.random.uniform(jax.random.fold_in(own, dim), (blocks,), jnp.float32, smallest / len(cuts), largest / len(cuts)))
        loudness = loudness * jnp.repeat(draws, extent[dim] // blocks).reshape([-1 if axis == dim else 1 for axis in range(len(extent))])
    return loudness


def length_profile(number_of, total, bound, skew):
    loads = [(1 << 20) // math.isqrt(rank ** skew) + 1 for rank in range(2, number_of + 1)]
    rest, given = total - bound - (number_of - 1), [1] * (number_of - 1)
    while rest > 0:
        candidates = [i for i in range(number_of - 1) if given[i] < bound]
        pool, budget = sum([loads[i] for i in candidates]), rest
        for i in candidates:
            addition = min(bound - given[i], max(1, budget * loads[i] // pool), rest)
            given[i] = given[i] + addition
            rest = rest - addition
    return np.array([bound] + given)


def ragged_sizes(stream_key, count, total, most, slope):
    if count == 2:
        one = jax.random.randint(stream_key, (), max(1, total - most), min(most, total - 1) + 1)
        return jnp.stack([one, total - one])
    lengths = jnp.asarray(length_profile(count, total, most, slope), jnp.int32)
    pairs = (count - 1) // 2
    source_of, taker = lengths[1:1 + 2 * pairs:2], lengths[2:2 + 2 * pairs:2]
    margin = jnp.minimum(source_of - 1, most - taker)
    moved = jax.random.randint(jax.random.fold_in(stream_key, 1), (pairs,), 0, 1 << 20) % (margin + 1)
    lengths = lengths.at[1:1 + 2 * pairs:2].set(source_of - moved).at[2:2 + 2 * pairs:2].set(taker + moved)
    return lengths[jax.random.permutation(jax.random.fold_in(stream_key, 2), count)]


def gaussian(own_key, shape, deviation, limit, cuts=(), kind=jnp.bfloat16):
    values = deviation * jax.random.normal(own_key, shape, jnp.float32)
    if cuts:
        values = values * shard_levels(own_key, shape, cuts, -0.22, 0.18)
    return jnp.clip(values, -limit, limit).astype(kind)


def setup_inputs(seed: int = 0) -> dict:
    streams_of = jax.random.split(jax.random.key(seed), 22)
    tokens_in = gaussian(streams_of[0], (SEQS, SEQ, D), 1.0, 6.0, ((0, 16),))
    segment_ids = jax.vmap(lambda own: jnp.searchsorted(jnp.cumsum(ragged_sizes(own, 4, SEQ, SEQ // 2, 0)), jnp.arange(SEQ), side="right"))(jax.random.split(streams_of[1], SEQS)).reshape((SEQS, SEQ)).astype(jnp.int32)
    d_out = gaussian(streams_of[2], (SEQS, SEQ, D), 1.0, 6.0, ((0, 16),))
    qkv_weight = gaussian(streams_of[3], (D, 3, H * HD), D ** -0.5, 0.125, ((0, 16), (2, 2)), jnp.float32)
    qkv_bias = gaussian(streams_of[4], (N_TENSOR, QKVB), 0.3, 1.8, ((0, 2), (1, 16)), jnp.float32)
    out_weight = gaussian(streams_of[5], (H * HD, D), (H * HD // 16) ** -0.5, 0.5, ((0, 2), (1, 16)), jnp.float32)
    gating_weight = gaussian(streams_of[6], (D, 2, FF), D ** -0.5, 0.125, ((0, 16), (2, 2)), jnp.float32)
    down_weight = gaussian(streams_of[7], (FF, D), FF ** -0.5, 0.078125, ((0, 2), (1, 16)), jnp.float32)
    norm_params = draw_norm_params(jax.random.fold_in(streams_of[21], 71), 0)
    qkv_first = gaussian(streams_of[9], (D, 3, H * HD), (0.22 * (SEQ * SEQS) ** 0.5), 80.0, ((0, 16), (2, 2)), jnp.float32)
    qkv_second = jnp.clip(jnp.exp(math.log(3440.64) - 1.3862944 * jax.random.uniform(streams_of[10], (D, 3, H * HD), jnp.float32) ** shard_levels(streams_of[10], (D, 3, H * HD), ((0, 16), (2, 2)), -0.2, 0.2)), 860.16, 3440.64)
    bias_first = gaussian(streams_of[11], (N_TENSOR, QKVB), (0.22 * (SEQ * SEQS) ** 0.5), 80.0, ((0, 2), (1, 16)), jnp.float32)
    bias_second = jnp.clip(jnp.exp(math.log(3440.64) - 1.3862944 * jax.random.uniform(streams_of[12], (N_TENSOR, QKVB), jnp.float32) ** shard_levels(streams_of[12], (N_TENSOR, QKVB), ((0, 2), (1, 16)), -0.2, 0.2)), 860.16, 3440.64)
    out_first = gaussian(streams_of[13], (H * HD, D), (0.044 * (SEQ * SEQS) ** 0.5), 16.0, ((0, 2), (1, 16)), jnp.float32)
    out_second = jnp.clip(jnp.exp(math.log(139.264) - 1.3981289 * jax.random.uniform(streams_of[14], (H * HD, D), jnp.float32) ** shard_levels(streams_of[14], (H * HD, D), ((0, 2), (1, 16)), -0.2, 0.2)), 34.4064, 139.264)
    gating_first = gaussian(streams_of[15], (D, 2, FF), (0.039 * (SEQ * SEQS) ** 0.5), 16.0, ((0, 16), (2, 2)), jnp.float32)
    gating_second = jnp.clip(jnp.exp(math.log(106.496) - 1.4017986 * jax.random.uniform(streams_of[16], (D, 2, FF), jnp.float32) ** shard_levels(streams_of[16], (D, 2, FF), ((0, 16), (2, 2)), -0.2, 0.2)), 26.2144, 106.496)
    down_first = gaussian(streams_of[17], (FF, D), (0.067 * (SEQ * SEQS) ** 0.5), 24.0, ((0, 2), (1, 16)), jnp.float32)
    down_second = jnp.clip(jnp.exp(math.log(311.296) - 1.3862944 * jax.random.uniform(streams_of[18], (FF, D), jnp.float32) ** shard_levels(streams_of[18], (FF, D), ((0, 2), (1, 16)), -0.2, 0.2)), 77.824, 311.296)
    norm_first = gaussian(streams_of[19], (4, D), (0.17 * (SEQ * SEQS) ** 0.5), 64.0, ((1, 16),), jnp.float32)
    norm_second = jnp.clip(jnp.exp(math.log(1925.12) - 1.36524097 * jax.random.uniform(streams_of[20], (4, D), jnp.float32) ** shard_levels(streams_of[20], (4, D), ((1, 16),), -0.2, 0.2)), 491.52, 1925.12)
    return {"tokens_in": tokens_in, "segment_ids": segment_ids, "d_out": d_out, "qkv_weight": qkv_weight, "qkv_bias": qkv_bias, "out_weight": out_weight, "gating_weight": gating_weight, "down_weight": down_weight, "norm_params": norm_params, "qkv_first": qkv_first, "qkv_second": qkv_second, "bias_first": bias_first, "bias_second": bias_second, "out_first": out_first, "out_second": out_second, "gating_first": gating_first, "gating_second": gating_second, "down_first": down_first, "down_second": down_second, "norm_first": norm_first, "norm_second": norm_second}


@jax.custom_vjp
def low(v):
    return lax.optimization_barrier(v.astype(jnp.bfloat16)).astype(jnp.float32)

@jax.custom_vjp
def low_back(v):
    return v

def low_keep(v):
    return (low(v), None)

def low_pass(kept, grad):
    return (grad,)

def back_keep(v):
    return (v, None)

def back_low(kept, grad):
    return (low(grad),)
low.defvjp(low_keep, low_pass)
low_back.defvjp(back_keep, back_low)

def layer_norm(values, scale_row, shift_row):
    centre = values - lax.optimization_barrier(jnp.mean(values, axis=-1, keepdims=True))
    spread = lax.optimization_barrier(jnp.mean(centre * centre, axis=-1, keepdims=True))
    return centre * lax.rsqrt(spread + 1e-05) * scale_row + shift_row

def doc_positions(segments):
    seq_len = segments.shape[-1]
    earlier = lax.optimization_barrier(jnp.sum((segments[None, :] < segments[:, None]).astype(jnp.int32), axis=1))
    return (jnp.arange(seq_len, dtype=jnp.int32) - earlier).astype(jnp.float32)

def rotary_tables(positions):
    half_rot = ROT // 2
    frequency = 10000.0 ** (-2.0 * jnp.arange(half_rot, dtype=jnp.float32) / ROT)
    angles = positions[:, None] * frequency[None, :]
    return (jnp.cos(angles), jnp.sin(angles))

def rotate(values, cosine, sine_part):
    half_rot = ROT // 2
    first_half = values[..., :half_rot]
    second = values[..., half_rot:ROT]
    cos_wide = cosine[:, None, :]
    sin_wide = sine_part[:, None, :]
    return jnp.concatenate([first_half * cos_wide - second * sin_wide, second * cos_wide + first_half * sin_wide, values[..., ROT:]], axis=-1)

def sequence_attention(block_in):
    projected, segments = block_in
    seq_len = segments.shape[0]
    head_width = H * HD
    cosine, sine_part = rotary_tables(doc_positions(segments))
    query_rot = low(rotate(projected[:, :head_width].reshape(seq_len, H, HD), cosine, sine_part))
    key_rot = low(rotate(projected[:, head_width:2 * head_width].reshape(seq_len, H, HD), cosine, sine_part))
    values = low(projected[:, 2 * head_width:].reshape(seq_len, H, HD))
    token_order = jnp.arange(seq_len)
    allowed = (segments[:, None] == segments[None, :]) & (token_order[:, None] >= token_order[None, :])
    raw_scores = jnp.einsum('qhd,khd->hqk', query_rot, key_rot, precision=lax.Precision.HIGHEST) * HD ** (-0.5)
    scores = low_back(jnp.where(allowed[None], raw_scores, -1e+30))
    row_top = lax.optimization_barrier(jnp.max(scores, axis=-1, keepdims=True))
    weights = jnp.exp(scores - row_top)
    probability = weights / lax.optimization_barrier(jnp.sum(weights, axis=-1, keepdims=True))
    attended = jnp.einsum('hqk,khd->qhd', low(probability), values, precision=lax.Precision.HIGHEST)
    return attended.reshape(seq_len, head_width)

def forward(params, tokens, segments):
    qkv_w, bias_w, out_w, gating_w, down_w, norm_w = [low(weight_in) for weight_in in params]
    model_width = tokens.shape[2]
    head_width = H * HD
    bias_flat = bias_w.reshape(N_TENSOR, 3, head_width // N_TENSOR).transpose(1, 0, 2).reshape(3 * head_width)
    normed_one = low(layer_norm(tokens, norm_w[0], norm_w[1]))
    projected = low_back(jnp.einsum('gsd,dc->gsc', normed_one, qkv_w.reshape(model_width, 3 * head_width), precision=lax.Precision.HIGHEST) + bias_flat)
    attended = lax.map(jax.checkpoint(sequence_attention), (projected, segments))
    attn_in = low(low_back(attended))
    residual = tokens + low_back(jnp.einsum('gsc,cd->gsd', attn_in, out_w, precision=lax.Precision.HIGHEST))
    normed_two = low(layer_norm(residual, norm_w[2], norm_w[3]))
    gated_out = low_back(jnp.einsum('gsd,dc->gsc', normed_two, gating_w.reshape(model_width, 2 * FF), precision=lax.Precision.HIGHEST))
    hidden = low(jax.nn.silu(gated_out[..., :FF]) * gated_out[..., FF:])
    return residual + low_back(jnp.einsum('gsf,fd->gsd', hidden, down_w, precision=lax.Precision.HIGHEST))

def adamw_update(weight_old, gradient, first_old, second_old, step_rate, decay_rate):
    first_new = 0.9 * first_old + 0.1 * gradient
    second_new = 0.95 * second_old + 0.05 * gradient * gradient
    corrected = first_new / (1.0 - 0.9 ** STEP) / (jnp.sqrt(second_new / (1.0 - 0.95 ** STEP)) + 1e-08)
    return (weight_old - step_rate * (corrected + decay_rate * weight_old), first_new, second_new)

def reference(tokens_in, segment_ids, d_out, qkv_weight, qkv_bias, out_weight, gating_weight, down_weight, norm_params, qkv_first, qkv_second, bias_first, bias_second, out_first, out_second, gating_first, gating_second, down_first, down_second, norm_first, norm_second):
    params = (qkv_weight, qkv_bias, out_weight, gating_weight, down_weight, norm_params)
    group_size = math.gcd(SEQS, max(1, 4096 // SEQ))
    group_count = SEQS // group_size

    def grouped(stacked):
        return stacked.reshape((group_count, group_size) + stacked.shape[1:])

    def scan_step(grad_sum, block_in):
        tokens_blk, segments_blk, cotangent_blk = block_in

        def run_forward(weights_in, tokens_inner):
            return forward(weights_in, tokens_inner, segments_blk)
        result_blk, pull_back = jax.vjp(run_forward, params, tokens_blk.astype(jnp.float32))
        weight_grads, token_grad = pull_back(cotangent_blk.astype(jnp.float32))
        return (jax.tree.map(jnp.add, grad_sum, weight_grads), (result_blk, token_grad))
    zeros_init = jax.tree.map(jnp.zeros_like, params)
    grad_total, (block_out, input_grad) = lax.scan(scan_step, zeros_init, (grouped(tokens_in), grouped(segment_ids), grouped(d_out)))
    grad_qkv, grad_bias, grad_out, grad_gating, grad_down, grad_norm = grad_total
    qkv_updated, qkv_mean, qkv_square = adamw_update(qkv_weight, grad_qkv, qkv_first, qkv_second, D ** (-0.5), 0.1)
    bias_updated, bias_mean, bias_square = adamw_update(qkv_bias, grad_bias, bias_first, bias_second, 0.3, 0.0)
    out_updated, out_mean, out_square = adamw_update(out_weight, grad_out, out_first, out_second, (H * HD // 16) ** (-0.5), 0.1)
    gating_updated, gating_mean, gating_square = adamw_update(gating_weight, grad_gating, gating_first, gating_second, D ** (-0.5), 0.1)
    down_updated, down_mean, down_square = adamw_update(down_weight, grad_down, down_first, down_second, FF ** (-0.5), 0.1)
    norm_updated, norm_mean, norm_square = adamw_update(norm_params, grad_norm, norm_first, norm_second, 0.25, 0.0)
    return (block_out.reshape(SEQS, SEQ, D), input_grad.reshape(SEQS, SEQ, D), qkv_updated, qkv_mean, qkv_square, bias_updated, bias_mean, bias_square, out_updated, out_mean, out_square, gating_updated, gating_mean, gating_square, down_updated, down_mean, down_square, norm_updated, norm_mean, norm_square)
```

```python
import functools

import jax
import jax.numpy as jnp
from jax import lax
from jax.experimental import pallas as pl
from jax.experimental.pallas import tpu as pltpu
from jax.sharding import PartitionSpec as P

D = 2048
H = 32
HD = 64
ROT = 16
FF = 5632
STEP = 10
TP = 4

F32 = jnp.float32
BF16 = jnp.bfloat16


def layer_norm(values, scale_row, shift_row):
    centre = values - jnp.mean(values, axis=-1, keepdims=True)
    spread = jnp.mean(centre * centre, axis=-1, keepdims=True)
    inverse = lax.rsqrt(spread + 1e-05)
    scaled = centre * inverse
    return (scaled * scale_row + shift_row, scaled, inverse)


def norm_back(grad_in, scaled, inverse, scale_row):
    grad_scaled = grad_in * scale_row
    mean_first = jnp.mean(grad_scaled, axis=-1, keepdims=True)
    mean_second = jnp.mean(grad_scaled * scaled, axis=-1, keepdims=True)
    grad_values = inverse * (grad_scaled - mean_first - scaled * mean_second)
    return (grad_values, jnp.sum(grad_in * scaled, axis=0), jnp.sum(grad_in, axis=0))


def adamw_update(weight_old, gradient, first_old, second_old, step_rate, decay_rate):
    first_new = 0.9 * first_old + 0.1 * gradient
    second_new = 0.95 * second_old + 0.05 * gradient * gradient
    corrected = first_new / (1.0 - 0.9**STEP) / (jnp.sqrt(second_new / (1.0 - 0.95**STEP)) + 1e-08)
    return (weight_old - step_rate * (corrected + decay_rate * weight_old), first_new, second_new)


def dot(a, b, ca, cb):
    return lax.dot_general(a, b, (((ca,), (cb,)), ((), ())), preferred_element_type=F32)


def spin(values, cos_t, lower_t, upper_t):
    wide = values.shape[1]
    return (
        values * cos_t
        + pltpu.roll(values, wide - ROT // 2, 1) * lower_t
        + pltpu.roll(values, ROT // 2, 1) * upper_t
    )


def spin_back(values, cos_t, lower_t, upper_t):
    wide = values.shape[1]
    return (
        values * cos_t
        + pltpu.roll(values * lower_t, ROT // 2, 1)
        + pltpu.roll(values * upper_t, wide - ROT // 2, 1)
    )


def mask_of(seg_col, seg_row, size):
    rows = lax.broadcasted_iota(jnp.int32, (size, size), 0)
    cols = lax.broadcasted_iota(jnp.int32, (size, size), 1)
    return (seg_col == seg_row) & (cols <= rows)


def attend_kernel(proj_ref, bias_ref, cos_ref, low_ref, upp_ref, col_ref, row_ref, qkv_ref, out_ref):
    size, wide = out_ref.shape
    proj = proj_ref[...] + bias_ref[...]
    cos_t, low_t, upp_t = cos_ref[...], low_ref[...], upp_ref[...]
    query = spin(proj[:, :wide], cos_t, low_t, upp_t).astype(BF16)
    key = spin(proj[:, wide : 2 * wide], cos_t, low_t, upp_t).astype(BF16)
    value = proj[:, 2 * wide :].astype(BF16)
    qkv_ref[:, :wide] = query
    qkv_ref[:, wide : 2 * wide] = key
    qkv_ref[:, 2 * wide :] = value
    allowed = mask_of(col_ref[...], row_ref[...], size)
    head_of = lax.broadcasted_iota(jnp.int32, (size, wide), 1) // HD
    total = jnp.zeros((size, wide), F32)
    for head in range(wide // HD):
        mine = head_of == head
        scores = dot(jnp.where(mine, query, jnp.zeros_like(query)), key, 1, 1) * HD ** (-0.5)
        scores = jnp.where(allowed, scores, -1e30)
        weights = jnp.exp(scores - jnp.max(scores, axis=1, keepdims=True))
        prob = weights / jnp.sum(weights, axis=1, keepdims=True)
        total = jnp.where(mine, dot(prob.astype(BF16), value, 1, 0), total)
    out_ref[...] = total.astype(BF16)


def attend_back_kernel(qkv_ref, do_ref, cos_ref, low_ref, upp_ref, col_ref, row_ref, dp_ref, sum_ref):
    size, wide = do_ref.shape
    query, key, value = qkv_ref[:, :wide], qkv_ref[:, wide : 2 * wide], qkv_ref[:, 2 * wide :]
    grad = do_ref[...]
    allowed = mask_of(col_ref[...], row_ref[...], size)
    head_of = lax.broadcasted_iota(jnp.int32, (size, wide), 1) // HD
    zero = jnp.zeros_like(query)
    dq = jnp.zeros((size, wide), F32)
    dk = jnp.zeros((size, wide), F32)
    dv = jnp.zeros((size, wide), F32)
    for head in range(wide // HD):
        mine = head_of == head
        query_h = jnp.where(mine, query, zero)
        grad_h = jnp.where(mine, grad, zero)
        scores = dot(query_h, key, 1, 1) * HD ** (-0.5)
        scores = jnp.where(allowed, scores, -1e30)
        weights = jnp.exp(scores - jnp.max(scores, axis=1, keepdims=True))
        prob = weights / jnp.sum(weights, axis=1, keepdims=True)
        dv = dv + dot(prob.astype(BF16), grad_h, 0, 0)
        dprob = dot(grad_h, value, 1, 1)
        delta = jnp.sum(prob * dprob, axis=1, keepdims=True)
        dscore = (prob * (dprob - delta)).astype(BF16)
        dq = jnp.where(mine, dot(dscore, key, 1, 0), dq)
        dk = dk + dot(dscore, query_h, 0, 0)
    cos_t, low_t, upp_t = cos_ref[...], low_ref[...], upp_ref[...]
    dq = spin_back(dq * HD ** (-0.5), cos_t, low_t, upp_t).astype(BF16)
    dk = spin_back(dk * HD ** (-0.5), cos_t, low_t, upp_t).astype(BF16)
    dv = dv.astype(BF16)
    dp_ref[:, :wide] = dq
    dp_ref[:, wide : 2 * wide] = dk
    dp_ref[:, 2 * wide :] = dv
    for part, grad_p in enumerate((dq, dk, dv)):
        sum_ref[0, :, part * wide : (part + 1) * wide] = jnp.sum(
            grad_p.astype(F32), axis=0, keepdims=True
        )


def row_blocks(size, wide):
    return pl.BlockSpec((size, wide), lambda i: (i, 0))


def attend(proj, bias, tables, seg_col, seg_row, seqs, size, wide):
    return pl.pallas_call(
        attend_kernel,
        grid=(seqs,),
        in_specs=[
            row_blocks(size, 3 * wide),
            pl.BlockSpec((1, 3 * wide), lambda i: (0, 0)),
            row_blocks(size, wide),
            row_blocks(size, wide),
            row_blocks(size, wide),
            row_blocks(size, 1),
            pl.BlockSpec((None, 1, size), lambda i: (i, 0, 0)),
        ],
        out_specs=[row_blocks(size, 3 * wide), row_blocks(size, wide)],
        out_shape=[
            jax.ShapeDtypeStruct((seqs * size, 3 * wide), BF16),
            jax.ShapeDtypeStruct((seqs * size, wide), BF16),
        ],
        cost_estimate=pl.CostEstimate(
            flops=seqs * 8 * size * size * wide, bytes_accessed=seqs * size * wide * 32, transcendentals=seqs * size * size * 4
        ),
        name="attend",
    )(proj, bias, *tables, seg_col, seg_row)


def attend_back(qkv, grad, tables, seg_col, seg_row, seqs, size, wide):
    return pl.pallas_call(
        attend_back_kernel,
        grid=(seqs,),
        in_specs=[
            row_blocks(size, 3 * wide),
            row_blocks(size, wide),
            row_blocks(size, wide),
            row_blocks(size, wide),
            row_blocks(size, wide),
            row_blocks(size, 1),
            pl.BlockSpec((None, 1, size), lambda i: (i, 0, 0)),
        ],
        out_specs=[
            row_blocks(size, 3 * wide),
            pl.BlockSpec((1, 1, 3 * wide), lambda i: (i, 0, 0)),
        ],
        out_shape=[
            jax.ShapeDtypeStruct((seqs * size, 3 * wide), BF16),
            jax.ShapeDtypeStruct((seqs, 1, 3 * wide), F32),
        ],
        cost_estimate=pl.CostEstimate(
            flops=seqs * 20 * size * size * wide, bytes_accessed=seqs * size * wide * 32, transcendentals=seqs * size * size * 4
        ),
        name="attend_back",
    )(qkv, grad, *tables, seg_col, seg_row)


class Links:
    def __init__(self, count):
        self.count = count
        self.lines = count // TP
        self.place = lax.axis_index("dp")
        self.tensor = lax.axis_index("tensor")
        self.u = self.place // TP
        self.j = self.place % TP
        self.x = self.j // 2
        self.c = self.j % 2

    def flip(self, values, bit):
        return lax.ppermute(values, "dp", [(i, i ^ bit) for i in range(self.count)])

    def swap(self, values):
        return lax.ppermute(values, "tensor", [(0, 1), (1, 0)])

    def along(self, values, pairs):
        return lax.ppermute(
            values, "dp", [(a * TP + r, b * TP + r) for a, b in pairs for r in range(TP)]
        )

    def pair(self, mine, other, second):
        return jnp.stack([jnp.where(second, other, mine), jnp.where(second, mine, other)])

    def group_gather(self, values):
        two = self.pair(values, self.flip(values, 1), self.c == 1)
        four = self.pair(two, self.flip(two, 2), self.x == 1)
        return four.reshape((TP,) + values.shape)

    def group_swap(self, blocks):
        def block(k):
            return lax.dynamic_index_in_dim(blocks, self.j ^ k, 0, False)

        got = [block(0)] + [self.flip(block(k), k) for k in range(1, TP)]
        odd = self.c == 1
        got = [jnp.where(odd, got[k ^ 1], got[k]) for k in range(TP)]
        odd = self.x == 1
        return jnp.stack([jnp.where(odd, got[k ^ 2], got[k]) for k in range(TP)])

    def line_pieces(self, values):
        n = self.lines
        if n != 4:
            return [
                self.along(values, [(i, (i + k) % n) for i in range(n)]) for k in range(1, n)
            ]
        up = self.along(values, [(0, 1), (1, 2), (2, 3)])
        down = self.along(values, [(3, 2), (2, 1), (1, 0)])
        two = self.along(values, [(0, 2), (1, 3), (2, 0), (3, 1)])
        far = self.along(two, [(2, 3), (1, 0)])
        return [jnp.where(self.u == 0, far, up), two, jnp.where(self.u == 3, far, down)]

    def line_gather(self, values):
        out = jnp.zeros((self.lines,) + values.shape, values.dtype)
        for k, piece in enumerate([values] + self.line_pieces(values)):
            out = lax.dynamic_update_index_in_dim(out, piece, (self.u - k) % self.lines, 0)
        return out

    def line_scatter_sum(self, blocks):
        n = self.lines

        def block(k):
            return lax.dynamic_index_in_dim(blocks, (self.u + k) % n, 0, False)

        total = block(0).astype(F32)
        if n != 4:
            for k in range(1, n):
                total = total + self.along(
                    block(k), [(i, (i + k) % n) for i in range(n)]
                ).astype(F32)
            return total
        outer = jnp.where(self.u == 0, blocks[3], blocks[0])
        far = self.along(outer, [(0, 1), (3, 2)])
        up = self.along(block(1), [(0, 1), (1, 2), (2, 3)])
        down = self.along(block(3), [(3, 2), (2, 1), (1, 0)])
        two = (block(2).astype(F32) + far.astype(F32)).astype(BF16)
        two = self.along(two, [(0, 2), (1, 3), (2, 0), (3, 1)])
        return total + up.astype(F32) + down.astype(F32) + two.astype(F32)

    def line_sum(self, values):
        n = self.lines
        total = values
        for k in range(1, n):
            total = total + self.along(values, [(i, (i + k) % n) for i in range(n)])
        return total

    def scatter_sum(self, partial):
        half = partial.shape[-1] // 2

        def take(values, axis, index):
            return lax.dynamic_index_in_dim(values, index, axis, False)

        other = self.flip(take(partial, 1, 1 - self.c).astype(BF16), 1)
        here = take(partial, 1, self.c) + other.astype(F32)
        left, right = here[..., :half], here[..., half:]
        left = take(left, 0, self.x) + self.flip(take(left, 0, 1 - self.x).astype(BF16), 2).astype(F32)
        right = take(right, 1, self.tensor) + self.swap(
            take(right, 1, 1 - self.tensor).astype(BF16)
        ).astype(F32)
        left = take(left, 0, self.tensor) + self.swap(
            take(left, 0, 1 - self.tensor).astype(BF16)
        ).astype(F32)
        right = take(right, 0, self.x) + self.flip(take(right, 0, 1 - self.x).astype(BF16), 2).astype(F32)
        return jnp.concatenate([left, right], axis=-1)

    def gather(self, values):
        half = values.shape[-1] // 2
        left, right = values[:, :half], values[:, half:]
        left = self.pair(left, self.swap(left), self.tensor == 1)
        left = self.pair(left, self.flip(left, 2), self.x == 1)
        right = self.pair(right, self.flip(right, 2), self.x == 1)
        right_other = self.swap(right)
        second = self.tensor == 1
        right = jnp.stack(
            [jnp.where(second, right_other, right), jnp.where(second, right, right_other)], axis=1
        )
        here = jnp.concatenate([left, right], axis=-1)
        there = self.flip(here, 1)
        second = self.c == 1
        return jnp.stack([jnp.where(second, there, here), jnp.where(second, here, there)], axis=1)


def per_device(
    count,
    tokens_in,
    segment_ids,
    d_out,
    qkv_weight,
    qkv_bias,
    out_weight,
    gating_weight,
    down_weight,
    norm_params,
    qkv_first,
    qkv_second,
    bias_first,
    bias_second,
    out_first,
    out_second,
    gating_first,
    gating_second,
    down_first,
    down_second,
    norm_first,
    norm_second,
):
    links = Links(count)
    rows = norm_params.shape[1]
    seq_len = tokens_in.shape[1]
    head_local = qkv_weight.shape[2]
    hidden_local = gating_weight.shape[2]
    wide = head_local // TP
    hid = hidden_local // TP
    half_seq = seq_len // 2
    group_rows = TP * seq_len

    small = jnp.concatenate(
        [norm_params.astype(BF16).reshape(-1), qkv_bias.astype(BF16).reshape(-1)]
    )
    small = links.line_gather(links.group_gather(small)).reshape(count, -1)
    norm_rows = small[:, : 4 * rows].reshape(count, 4, rows).transpose(1, 0, 2).reshape(4, D).astype(F32)
    bias_full = small[:, 4 * rows :].reshape(3, TP, wide)
    bias_row = lax.dynamic_index_in_dim(bias_full, links.j, 1, False).reshape(1, 3 * wide).astype(F32)

    tokens = links.group_gather(tokens_in[0])
    segments = links.group_gather(segment_ids[0])

    def weight_chunk(shard):
        blocks = shard.astype(BF16).transpose(1, 0, 2)
        return links.group_swap(blocks).reshape(TP * shard.shape[0], shard.shape[2])

    qkv_blocks = qkv_weight.reshape(rows, 3, TP, wide).transpose(0, 2, 1, 3).reshape(rows, TP, 3 * wide)
    out_blocks = out_weight.T.reshape(rows, TP, wide)
    gating_blocks = gating_weight.reshape(rows, 2, TP, hid).transpose(0, 2, 1, 3).reshape(rows, TP, 2 * hid)
    down_blocks = down_weight.T.reshape(rows, TP, hid)
    qkv_matrix = links.line_gather(weight_chunk(qkv_blocks)).reshape(D, 3 * wide)
    out_matrix = links.line_gather(weight_chunk(out_blocks)).reshape(D, wide)
    gating_matrix = links.line_gather(weight_chunk(gating_blocks)).reshape(D, 2 * hid)
    down_matrix = links.line_gather(weight_chunk(down_blocks)).reshape(D, hid)
    cotangent = links.group_gather(d_out[0]).reshape(group_rows, D)

    def own_half(values):
        return lax.dynamic_slice_in_dim(values, links.tensor * half_seq, half_seq, 0)

    earlier = jnp.sum((segments[:, None, :] < segments[:, :, None]).astype(jnp.int32), axis=2)
    positions = (jnp.arange(seq_len, dtype=jnp.int32)[None] - earlier).astype(F32)
    frequency = 10000.0 ** (-2.0 * jnp.arange(ROT // 2, dtype=F32) / ROT)
    angles = positions.reshape(group_rows, 1) * frequency[None, :]
    cosine, sine_part = jnp.cos(angles), jnp.sin(angles)
    zeros = jnp.zeros((group_rows, HD - ROT), F32)
    heads = wide // HD
    tables = (
        jnp.tile(jnp.concatenate([cosine, cosine, zeros + 1.0], axis=1), (1, heads)),
        jnp.tile(jnp.concatenate([-sine_part, jnp.zeros_like(sine_part), zeros], axis=1), (1, heads)),
        jnp.tile(jnp.concatenate([jnp.zeros_like(sine_part), sine_part, zeros], axis=1), (1, heads)),
    )
    seg_col = segments.reshape(group_rows, 1)
    seg_row = segments.reshape(TP, 1, seq_len)

    normed_one, _, _ = layer_norm(tokens.reshape(group_rows, D).astype(F32), norm_rows[0], norm_rows[1])
    normed_one = normed_one.astype(BF16)
    projected = dot(normed_one, qkv_matrix, 1, 0)
    qkv_rot, attended = attend(projected, bias_row, tables, seg_col, seg_row, TP, seq_len, wide)

    def to_parts(partial):
        return partial.reshape(2, 2, 2, half_seq, D)

    attention_term = links.scatter_sum(to_parts(dot(attended, out_matrix, 1, 1)))
    tokens_own = own_half(tokens_in[0]).astype(F32)
    residual = tokens_own + attention_term
    normed_two, scaled_two, inverse_two = layer_norm(residual, norm_rows[2], norm_rows[3])
    normed_two = links.gather(normed_two.astype(BF16)).reshape(group_rows, D)

    gated_out = dot(normed_two, gating_matrix, 1, 0)
    gate_part, up_part = gated_out[:, :hid], gated_out[:, hid:]
    sigmoid_gate = jax.nn.sigmoid(gate_part)
    hidden = (gate_part * sigmoid_gate * up_part).astype(BF16)
    grad_down = dot(cotangent, hidden, 0, 0).astype(BF16)
    down_sum = links.line_scatter_sum(grad_down.reshape(links.lines, TP * rows, hid))
    grad_hidden = dot(cotangent, down_matrix, 1, 0)
    grad_gate = (
        grad_hidden * up_part * sigmoid_gate * (1.0 + gate_part * (1.0 - sigmoid_gate))
    ).astype(BF16)
    grad_up = (grad_hidden * (gate_part * sigmoid_gate)).astype(BF16)
    grad_gated = jnp.concatenate([grad_gate, grad_up], axis=1)
    normed_grad_two = links.scatter_sum(to_parts(dot(grad_gated, gating_matrix, 1, 1)))
    grad_gating = dot(normed_two, grad_gated, 0, 0).astype(BF16)
    gating_sum = links.line_scatter_sum(grad_gating.reshape(links.lines, TP * rows, 2 * hid))

    residual_part, gain_two, shift_two = norm_back(
        normed_grad_two, scaled_two, inverse_two, norm_rows[2]
    )
    residual_grad = own_half(d_out[0]).astype(F32) + residual_part
    residual_low = links.gather(residual_grad.astype(BF16)).reshape(group_rows, D)
    grad_attended = dot(residual_low, out_matrix, 1, 0).astype(BF16)
    grad_out = dot(residual_low, attended, 0, 0).astype(BF16)
    out_sum = links.line_scatter_sum(grad_out.reshape(links.lines, TP * rows, wide))

    feedforward_term = links.scatter_sum(to_parts(dot(hidden, down_matrix, 1, 1)))
    block_own = residual + feedforward_term
    block_out = links.pair(block_own, links.swap(block_own), links.tensor == 1).reshape(seq_len, D)

    grad_projected, bias_sums = attend_back(
        qkv_rot, grad_attended, tables, seg_col, seg_row, TP, seq_len, wide
    )
    grad_qkv = dot(normed_one, grad_projected, 0, 0).astype(BF16)
    qkv_sum = links.line_scatter_sum(grad_qkv.reshape(links.lines, TP * rows, 3 * wide))
    normed_grad_one = links.scatter_sum(to_parts(dot(grad_projected, qkv_matrix, 1, 1)))
    _, scaled_one, inverse_one = layer_norm(tokens_own, norm_rows[0], norm_rows[1])
    input_part, gain_one, shift_one = norm_back(
        normed_grad_one, scaled_one, inverse_one, norm_rows[0]
    )
    input_own = residual_grad + input_part
    input_grad = links.pair(input_own, links.swap(input_own), links.tensor == 1).reshape(seq_len, D)

    norm_small = jnp.concatenate([gain_one, shift_one, gain_two, shift_two])
    norm_small = norm_small + links.swap(norm_small)
    bias_small = jnp.sum(bias_sums, axis=0).reshape(3, 1, wide)
    bias_small = jnp.where(
        lax.broadcasted_iota(jnp.int32, (3, TP, wide), 1) == links.j, bias_small, 0.0
    ).reshape(-1)
    small_grad = jnp.concatenate([norm_small, bias_small])
    small_grad = small_grad + links.flip(small_grad, 1)
    small_grad = small_grad + links.flip(small_grad, 2)
    small_grad = links.line_sum(small_grad)
    norm_grad = lax.dynamic_slice_in_dim(small_grad[: 4 * D].reshape(4, D), links.place * rows, rows, 1)
    bias_here = qkv_bias.shape[1]
    bias_grad = lax.dynamic_slice_in_dim(
        small_grad[4 * D :].reshape(1, -1), links.place * bias_here, bias_here, 1
    )

    def to_owner(total):
        blocks = total.astype(BF16).reshape(TP, rows, total.shape[1])
        return links.group_swap(blocks).transpose(1, 0, 2).astype(F32)

    down_shard = to_owner(down_sum).reshape(rows, hidden_local).T
    gating_shard = (
        to_owner(gating_sum).reshape(rows, TP, 2, hid).transpose(0, 2, 1, 3).reshape(gating_weight.shape)
    )
    out_shard = to_owner(out_sum).reshape(rows, head_local).T
    qkv_shard = (
        to_owner(qkv_sum).reshape(rows, TP, 3, wide).transpose(0, 2, 1, 3).reshape(qkv_weight.shape)
    )
    return (
        block_out[None],
        input_grad[None],
        *adamw_update(qkv_weight, qkv_shard, qkv_first, qkv_second, D ** (-0.5), 0.1),
        *adamw_update(qkv_bias, bias_grad, bias_first, bias_second, 0.3, 0.0),
        *adamw_update(out_weight, out_shard, out_first, out_second, (H * HD // 16) ** (-0.5), 0.1),
        *adamw_update(gating_weight, gating_shard, gating_first, gating_second, D ** (-0.5), 0.1),
        *adamw_update(down_weight, down_shard, down_first, down_second, FF ** (-0.5), 0.1),
        *adamw_update(norm_params, norm_grad, norm_first, norm_second, 0.25, 0.0),
    )


def solution(mesh):
    tokens = P("dp", None, None)
    qkv = P("dp", None, "tensor")
    rest = P("tensor", "dp")
    norm = P(None, "dp")
    weights = (qkv, rest, rest, qkv, rest, norm)
    states = (qkv, qkv, rest, rest, rest, rest, qkv, qkv, rest, rest, norm, norm)
    return jax.shard_map(
        functools.partial(per_device, mesh.shape["dp"]),
        mesh=mesh,
        in_specs=(tokens, P("dp", None), tokens, *weights, *states),
        out_specs=(tokens, tokens, *(spec for spec in weights for _ in range(3))),
        check_vma=False,
    )
```

```python
import functools

import jax
import jax.numpy as jnp
from jax import lax
from jax.experimental import pallas as pl
from jax.experimental.pallas import tpu as pltpu
from jax.sharding import PartitionSpec as P

D = 2048
H = 32
HD = 64
ROT = 16
FF = 5632
STEP = 10
TP = 4

F32 = jnp.float32
BF16 = jnp.bfloat16


def layer_norm(values, scale_row, shift_row):
    centre = values - jnp.mean(values, axis=-1, keepdims=True)
    spread = jnp.mean(centre * centre, axis=-1, keepdims=True)
    inverse = lax.rsqrt(spread + 1e-05)
    scaled = centre * inverse
    return (scaled * scale_row + shift_row, scaled, inverse)


def norm_back(grad_in, scaled, inverse, scale_row):
    grad_scaled = grad_in * scale_row
    mean_first = jnp.mean(grad_scaled, axis=-1, keepdims=True)
    mean_second = jnp.mean(grad_scaled * scaled, axis=-1, keepdims=True)
    grad_values = inverse * (grad_scaled - mean_first - scaled * mean_second)
    return (grad_values, jnp.sum(grad_in * scaled, axis=0), jnp.sum(grad_in, axis=0))


def adamw_update(weight_old, gradient, first_old, second_old, step_rate, decay_rate):
    first_new = 0.9 * first_old + 0.1 * gradient
    second_new = 0.95 * second_old + 0.05 * gradient * gradient
    corrected = first_new / (1.0 - 0.9**STEP) / (jnp.sqrt(second_new / (1.0 - 0.95**STEP)) + 1e-08)
    return (weight_old - step_rate * (corrected + decay_rate * weight_old), first_new, second_new)


def dot(a, b, ca, cb):
    return lax.dot_general(a, b, (((ca,), (cb,)), ((), ())), preferred_element_type=F32)


def spin(values, cos_t, lower_t, upper_t):
    wide = values.shape[1]
    return (
        values * cos_t
        + pltpu.roll(values, wide - ROT // 2, 1) * lower_t
        + pltpu.roll(values, ROT // 2, 1) * upper_t
    )


def spin_back(values, cos_t, lower_t, upper_t):
    wide = values.shape[1]
    return (
        values * cos_t
        + pltpu.roll(values * lower_t, ROT // 2, 1)
        + pltpu.roll(values * upper_t, wide - ROT // 2, 1)
    )


def mask_of(seg_col, seg_row, size):
    rows = lax.broadcasted_iota(jnp.int32, (size, size), 0)
    cols = lax.broadcasted_iota(jnp.int32, (size, size), 1)
    return (seg_col == seg_row) & (cols <= rows)


def attend_back_kernel(qkv_ref, do_ref, cos_ref, low_ref, upp_ref, col_ref, row_ref, dp_ref, sum_ref):
    size, wide = do_ref.shape
    query, key, value = qkv_ref[:, :wide], qkv_ref[:, wide : 2 * wide], qkv_ref[:, 2 * wide :]
    grad = do_ref[...]
    allowed = mask_of(col_ref[...], row_ref[...], size)
    head_of = lax.broadcasted_iota(jnp.int32, (size, wide), 1) // HD
    zero = jnp.zeros_like(query)
    dq = jnp.zeros((size, wide), F32)
    dk = jnp.zeros((size, wide), F32)
    dv = jnp.zeros((size, wide), F32)
    for head in range(wide // HD):
        mine = head_of == head
        query_h = jnp.where(mine, query, zero)
        grad_h = jnp.where(mine, grad, zero)
        scores = dot(query_h, key, 1, 1) * HD ** (-0.5)
        scores = jnp.where(allowed, scores, -1e30)
        weights = jnp.exp(scores - jnp.max(scores, axis=1, keepdims=True))
        prob = weights / jnp.sum(weights, axis=1, keepdims=True)
        dv = dv + dot(prob.astype(BF16), grad_h, 0, 0)
        dprob = dot(grad_h, value, 1, 1)
        delta = jnp.sum(prob * dprob, axis=1, keepdims=True)
        dscore = (prob * (dprob - delta)).astype(BF16)
        dq = jnp.where(mine, dot(dscore, key, 1, 0), dq)
        dk = dk + dot(dscore, query_h, 0, 0)
    cos_t, low_t, upp_t = cos_ref[...], low_ref[...], upp_ref[...]
    dq = spin_back(dq * HD ** (-0.5), cos_t, low_t, upp_t).astype(BF16)
    dk = spin_back(dk * HD ** (-0.5), cos_t, low_t, upp_t).astype(BF16)
    dv = dv.astype(BF16)
    dp_ref[:, :wide] = dq
    dp_ref[:, wide : 2 * wide] = dk
    dp_ref[:, 2 * wide :] = dv
    for part, grad_p in enumerate((dq, dk, dv)):
        sum_ref[0, :, part * wide : (part + 1) * wide] = jnp.sum(
            grad_p.astype(F32), axis=0, keepdims=True
        )


def row_blocks(size, wide):
    return pl.BlockSpec((size, wide), lambda i: (i, 0))


def attend_back(qkv, grad, tables, seg_col, seg_row, seqs, size, wide):
    return pl.pallas_call(
        attend_back_kernel,
        grid=(seqs,),
        in_specs=[
            row_blocks(size, 3 * wide),
            row_blocks(size, wide),
            row_blocks(size, wide),
            row_blocks(size, wide),
            row_blocks(size, wide),
            row_blocks(size, 1),
            pl.BlockSpec((None, 1, size), lambda i: (i, 0, 0)),
        ],
        out_specs=[
            row_blocks(size, 3 * wide),
            pl.BlockSpec((1, 1, 3 * wide), lambda i: (i, 0, 0)),
        ],
        out_shape=[
            jax.ShapeDtypeStruct((seqs * size, 3 * wide), BF16),
            jax.ShapeDtypeStruct((seqs, 1, 3 * wide), F32),
        ],
        cost_estimate=pl.CostEstimate(
            flops=seqs * 20 * size * size * wide, bytes_accessed=seqs * size * wide * 32, transcendentals=seqs * size * size * 4
        ),
        name="attend_back",
    )(qkv, grad, *tables, seg_col, seg_row)


class Place:
    def __init__(self, count):
        self.count = count
        self.lines = count // TP
        self.me = lax.axis_index("dp")
        self.t = lax.axis_index("tensor")
        self.u = self.me // TP
        self.j = self.me % TP
        self.x = self.j // 2
        self.c = self.j % 2
        self.core_peer = self.me + 1 - 2 * self.c
        self.x_peer = self.me + 2 - 4 * self.x

    def group(self, k):
        x = (self.x + k // 2) % 2
        return self.u * TP + x * 2 + self.c, (self.t + k % 2) % 2, x


def remote(src, dst, send_sem, recv_sem, dp, t):
    return pltpu.make_async_remote_copy(
        src_ref=src,
        dst_ref=dst,
        send_sem=send_sem,
        recv_sem=recv_sem,
        device_id=(dp, t),
        device_id_type=pl.DeviceIdType.MESH,
    )


def wait_bytes(ref, sem):
    pltpu.make_async_copy(ref, ref, sem).wait()


def greet(place):
    barrier = pltpu.get_barrier_semaphore()

    @pl.loop(1, place.count)
    def _(k):
        pl.semaphore_signal(
            barrier,
            inc=1,
            device_id=((place.me + k) % place.count, place.t),
            device_id_type=pl.DeviceIdType.MESH,
        )

    for k in (1, 3):
        dp, t, _ = place.group(k)
        pl.semaphore_signal(barrier, inc=1, device_id=(dp, t), device_id_type=pl.DeviceIdType.MESH)
    pl.semaphore_wait(barrier, place.count + 1)


def each_dest(place, act):
    if place.lines == 4:

        @pl.loop(1, TP)
        def _(q):
            j = (place.j + q) % TP
            act(place.u * TP + j, place.u, j)

        @pl.loop(0, TP)
        def _(q):
            j = (place.j + q) % TP
            for dz in (2, 1, 3):
                u = (place.u + dz) % 4
                act(u * TP + j, u, j)

    else:

        @pl.loop(1, place.count)
        def _(k):
            dest = (place.me + k) % place.count
            act(dest, dest // TP, dest % TP)


class WeightGather:
    def __init__(self, place, index, src, dst, send_sem, recv_sem):
        self.place, self.src, self.dst = place, src, dst
        self.send_sem, self.recv_sem = send_sem.at[index], recv_sem.at[index]
        self.rows = src.shape[1]

    def copy(self, dest, u, j):
        p = self.place
        mine = self.dst.at[pl.ds(p.me * self.rows, self.rows)]
        far = 0
        if p.lines == 4:
            far = (((p.u == 0) & (u == 2)) | ((p.u == 3) & (u == 1))).astype(jnp.int32)
        return remote(self.src.at[j], mine, self.send_sem.at[dest], self.recv_sem.at[far], dest, p.t)

    def when_sent(self, u, act):
        p = self.place
        if p.lines == 4:
            pl.when(jnp.abs(p.u - u) < 3)(act)
        else:
            act()

    def start(self):
        p = self.place
        mine = self.dst.at[pl.ds(p.me * self.rows, self.rows)]
        pltpu.make_async_copy(self.src.at[p.j], mine, self.recv_sem.at[0]).start()
        each_dest(p, lambda dest, u, j: self.when_sent(u, lambda: self.copy(dest, u, j).start()))

    def forward(self):
        p = self.place
        size = TP * self.rows
        chunk = self.dst.at[pl.ds(jnp.where(p.u == 2, 0, 3) * size, size)]
        dest = p.me + jnp.where(p.u == 2, TP, -TP)
        return remote(chunk, chunk, self.send_sem.at[p.me], self.recv_sem.at[1], dest, p.t)

    def arrive(self):
        p = self.place
        size = TP * self.rows
        if p.lines == 4:
            wait_bytes(self.dst.at[pl.ds(0, size)], self.recv_sem.at[1])
            pl.when((p.u == 1) | (p.u == 2))(lambda: self.forward().start())
            wait_bytes(self.dst.at[pl.ds(0, 3 * size)], self.recv_sem.at[0])
        else:
            wait_bytes(self.dst, self.recv_sem.at[0])

    def finish(self):
        p = self.place
        each_dest(
            p, lambda dest, u, j: self.when_sent(u, lambda: self.copy(dest, u, j).wait_send())
        )
        if p.lines == 4:
            pl.when((p.u == 1) | (p.u == 2))(lambda: self.forward().wait_send())


class GroupSum:
    def __init__(self, place, to_core, from_core, here, low, parts, core_sem, part_sem):
        self.place = place
        self.to_core, self.from_core, self.here, self.low, self.parts = to_core, from_core, here, low, parts
        self.core_sem, self.part_sem = core_sem, part_sem

    def core_copy(self, x):
        p = self.place
        return remote(
            self.to_core.at[x], self.from_core.at[x], self.core_sem.at[0, x], self.core_sem.at[1, x], p.core_peer, p.t
        )

    def part_copy(self, k):
        p = self.place
        half = self.parts.shape[1]
        dp, t, x = p.group(k)
        block = self.low.at[x, pl.ds(pl.multiple_of(t * half, half), half)]
        return remote(block, self.parts.at[k - 1], self.part_sem.at[0, k], self.part_sem.at[1, k], dp, t)

    def run(self, product):
        p = self.place
        size, step = self.here.shape[1], min(512, D)
        for x in range(2):

            @pl.loop(0, D // step)
            def _(n):
                at = pl.ds(pl.multiple_of(n * step, step), step)
                self.to_core[x, :, at] = product(x * 2 + 1 - p.c, n, step).astype(BF16)

            self.core_copy(x).start()
        for x in range(2):

            @pl.loop(0, D // step)
            def _(n):
                at = pl.ds(pl.multiple_of(n * step, step), step)
                self.here[x, :, at] = product(x * 2 + p.c, n, step)

        for x in range(2):
            self.core_copy(x).wait_recv()

            @pl.loop(0, size // 32)
            def _(i):
                at = pl.ds(pl.multiple_of(i * 32, 32), 32)
                total = self.here[x, at, :] + self.from_core[x, at, :].astype(F32)
                self.here[x, at, :] = total
                self.low[x, at, :] = total.astype(BF16)

        for k in (3, 2, 1):
            self.part_copy(k).start()
        for k in (3, 2, 1):
            self.part_copy(k).wait_recv()

    def total(self, at, rows):
        p = self.place
        half = self.parts.shape[1]
        value = self.here[p.x, pl.ds(pl.multiple_of(p.t * half + at, 32), rows), :]
        for k in range(3):
            value = value + self.parts[k, pl.ds(pl.multiple_of(at, 32), rows), :].astype(F32)
        return value

    def finish(self):
        for x in range(2):
            self.core_copy(x).wait_send()
        for k in (1, 2, 3):
            self.part_copy(k).wait_send()


class GroupGather:
    def __init__(self, place, out, size, part_sem, core_sem):
        self.place, self.out, self.half = place, out, size // 2
        self.part_sem, self.core_sem = part_sem, core_sem

    def block(self, x, t):
        p = self.place
        start = ((x * 2 + p.c) * 2 + t) * self.half
        return self.out.at[pl.ds(pl.multiple_of(start, self.half), self.half)]

    def part_copy(self, k):
        p = self.place
        dp, t, _ = p.group(k)
        mine = self.block(p.x, p.t)
        return remote(mine, mine, self.part_sem.at[0, k], self.part_sem.at[1, k], dp, t)

    def core_copy(self, k):
        p = self.place
        _, t, x = p.group(k)
        block = self.block(x, t)
        return remote(block, block, self.core_sem.at[0, k], self.core_sem.at[1, k], p.core_peer, p.t)

    def run(self):
        for k in (3, 2, 1):
            self.part_copy(k).start()
        self.core_copy(0).start()
        for k in (1, 2, 3):
            self.part_copy(k).wait_recv()
            self.core_copy(k).start()
        for k in range(4):
            self.core_copy(k).wait_recv()

    def finish(self):
        for k in (1, 2, 3):
            self.part_copy(k).wait_send()
        for k in range(4):
            self.core_copy(k).wait_send()


class GroupPieces:
    def __init__(self, place, src, out, sem):
        self.place, self.src, self.out, self.sem = place, src, out, sem

    def own(self):
        return pltpu.make_async_copy(self.src, self.out.at[self.place.j], self.sem.at[0, 0])

    def near(self, k):
        p = self.place
        dest = p.core_peer if k == 1 else p.x_peer
        return remote(self.src, self.out.at[p.j], self.sem.at[0, k], self.sem.at[1, k], dest, p.t)

    def relay(self):
        p = self.place
        block = self.out.at[(p.j + 2) % TP]
        return remote(block, block, self.sem.at[0, 3], self.sem.at[1, 3], p.core_peer, p.t)

    def start(self):
        self.near(2).start()
        self.near(1).start()
        self.own().start()

    def pass_on(self):
        self.near(2).wait_recv()
        self.relay().start()

    def arrive(self):
        self.near(1).wait_recv()
        self.relay().wait_recv()
        self.own().wait()

    def finish(self):
        self.near(1).wait_send()
        self.near(2).wait_send()
        self.relay().wait_send()


def tables_of(aux, wide):
    half = ROT // 2
    line = lax.broadcasted_iota(jnp.int32, (aux.shape[1], wide), 0)
    lane = lax.broadcasted_iota(jnp.int32, (aux.shape[1], wide), 1) % HD
    first = lane < half
    second = (lane >= half) & (lane < ROT)

    def spread(pick, sign):
        table = jnp.where(pick, sign, 0.0).astype(F32)
        return lax.dot_general(
            aux, table, (((1,), (0,)), ((), ())), precision=lax.Precision.HIGHEST, preferred_element_type=F32
        )

    rest = lax.broadcasted_iota(jnp.int32, (aux.shape[0], wide), 1) % HD >= ROT
    cos_t = spread((line == lane % half) & (first | second), 1.0) + jnp.where(rest, 1.0, 0.0)
    low_t = spread((line == lane + half) & first, -1.0)
    upp_t = spread((line == lane) & second, 1.0)
    return cos_t, low_t, upp_t


def attend_values(query, key, value, allowed):
    head_of = lax.broadcasted_iota(jnp.int32, query.shape, 1) // HD
    total = jnp.zeros(query.shape, F32)
    for head in range(query.shape[1] // HD):
        mine = head_of == head
        scores = dot(jnp.where(mine, query, jnp.zeros_like(query)), key, 1, 1) * HD ** (-0.5)
        scores = jnp.where(allowed, scores, -1e30)
        weights = jnp.exp(scores - jnp.max(scores, axis=1, keepdims=True))
        prob = weights / jnp.sum(weights, axis=1, keepdims=True)
        total = jnp.where(mine, dot(prob.astype(BF16), value, 1, 0), total)
    return total


def forward_kernel(
    count,
    small_src, aux_src, row_src, tok_src, cot_src, wq_src, wo_src, wg_src, wd_src,
    wq_out, wo_out, wg_out, wd_out, h1_out, h2_out, cot_out, aux_out, row_out,
    qkv, att, hid, slope, gain, resid, norms,
    wq, wo, wg, wd, tok, h1, h2, small, aux_all, row_all, to_core, from_core, here, low, parts,
    w_send, w_recv, small_sem, aux_sem, row_sem, tok_sem, cot_sem, core_sem, part_sem, part2_sem, core2_sem, out_sem,
):
    p = Place(count)
    size = tok_src.shape[0]
    half = size // 2
    wide = att.shape[1]
    rows = wq_src.shape[1]
    greet(p)

    auxes = GroupPieces(p, aux_src, aux_all, aux_sem)
    rowses = GroupPieces(p, row_src, row_all, row_sem)
    tokens = GroupPieces(p, tok_src, tok, tok_sem)
    cots = GroupPieces(p, cot_src, cot_out, cot_sem)

    def small_copy(dest):
        return remote(small_src, small.at[p.me], small_sem.at[dest], small_sem.at[count], dest, p.t)

    own_small = pltpu.make_async_copy(small_src, small.at[p.me], small_sem.at[count])
    own_small.start()
    each_dest(p, lambda dest, u, j: small_copy(dest).start())
    auxes.start()
    rowses.start()
    tokens.start()
    gathers = [
        WeightGather(p, i, src, dst, w_send, w_recv)
        for i, (src, dst) in enumerate(((wq_src, wq), (wo_src, wo), (wg_src, wg), (wd_src, wd)))
    ]
    gathers[0].start()
    gathers[1].start()
    auxes.pass_on()
    rowses.pass_on()
    tokens.pass_on()
    gathers[2].start()

    wait_bytes(small, small_sem.at[count])
    per_tile = 128 // rows
    for m in range(D // 128):
        tile = jnp.zeros((8, 128), F32)
        for i in range(per_tile):
            tile = tile + small[m * per_tile + i].astype(F32)[0:8]
        norms[0:8, m * 128 : (m + 1) * 128] = tile
    bias_rows = small.shape[1] - 16
    total = jnp.zeros((bias_rows, 128), F32)
    for d in range(count):
        total = total + small[d].astype(F32)[16:]
    for i in range(bias_rows):
        norms[8:9, i * 128 : (i + 1) * 128] = total[i : i + 1]

    auxes.arrive()
    rowses.arrive()
    tokens.arrive()
    aux_out[...] = aux_all[...]
    row_out[...] = row_all[...]

    @pl.loop(0, TP * size // 32)
    def _(i):
        s, at = i // (size // 32), pl.multiple_of(i % (size // 32) * 32, 32)
        values = tok[s, pl.ds(at, 32), :].astype(F32)
        normed, _, _ = layer_norm(values, norms[0:1, :D], norms[1:2, :D])
        h1[pl.ds(pl.multiple_of(i * 32, 32), 32), :] = normed.astype(BF16)

    h1_copy = pltpu.make_async_copy(h1, h1_out, out_sem.at[0])
    h1_copy.start()
    gathers[0].arrive()
    head_wide = (bias_rows * 128) // 3

    @pl.loop(0, TP)
    def _(s):
        at = pl.ds(pl.multiple_of(s * size, size), size)
        proj = dot(h1[at, :], wq[...], 1, 0)
        aux = aux_all[s]
        tables = tables_of(aux, wide)

        def part(k):
            lanes = pl.ds(pl.multiple_of(k * head_wide + p.j * wide, 128), wide)
            return proj[:, k * wide : (k + 1) * wide] + norms[8:9, lanes]

        query = spin(part(0), *tables).astype(BF16)
        key = spin(part(1), *tables).astype(BF16)
        value = part(2).astype(BF16)
        qkv[at, :wide] = query
        qkv[at, wide : 2 * wide] = key
        qkv[at, 2 * wide :] = value
        allowed = mask_of(aux[:, ROT : ROT + 1], row_all[s, 0:1, :], size)
        att[at, :] = attend_values(query, key, value, allowed).astype(BF16)

    gathers[1].arrive()
    sums = GroupSum(p, to_core, from_core, here, low, parts, core_sem, part_sem)

    def attention_product(s, n, step):
        at = pl.ds(pl.multiple_of(s * size, size), size)
        return dot(att[at, :], wo[pl.ds(pl.multiple_of(n * step, step), step), :], 1, 1)

    sums.run(attention_product)

    @pl.loop(0, half // 32)
    def _(i):
        at = pl.multiple_of(i * 32, 32)
        values = tok_src[pl.ds(pl.multiple_of(p.t * half + at, 32), 32), :].astype(F32)
        values = values + sums.total(at, 32)
        resid[pl.ds(at, 32), :] = values
        normed, _, _ = layer_norm(values, norms[2:3, :D], norms[3:4, :D])
        start = (p.j * 2 + p.t) * half + at
        h2[pl.ds(pl.multiple_of(start, 32), 32), :] = normed.astype(BF16)

    spread = GroupGather(p, h2, size, part2_sem, core2_sem)
    spread.run()
    gathers[3].start()
    cots.start()
    h2_copy = pltpu.make_async_copy(h2, h2_out, out_sem.at[1])
    h2_copy.start()
    gathers[2].arrive()

    full = hid.shape[1] - 128

    @pl.loop(0, TP)
    def _(s):
        at = pl.ds(pl.multiple_of(s * size, size), size)
        rows_in = h2[at, :]
        gate = dot(rows_in, wg[:, :full], 1, 0)
        up = dot(rows_in, wg[:, full : 2 * full], 1, 0)
        sig = jax.nn.sigmoid(gate)
        hid[at, :full] = (gate * sig * up).astype(BF16)
        slope[at, :full] = (up * sig * (1.0 + gate * (1.0 - sig))).astype(BF16)
        gain[at, :full] = (gate * sig).astype(BF16)
        gate = dot(rows_in, wg[:, 2 * full :], 1, 0)
        up = pltpu.roll(gate, 64, 1)
        sig = jax.nn.sigmoid(gate)
        first = lax.broadcasted_iota(jnp.int32, gate.shape, 1) < 64
        hid[at, full:] = jnp.where(first, gate * sig * up, 0.0).astype(BF16)
        slope[at, full:] = jnp.where(first, up * sig * (1.0 + gate * (1.0 - sig)), 0.0).astype(BF16)
        gain[at, full:] = jnp.where(first, gate * sig, 0.0).astype(BF16)

    copies = [h1_copy, h2_copy]
    for i, (src, dst) in enumerate(((wq, wq_out), (wo, wo_out), (wg, wg_out))):
        copies.append(pltpu.make_async_copy(src, dst, out_sem.at[2 + i]))
        copies[-1].start()
    cots.pass_on()
    cots.arrive()
    gathers[3].arrive()
    copies.append(pltpu.make_async_copy(wd, wd_out, out_sem.at[5]))
    copies[-1].start()
    for copy in copies:
        copy.wait()
    each_dest(p, lambda dest, u, j: small_copy(dest).wait_send())
    for part in (auxes, rowses, tokens, cots, sums, spread, *gathers):
        part.finish()


def forward(count, small, aux, row, tokens, cot, wq, wo, wg, wd):
    size = tokens.shape[0]
    group = TP * size
    wide, hidden = wo.shape[2], wd.shape[2]
    any_spec = pl.BlockSpec(memory_space=pl.ANY)
    vmem = pl.BlockSpec(memory_space=pltpu.VMEM)
    dma = pltpu.SemaphoreType.DMA

    def out(*shape, dtype=BF16):
        return jax.ShapeDtypeStruct(shape, dtype)

    pad = -(-hidden // 128) * 128
    weights = [wq, wo, wg, wd]
    return pl.pallas_call(
        functools.partial(forward_kernel, count),
        in_specs=[vmem, vmem, vmem, vmem] + [any_spec] * 5,
        out_specs=[any_spec] * 7 + [vmem] * 9,
        out_shape=[out(D, w.shape[2]) for w in weights]
        + [
            out(group, D),
            out(group, D),
            out(TP, size, D),
            out(TP, size, 128, dtype=F32),
            out(TP, 8, size, dtype=F32),
            out(group, 3 * wide),
            out(group, wide),
            out(group, pad),
            out(group, pad),
            out(group, pad),
            out(size // 2, D, dtype=F32),
            out(16, max(D, 128 * (small.shape[0] - 16)), dtype=F32),
        ],
        scratch_shapes=[pltpu.VMEM((D, w.shape[2]), BF16) for w in weights]
        + [
            pltpu.VMEM((TP, size, D), BF16),
            pltpu.VMEM((group, D), BF16),
            pltpu.VMEM((group, D), BF16),
            pltpu.VMEM((count,) + small.shape, BF16),
            pltpu.VMEM((TP, size, 128), F32),
            pltpu.VMEM((TP, 8, size), F32),
            pltpu.VMEM((2, size, D), BF16),
            pltpu.VMEM((2, size, D), BF16),
            pltpu.VMEM((2, size, D), F32),
            pltpu.VMEM((2, size, D), BF16),
            pltpu.VMEM((3, size // 2, D), BF16),
            dma((4, count)),
            dma((4, 2)),
            dma((count + 1,)),
            dma((2, 4)),
            dma((2, 4)),
            dma((2, 4)),
            dma((2, 4)),
            dma((2, 2)),
            dma((2, 4)),
            dma((2, 4)),
            dma((2, 4)),
            dma((6,)),
        ],
        compiler_params=pltpu.CompilerParams(
            collective_id=0, has_side_effects=True, vmem_limit_bytes=60 * 1024 * 1024
        ),
        cost_estimate=pl.CostEstimate(flops=12 * 10**9, bytes_accessed=80 * 10**6, transcendentals=10**7),
        name="forward",
    )(small, aux, row, tokens, cot, *weights)


class Links:
    def __init__(self, count):
        self.count = count
        self.lines = count // TP
        self.place = lax.axis_index("dp")
        self.tensor = lax.axis_index("tensor")
        self.u = self.place // TP
        self.j = self.place % TP
        self.x = self.j // 2
        self.c = self.j % 2

    def flip(self, values, bit):
        return lax.ppermute(values, "dp", [(i, i ^ bit) for i in range(self.count)])

    def swap(self, values):
        return lax.ppermute(values, "tensor", [(0, 1), (1, 0)])

    def along(self, values, pairs):
        return lax.ppermute(
            values, "dp", [(a * TP + r, b * TP + r) for a, b in pairs for r in range(TP)]
        )

    def pair(self, mine, other, second):
        return jnp.stack([jnp.where(second, other, mine), jnp.where(second, mine, other)])

    def group_gather(self, values):
        two = self.pair(values, self.flip(values, 1), self.c == 1)
        four = self.pair(two, self.flip(two, 2), self.x == 1)
        return four.reshape((TP,) + values.shape)

    def group_swap(self, blocks):
        def block(k):
            return lax.dynamic_index_in_dim(blocks, self.j ^ k, 0, False)

        got = [block(0)] + [self.flip(block(k), k) for k in range(1, TP)]
        odd = self.c == 1
        got = [jnp.where(odd, got[k ^ 1], got[k]) for k in range(TP)]
        odd = self.x == 1
        return jnp.stack([jnp.where(odd, got[k ^ 2], got[k]) for k in range(TP)])

    def line_pieces(self, values):
        n = self.lines
        if n != 4:
            return [
                self.along(values, [(i, (i + k) % n) for i in range(n)]) for k in range(1, n)
            ]
        up = self.along(values, [(0, 1), (1, 2), (2, 3)])
        down = self.along(values, [(3, 2), (2, 1), (1, 0)])
        two = self.along(values, [(0, 2), (1, 3), (2, 0), (3, 1)])
        far = self.along(two, [(2, 3), (1, 0)])
        return [jnp.where(self.u == 0, far, up), two, jnp.where(self.u == 3, far, down)]

    def line_gather(self, values):
        out = jnp.zeros((self.lines,) + values.shape, values.dtype)
        for k, piece in enumerate([values] + self.line_pieces(values)):
            out = lax.dynamic_update_index_in_dim(out, piece, (self.u - k) % self.lines, 0)
        return out

    def line_scatter_sum(self, blocks):
        n = self.lines

        def block(k):
            return lax.dynamic_index_in_dim(blocks, (self.u + k) % n, 0, False)

        total = block(0).astype(F32)
        if n != 4:
            for k in range(1, n):
                total = total + self.along(
                    block(k), [(i, (i + k) % n) for i in range(n)]
                ).astype(F32)
            return total
        outer = jnp.where(self.u == 0, blocks[3], blocks[0])
        far = self.along(outer, [(0, 1), (3, 2)])
        up = self.along(block(1), [(0, 1), (1, 2), (2, 3)])
        down = self.along(block(3), [(3, 2), (2, 1), (1, 0)])
        two = (block(2).astype(F32) + far.astype(F32)).astype(BF16)
        two = self.along(two, [(0, 2), (1, 3), (2, 0), (3, 1)])
        return total + up.astype(F32) + down.astype(F32) + two.astype(F32)

    def line_sum(self, values):
        n = self.lines
        total = values
        for k in range(1, n):
            total = total + self.along(values, [(i, (i + k) % n) for i in range(n)])
        return total

    def scatter_sum(self, partial):
        half = partial.shape[-1] // 2

        def take(values, axis, index):
            return lax.dynamic_index_in_dim(values, index, axis, False)

        other = self.flip(take(partial, 1, 1 - self.c).astype(BF16), 1)
        here = take(partial, 1, self.c) + other.astype(F32)
        left, right = here[..., :half], here[..., half:]
        left = take(left, 0, self.x) + self.flip(take(left, 0, 1 - self.x).astype(BF16), 2).astype(F32)
        right = take(right, 1, self.tensor) + self.swap(
            take(right, 1, 1 - self.tensor).astype(BF16)
        ).astype(F32)
        left = take(left, 0, self.tensor) + self.swap(
            take(left, 0, 1 - self.tensor).astype(BF16)
        ).astype(F32)
        right = take(right, 0, self.x) + self.flip(take(right, 0, 1 - self.x).astype(BF16), 2).astype(F32)
        return jnp.concatenate([left, right], axis=-1)

    def gather(self, values):
        half = values.shape[-1] // 2
        left, right = values[:, :half], values[:, half:]
        left = self.pair(left, self.swap(left), self.tensor == 1)
        left = self.pair(left, self.flip(left, 2), self.x == 1)
        right = self.pair(right, self.flip(right, 2), self.x == 1)
        right_other = self.swap(right)
        second = self.tensor == 1
        right = jnp.stack(
            [jnp.where(second, right_other, right), jnp.where(second, right, right_other)], axis=1
        )
        here = jnp.concatenate([left, right], axis=-1)
        there = self.flip(here, 1)
        second = self.c == 1
        return jnp.stack([jnp.where(second, there, here), jnp.where(second, here, there)], axis=1)


def per_device(
    count,
    tokens_in,
    segment_ids,
    d_out,
    qkv_weight,
    qkv_bias,
    out_weight,
    gating_weight,
    down_weight,
    norm_params,
    qkv_first,
    qkv_second,
    bias_first,
    bias_second,
    out_first,
    out_second,
    gating_first,
    gating_second,
    down_first,
    down_second,
    norm_first,
    norm_second,
):
    links = Links(count)
    rows = norm_params.shape[1]
    seq_len = tokens_in.shape[1]
    head_local = qkv_weight.shape[2]
    hidden_local = gating_weight.shape[2]
    wide = head_local // TP
    hid = hidden_local // TP
    half_seq = seq_len // 2
    group_rows = TP * seq_len

    def cut(shard):
        return shard.astype(BF16).transpose(1, 0, 2)

    full = hid // 128 * 128
    gates = gating_weight.astype(BF16).reshape(rows, 2, TP, hid)
    gates = jnp.concatenate(
        [gates[:, 0, :, :full], gates[:, 1, :, :full], gates[:, 0, :, full:], gates[:, 1, :, full:]], axis=2
    )
    weights = (
        cut(qkv_weight.reshape(rows, 3, TP, wide).transpose(0, 2, 1, 3).reshape(rows, TP, 3 * wide)),
        cut(out_weight.T.reshape(rows, TP, wide)),
        gates.transpose(1, 0, 2),
        cut(down_weight.T.reshape(rows, TP, hid)),
    )
    bias_here = qkv_bias.shape[1]
    small_norm = lax.dynamic_update_slice(
        jnp.zeros((16, 128), F32), norm_params, (0, (links.place * rows) % 128)
    )
    small_bias = lax.dynamic_update_slice(
        jnp.zeros((3 * head_local,), F32), qkv_bias[0], (links.place * bias_here,)
    )
    small = jnp.concatenate([small_norm, small_bias.reshape(-1, 128)]).astype(BF16)
    segments = segment_ids[0]
    earlier = jnp.sum((segments[None, :] < segments[:, None]).astype(jnp.int32), axis=1)
    positions = (jnp.arange(seq_len, dtype=jnp.int32) - earlier).astype(F32)
    frequency = 10000.0 ** (-2.0 * jnp.arange(ROT // 2, dtype=F32) / ROT)
    angles = positions[:, None] * frequency[None, :]
    aux = jnp.concatenate([jnp.cos(angles), jnp.sin(angles), segments[:, None].astype(F32)], axis=1)
    aux = jnp.pad(aux, ((0, 0), (0, 128 - aux.shape[1])))
    row = jnp.broadcast_to(segments.astype(F32)[None], (8, seq_len))

    (
        qkv_matrix, out_matrix, gating_matrix, down_matrix, normed_one, normed_two, cotangent, aux_all, row_all,
        qkv_rot, attended, hidden, slope, gain, residual, norm_rows,
    ) = forward(count, small, aux, row, tokens_in[0], d_out[0], *weights)
    norm_rows = norm_rows[:4, :D]
    cotangent = cotangent.reshape(group_rows, D)
    hidden, slope, gain = hidden[:, :hid], slope[:, :hid], gain[:, :hid]

    def own_half(values):
        return lax.dynamic_slice_in_dim(values, links.tensor * half_seq, half_seq, 0)

    def to_parts(partial):
        return partial.reshape(2, 2, 2, half_seq, D)

    heads = wide // HD
    cosine, sine_part = aux_all.reshape(group_rows, 128)[:, : ROT // 2], aux_all.reshape(group_rows, 128)[:, ROT // 2 : ROT]
    zeros = jnp.zeros((group_rows, HD - ROT), F32)
    tables = (
        jnp.tile(jnp.concatenate([cosine, cosine, zeros + 1.0], axis=1), (1, heads)),
        jnp.tile(jnp.concatenate([-sine_part, jnp.zeros_like(sine_part), zeros], axis=1), (1, heads)),
        jnp.tile(jnp.concatenate([jnp.zeros_like(sine_part), sine_part, zeros], axis=1), (1, heads)),
    )
    seg_col = aux_all.reshape(group_rows, 128)[:, ROT : ROT + 1].astype(jnp.int32)
    seg_row = row_all[:, 0:1, :].astype(jnp.int32)
    tokens_own = own_half(tokens_in[0]).astype(F32)
    _, scaled_two, inverse_two = layer_norm(residual, norm_rows[2], norm_rows[3])

    grad_down = dot(cotangent, hidden, 0, 0).astype(BF16)
    down_sum = links.line_scatter_sum(grad_down.reshape(links.lines, TP * rows, hid))
    grad_hidden = dot(cotangent, down_matrix, 1, 0)
    grad_gate = (grad_hidden * slope.astype(F32)).astype(BF16)
    grad_up = (grad_hidden * gain.astype(F32)).astype(BF16)
    grad_gated = jnp.concatenate(
        [grad_gate[:, :full], grad_up[:, :full], grad_gate[:, full:], grad_up[:, full:]], axis=1
    )
    normed_grad_two = links.scatter_sum(to_parts(dot(grad_gated, gating_matrix, 1, 1)))
    grad_gating = dot(normed_two, grad_gated, 0, 0).astype(BF16)
    gating_sum = links.line_scatter_sum(grad_gating.reshape(links.lines, TP * rows, 2 * hid))

    residual_part, gain_two, shift_two = norm_back(
        normed_grad_two, scaled_two, inverse_two, norm_rows[2]
    )
    residual_grad = own_half(d_out[0]).astype(F32) + residual_part
    residual_low = links.gather(residual_grad.astype(BF16)).reshape(group_rows, D)
    grad_attended = dot(residual_low, out_matrix, 1, 0).astype(BF16)
    grad_out = dot(residual_low, attended, 0, 0).astype(BF16)
    out_sum = links.line_scatter_sum(grad_out.reshape(links.lines, TP * rows, wide))

    feedforward_term = links.scatter_sum(to_parts(dot(hidden, down_matrix, 1, 1)))
    block_own = residual + feedforward_term
    block_out = links.pair(block_own, links.swap(block_own), links.tensor == 1).reshape(seq_len, D)

    grad_projected, bias_sums = attend_back(
        qkv_rot, grad_attended, tables, seg_col, seg_row, TP, seq_len, wide
    )
    grad_qkv = dot(normed_one, grad_projected, 0, 0).astype(BF16)
    qkv_sum = links.line_scatter_sum(grad_qkv.reshape(links.lines, TP * rows, 3 * wide))
    normed_grad_one = links.scatter_sum(to_parts(dot(grad_projected, qkv_matrix, 1, 1)))
    _, scaled_one, inverse_one = layer_norm(tokens_own, norm_rows[0], norm_rows[1])
    input_part, gain_one, shift_one = norm_back(
        normed_grad_one, scaled_one, inverse_one, norm_rows[0]
    )
    input_own = residual_grad + input_part
    input_grad = links.pair(input_own, links.swap(input_own), links.tensor == 1).reshape(seq_len, D)

    norm_small = jnp.concatenate([gain_one, shift_one, gain_two, shift_two])
    norm_small = norm_small + links.swap(norm_small)
    bias_small = jnp.sum(bias_sums, axis=0).reshape(3, 1, wide)
    bias_small = jnp.where(
        lax.broadcasted_iota(jnp.int32, (3, TP, wide), 1) == links.j, bias_small, 0.0
    ).reshape(-1)
    small_grad = jnp.concatenate([norm_small, bias_small])
    small_grad = small_grad + links.flip(small_grad, 1)
    small_grad = small_grad + links.flip(small_grad, 2)
    small_grad = links.line_sum(small_grad)
    norm_grad = lax.dynamic_slice_in_dim(small_grad[: 4 * D].reshape(4, D), links.place * rows, rows, 1)
    bias_grad = lax.dynamic_slice_in_dim(
        small_grad[4 * D :].reshape(1, -1), links.place * bias_here, bias_here, 1
    )

    def to_owner(total):
        blocks = total.astype(BF16).reshape(TP, rows, total.shape[1])
        return links.group_swap(blocks).transpose(1, 0, 2).astype(F32)

    down_shard = to_owner(down_sum).reshape(rows, hidden_local).T
    gating_parts = to_owner(gating_sum)
    gate_parts = jnp.concatenate([gating_parts[..., :full], gating_parts[..., 2 * full : full + hid]], axis=2)
    up_parts = jnp.concatenate([gating_parts[..., full : 2 * full], gating_parts[..., full + hid :]], axis=2)
    gating_shard = jnp.stack([gate_parts, up_parts], axis=1).reshape(gating_weight.shape)
    out_shard = to_owner(out_sum).reshape(rows, head_local).T
    qkv_shard = (
        to_owner(qkv_sum).reshape(rows, TP, 3, wide).transpose(0, 2, 1, 3).reshape(qkv_weight.shape)
    )
    return (
        block_out[None],
        input_grad[None],
        *adamw_update(qkv_weight, qkv_shard, qkv_first, qkv_second, D ** (-0.5), 0.1),
        *adamw_update(qkv_bias, bias_grad, bias_first, bias_second, 0.3, 0.0),
        *adamw_update(out_weight, out_shard, out_first, out_second, (H * HD // 16) ** (-0.5), 0.1),
        *adamw_update(gating_weight, gating_shard, gating_first, gating_second, D ** (-0.5), 0.1),
        *adamw_update(down_weight, down_shard, down_first, down_second, FF ** (-0.5), 0.1),
        *adamw_update(norm_params, norm_grad, norm_first, norm_second, 0.25, 0.0),
    )


def solution(mesh):
    tokens = P("dp", None, None)
    qkv = P("dp", None, "tensor")
    rest = P("tensor", "dp")
    norm = P(None, "dp")
    weights = (qkv, rest, rest, qkv, rest, norm)
    states = (qkv, qkv, rest, rest, rest, rest, qkv, qkv, rest, rest, norm, norm)
    return jax.shard_map(
        functools.partial(per_device, mesh.shape["dp"]),
        mesh=mesh,
        in_specs=(tokens, P("dp", None), tokens, *weights, *states),
        out_specs=(tokens, tokens, *(spec for spec in weights for _ in range(3))),
        check_vma=False,
    )
```

```python
import functools

import jax
import jax.numpy as jnp
from jax import lax
from jax.experimental import pallas as pl
from jax.experimental.pallas import tpu as pltpu
from jax.sharding import PartitionSpec as P

D = 2048
H = 32
HD = 64
ROT = 16
FF = 5632
STEP = 10
TP = 4

F32 = jnp.float32
BF16 = jnp.bfloat16


def layer_norm(values, scale_row, shift_row):
    centre = values - jnp.mean(values, axis=-1, keepdims=True)
    spread = jnp.mean(centre * centre, axis=-1, keepdims=True)
    inverse = lax.rsqrt(spread + 1e-05)
    scaled = centre * inverse
    return (scaled * scale_row + shift_row, scaled, inverse)


def norm_back(grad_in, scaled, inverse, scale_row):
    grad_scaled = grad_in * scale_row
    mean_first = jnp.mean(grad_scaled, axis=-1, keepdims=True)
    mean_second = jnp.mean(grad_scaled * scaled, axis=-1, keepdims=True)
    grad_values = inverse * (grad_scaled - mean_first - scaled * mean_second)
    return (grad_values, jnp.sum(grad_in * scaled, axis=0), jnp.sum(grad_in, axis=0))


def adamw_update(weight_old, gradient, first_old, second_old, step_rate, decay_rate):
    first_new = 0.9 * first_old + 0.1 * gradient
    second_new = 0.95 * second_old + 0.05 * gradient * gradient
    corrected = first_new / (1.0 - 0.9**STEP) / (jnp.sqrt(second_new / (1.0 - 0.95**STEP)) + 1e-08)
    return (weight_old - step_rate * (corrected + decay_rate * weight_old), first_new, second_new)


def dot(a, b, ca, cb):
    return lax.dot_general(a, b, (((ca,), (cb,)), ((), ())), preferred_element_type=F32)


def spin(values, cos_t, lower_t, upper_t):
    wide = values.shape[1]
    return (
        values * cos_t
        + pltpu.roll(values, wide - ROT // 2, 1) * lower_t
        + pltpu.roll(values, ROT // 2, 1) * upper_t
    )


def spin_back(values, cos_t, lower_t, upper_t):
    wide = values.shape[1]
    return (
        values * cos_t
        + pltpu.roll(values * lower_t, ROT // 2, 1)
        + pltpu.roll(values * upper_t, wide - ROT // 2, 1)
    )


def mask_of(seg_col, seg_row, size):
    rows = lax.broadcasted_iota(jnp.int32, (size, size), 0)
    cols = lax.broadcasted_iota(jnp.int32, (size, size), 1)
    return (seg_col == seg_row) & (cols <= rows)


def attend_back_values(query, key, value, grad, allowed, tables):
    head_of = lax.broadcasted_iota(jnp.int32, query.shape, 1) // HD
    zero = jnp.zeros_like(query)
    dq = jnp.zeros(query.shape, F32)
    dk = jnp.zeros(query.shape, F32)
    dv = jnp.zeros(query.shape, F32)
    for head in range(query.shape[1] // HD):
        mine = head_of == head
        query_h = jnp.where(mine, query, zero)
        grad_h = jnp.where(mine, grad, zero)
        scores = dot(query_h, key, 1, 1) * HD ** (-0.5)
        scores = jnp.where(allowed, scores, -1e30)
        weights = jnp.exp(scores - jnp.max(scores, axis=1, keepdims=True))
        prob = weights / jnp.sum(weights, axis=1, keepdims=True)
        dv = dv + dot(prob.astype(BF16), grad_h, 0, 0)
        dprob = dot(grad_h, value, 1, 1)
        delta = jnp.sum(prob * dprob, axis=1, keepdims=True)
        dscore = (prob * (dprob - delta)).astype(BF16)
        dq = jnp.where(mine, dot(dscore, key, 1, 0), dq)
        dk = dk + dot(dscore, query_h, 0, 0)
    dq = spin_back(dq * HD ** (-0.5), *tables).astype(BF16)
    dk = spin_back(dk * HD ** (-0.5), *tables).astype(BF16)
    return dq, dk, dv.astype(BF16)


class Place:
    def __init__(self, count):
        self.count = count
        self.lines = count // TP
        self.me = lax.axis_index("dp")
        self.t = lax.axis_index("tensor")
        self.u = self.me // TP
        self.j = self.me % TP
        self.x = self.j // 2
        self.c = self.j % 2
        self.core_peer = self.me + 1 - 2 * self.c
        self.x_peer = self.me + 2 - 4 * self.x

    def group(self, k):
        x = (self.x + k // 2) % 2
        return self.u * TP + x * 2 + self.c, (self.t + k % 2) % 2, x


def remote(src, dst, send_sem, recv_sem, dp, t):
    return pltpu.make_async_remote_copy(
        src_ref=src,
        dst_ref=dst,
        send_sem=send_sem,
        recv_sem=recv_sem,
        device_id=(dp, t),
        device_id_type=pl.DeviceIdType.MESH,
    )


def wait_bytes(ref, sem):
    pltpu.make_async_copy(ref, ref, sem).wait()


def greet(place):
    barrier = pltpu.get_barrier_semaphore()

    @pl.loop(1, place.count)
    def _(k):
        pl.semaphore_signal(
            barrier,
            inc=1,
            device_id=((place.me + k) % place.count, place.t),
            device_id_type=pl.DeviceIdType.MESH,
        )

    for k in (1, 3):
        dp, t, _ = place.group(k)
        pl.semaphore_signal(barrier, inc=1, device_id=(dp, t), device_id_type=pl.DeviceIdType.MESH)
    pl.semaphore_wait(barrier, place.count + 1)


def each_dest(place, act):
    if place.lines == 4:

        @pl.loop(1, TP)
        def _(q):
            j = (place.j + q) % TP
            act(place.u * TP + j, place.u, j)

        @pl.loop(0, TP)
        def _(q):
            j = (place.j + q) % TP
            for dz in (2, 1, 3):
                u = (place.u + dz) % 4
                act(u * TP + j, u, j)

    else:

        @pl.loop(1, place.count)
        def _(k):
            dest = (place.me + k) % place.count
            act(dest, dest // TP, dest % TP)


class WeightGather:
    def __init__(self, place, index, src, dst, send_sem, recv_sem):
        self.place, self.src, self.dst = place, src, dst
        self.send_sem, self.recv_sem = send_sem.at[index], recv_sem.at[index]
        self.rows = src.shape[1]

    def copy(self, dest, u, j):
        p = self.place
        mine = self.dst.at[pl.ds(p.me * self.rows, self.rows)]
        far = 0
        if p.lines == 4:
            far = (((p.u == 0) & (u == 2)) | ((p.u == 3) & (u == 1))).astype(jnp.int32)
        return remote(self.src.at[j], mine, self.send_sem.at[dest], self.recv_sem.at[far], dest, p.t)

    def when_sent(self, u, act):
        p = self.place
        if p.lines == 4:
            pl.when(jnp.abs(p.u - u) < 3)(act)
        else:
            act()

    def start(self):
        p = self.place
        mine = self.dst.at[pl.ds(p.me * self.rows, self.rows)]
        pltpu.make_async_copy(self.src.at[p.j], mine, self.recv_sem.at[0]).start()
        each_dest(p, lambda dest, u, j: self.when_sent(u, lambda: self.copy(dest, u, j).start()))

    def forward(self):
        p = self.place
        size = TP * self.rows
        chunk = self.dst.at[pl.ds(jnp.where(p.u == 2, 0, 3) * size, size)]
        dest = p.me + jnp.where(p.u == 2, TP, -TP)
        return remote(chunk, chunk, self.send_sem.at[p.me], self.recv_sem.at[1], dest, p.t)

    def arrive(self):
        p = self.place
        size = TP * self.rows
        if p.lines == 4:
            wait_bytes(self.dst.at[pl.ds(0, size)], self.recv_sem.at[1])
            pl.when((p.u == 1) | (p.u == 2))(lambda: self.forward().start())
            wait_bytes(self.dst.at[pl.ds(0, 3 * size)], self.recv_sem.at[0])
        else:
            wait_bytes(self.dst, self.recv_sem.at[0])

    def finish(self):
        p = self.place
        each_dest(
            p, lambda dest, u, j: self.when_sent(u, lambda: self.copy(dest, u, j).wait_send())
        )
        if p.lines == 4:
            pl.when((p.u == 1) | (p.u == 2))(lambda: self.forward().wait_send())


class GroupSum:
    def __init__(self, place, to_core, from_core, low, own, parts, core_sem, part_sem, free_sem=None):
        self.place = place
        self.to_core, self.from_core, self.low, self.own, self.parts = to_core, from_core, low, own, parts
        self.core_sem, self.part_sem, self.free_sem = core_sem, part_sem, free_sem

    def core_copy(self, i):
        p = self.place
        return remote(
            self.to_core.at[i], self.from_core.at[i], self.core_sem.at[0, i], self.core_sem.at[1, i], p.core_peer, p.t
        )

    def part_copy(self, k):
        p = self.place
        half = self.parts.shape[1]
        dp, t, _ = p.group(k)
        block = self.low.at[0 if k >= 2 else 1, pl.ds(pl.multiple_of(t * half, half), half)]
        return remote(block, self.parts.at[k - 1], self.part_sem.at[0, k], self.part_sem.at[1, k], dp, t)

    def start(self, product):
        p = self.place
        step = min(512, D)
        other = [(p.x + 1) % 2, p.x]
        for i in range(2):

            @pl.loop(0, D // step)
            def _(n):
                at = pl.ds(pl.multiple_of(n * step, step), step)
                self.to_core[i, :, at] = product(other[i] * 2 + 1 - p.c, n, step).astype(BF16)

            self.core_copy(i).start()
        for i in range(2):
            self.core_copy(i).wait_recv()

            @pl.loop(0, D // step)
            def _(n):
                at = pl.ds(pl.multiple_of(n * step, step), step)
                total = product(other[i] * 2 + p.c, n, step) + self.from_core[i, :, at].astype(F32)
                self.low[i, :, at] = total.astype(BF16)
                if i == 1:
                    self.own[:, at] = total

            for k in (3, 2) if i == 0 else (1,):
                self.part_copy(k).start()

    def arrive(self):
        for k in (3, 2, 1):
            self.part_copy(k).wait_recv()

    def total(self, at, rows):
        p = self.place
        half = self.parts.shape[1]
        value = self.own[pl.ds(pl.multiple_of(p.t * half + at, 32), rows), :]
        for k in range(3):
            value = value + self.parts[k, pl.ds(pl.multiple_of(at, 32), rows), :].astype(F32)
        return value

    def finish(self):
        for i in range(2):
            self.core_copy(i).wait_send()
        for k in (1, 2, 3):
            self.part_copy(k).wait_send()

    def release(self):
        p = self.place
        pl.semaphore_signal(
            self.free_sem.at[0], inc=1, device_id=(p.core_peer, p.t), device_id_type=pl.DeviceIdType.MESH
        )
        for k in (1, 2, 3):
            dp, t, _ = p.group(k)
            pl.semaphore_signal(
                self.free_sem.at[k], inc=1, device_id=(dp, t), device_id_type=pl.DeviceIdType.MESH
            )

    def acquire(self):
        self.finish()
        for k in range(4):
            pl.semaphore_wait(self.free_sem.at[k], 1)


class GroupGather:
    def __init__(self, place, out, size, part_sem, core_sem):
        self.place, self.out, self.half = place, out, size // 2
        self.part_sem, self.core_sem = part_sem, core_sem

    def block(self, x, t):
        p = self.place
        start = ((x * 2 + p.c) * 2 + t) * self.half
        return self.out.at[pl.ds(pl.multiple_of(start, self.half), self.half)]

    def part_copy(self, k):
        p = self.place
        dp, t, _ = p.group(k)
        mine = self.block(p.x, p.t)
        return remote(mine, mine, self.part_sem.at[0, k], self.part_sem.at[1, k], dp, t)

    def core_copy(self, k):
        p = self.place
        _, t, x = p.group(k)
        block = self.block(x, t)
        return remote(block, block, self.core_sem.at[0, k], self.core_sem.at[1, k], p.core_peer, p.t)

    def run(self):
        for k in (3, 2, 1):
            self.part_copy(k).start()
        self.core_copy(0).start()
        for k in (1, 2, 3):
            self.part_copy(k).wait_recv()
            self.core_copy(k).start()
        for k in range(4):
            self.core_copy(k).wait_recv()

    def finish(self):
        for k in (1, 2, 3):
            self.part_copy(k).wait_send()
        for k in range(4):
            self.core_copy(k).wait_send()


class GroupPieces:
    def __init__(self, place, src, out, sem):
        self.place, self.src, self.out, self.sem = place, src, out, sem

    def own(self):
        return pltpu.make_async_copy(self.src, self.out.at[self.place.j], self.sem.at[0, 0])

    def near(self, k):
        p = self.place
        dest = p.core_peer if k == 1 else p.x_peer
        return remote(self.src, self.out.at[p.j], self.sem.at[0, k], self.sem.at[1, k], dest, p.t)

    def relay(self):
        p = self.place
        block = self.out.at[(p.j + 2) % TP]
        return remote(block, block, self.sem.at[0, 3], self.sem.at[1, 3], p.core_peer, p.t)

    def start(self):
        self.near(2).start()
        self.near(1).start()
        self.own().start()

    def pass_on(self):
        self.near(2).wait_recv()
        self.relay().start()

    def arrive(self):
        self.near(1).wait_recv()
        self.relay().wait_recv()
        self.own().wait()

    def finish(self):
        self.near(1).wait_send()
        self.near(2).wait_send()
        self.relay().wait_send()


def tables_of(aux, wide):
    half = ROT // 2
    line = lax.broadcasted_iota(jnp.int32, (aux.shape[1], wide), 0)
    lane = lax.broadcasted_iota(jnp.int32, (aux.shape[1], wide), 1) % HD
    first = lane < half
    second = (lane >= half) & (lane < ROT)

    def spread(pick, sign):
        table = jnp.where(pick, sign, 0.0).astype(F32)
        return lax.dot_general(
            aux, table, (((1,), (0,)), ((), ())), precision=lax.Precision.HIGHEST, preferred_element_type=F32
        )

    rest = lax.broadcasted_iota(jnp.int32, (aux.shape[0], wide), 1) % HD >= ROT
    cos_t = spread((line == lane % half) & (first | second), 1.0) + jnp.where(rest, 1.0, 0.0)
    low_t = spread((line == lane + half) & first, -1.0)
    upp_t = spread((line == lane) & second, 1.0)
    return cos_t, low_t, upp_t


def attend_values(query, key, value, allowed):
    head_of = lax.broadcasted_iota(jnp.int32, query.shape, 1) // HD
    total = jnp.zeros(query.shape, F32)
    for head in range(query.shape[1] // HD):
        mine = head_of == head
        scores = dot(jnp.where(mine, query, jnp.zeros_like(query)), key, 1, 1) * HD ** (-0.5)
        scores = jnp.where(allowed, scores, -1e30)
        weights = jnp.exp(scores - jnp.max(scores, axis=1, keepdims=True))
        prob = weights / jnp.sum(weights, axis=1, keepdims=True)
        total = jnp.where(mine, dot(prob.astype(BF16), value, 1, 0), total)
    return total


def forward_kernel(
    count,
    small_src, aux_src, row_src, tok_src, cot_src, wq_src, wo_src, wg_src, wd_src,
    wq_out, wo_out, wg_out, wd_out, h1_out, h2_out, cot_out, aux_out, row_out,
    qkv, att, hid, slopes, resid, norms,
    wq, wo, wg, wd, tok, h1, h2, small, aux_all, row_all, to_core, from_core, low, own, parts,
    w_send, w_recv, small_sem, aux_sem, row_sem, tok_sem, cot_sem, core_sem, part_sem, part2_sem, core2_sem, out_sem,
):
    p = Place(count)
    size = tok_src.shape[0]
    half = size // 2
    wide = att.shape[1]
    rows = wq_src.shape[1]
    greet(p)

    auxes = GroupPieces(p, aux_src, aux_all, aux_sem)
    rowses = GroupPieces(p, row_src, row_all, row_sem)
    tokens = GroupPieces(p, tok_src, tok, tok_sem)
    cots = GroupPieces(p, cot_src, cot_out, cot_sem)

    def small_copy(dest):
        return remote(small_src, small.at[p.me], small_sem.at[dest], small_sem.at[count], dest, p.t)

    own_small = pltpu.make_async_copy(small_src, small.at[p.me], small_sem.at[count])
    own_small.start()
    each_dest(p, lambda dest, u, j: small_copy(dest).start())
    auxes.start()
    rowses.start()
    tokens.start()
    gathers = [
        WeightGather(p, i, src, dst, w_send, w_recv)
        for i, (src, dst) in enumerate(((wq_src, wq), (wo_src, wo), (wg_src, wg), (wd_src, wd)))
    ]
    gathers[0].start()
    gathers[1].start()
    auxes.pass_on()
    rowses.pass_on()
    tokens.pass_on()
    gathers[2].start()

    wait_bytes(small, small_sem.at[count])
    per_tile = 128 // rows
    for m in range(D // 128):
        tile = jnp.zeros((8, 128), F32)
        for i in range(per_tile):
            tile = tile + small[m * per_tile + i].astype(F32)[0:8]
        norms[0:8, m * 128 : (m + 1) * 128] = tile
    bias_rows = small.shape[1] - 16
    total = jnp.zeros((bias_rows, 128), F32)
    for d in range(count):
        total = total + small[d].astype(F32)[16:]
    for i in range(bias_rows):
        norms[8:9, i * 128 : (i + 1) * 128] = total[i : i + 1]

    auxes.arrive()
    rowses.arrive()
    tokens.arrive()
    aux_out[...] = aux_all[...]
    row_out[...] = row_all[...]

    @pl.loop(0, TP * size // 32)
    def _(i):
        s, at = i // (size // 32), pl.multiple_of(i % (size // 32) * 32, 32)
        values = tok[s, pl.ds(at, 32), :].astype(F32)
        normed, _, _ = layer_norm(values, norms[0:1, :D], norms[1:2, :D])
        h1[pl.ds(pl.multiple_of(i * 32, 32), 32), :] = normed.astype(BF16)

    h1_copy = pltpu.make_async_copy(h1, h1_out, out_sem.at[0])
    h1_copy.start()
    gathers[0].arrive()
    head_wide = (bias_rows * 128) // 3

    @pl.loop(0, TP)
    def _(s):
        at = pl.ds(pl.multiple_of(s * size, size), size)
        proj = dot(h1[at, :], wq[...], 1, 0)
        aux = aux_all[s]
        tables = tables_of(aux, wide)

        def part(k):
            lanes = pl.ds(pl.multiple_of(k * head_wide + p.j * wide, 128), wide)
            return proj[:, k * wide : (k + 1) * wide] + norms[8:9, lanes]

        query = spin(part(0), *tables).astype(BF16)
        key = spin(part(1), *tables).astype(BF16)
        value = part(2).astype(BF16)
        qkv[at, :wide] = query
        qkv[at, wide : 2 * wide] = key
        qkv[at, 2 * wide :] = value
        allowed = mask_of(aux[:, ROT : ROT + 1], row_all[s, 0:1, :], size)
        att[at, :] = attend_values(query, key, value, allowed).astype(BF16)

    gathers[1].arrive()
    sums = GroupSum(p, to_core, from_core, low, own, parts, core_sem, part_sem)

    def attention_product(s, n, step):
        at = pl.ds(pl.multiple_of(s * size, size), size)
        return dot(att[at, :], wo[pl.ds(pl.multiple_of(n * step, step), step), :], 1, 1)

    sums.start(attention_product)
    sums.arrive()

    @pl.loop(0, half // 32)
    def _(i):
        at = pl.multiple_of(i * 32, 32)
        values = tok_src[pl.ds(pl.multiple_of(p.t * half + at, 32), 32), :].astype(F32)
        values = values + sums.total(at, 32)
        resid[pl.ds(at, 32), :] = values
        normed, _, _ = layer_norm(values, norms[2:3, :D], norms[3:4, :D])
        start = (p.j * 2 + p.t) * half + at
        h2[pl.ds(pl.multiple_of(start, 32), 32), :] = normed.astype(BF16)

    spread = GroupGather(p, h2, size, part2_sem, core2_sem)
    spread.run()
    gathers[3].start()
    cots.start()
    h2_copy = pltpu.make_async_copy(h2, h2_out, out_sem.at[1])
    h2_copy.start()
    gathers[2].arrive()

    full = hid.shape[1] - 128
    slope, gain = slopes.at[: TP * size], slopes.at[TP * size :]

    @pl.loop(0, TP)
    def _(s):
        at = pl.ds(pl.multiple_of(s * size, size), size)
        rows_in = h2[at, :]
        gate = dot(rows_in, wg[:, :full], 1, 0)
        up = dot(rows_in, wg[:, full : 2 * full], 1, 0)
        sig = jax.nn.sigmoid(gate)
        hid[at, :full] = (gate * sig * up).astype(BF16)
        slope[at, :full] = (up * sig * (1.0 + gate * (1.0 - sig))).astype(BF16)
        gain[at, :full] = (gate * sig).astype(BF16)
        gate = dot(rows_in, wg[:, 2 * full :], 1, 0)
        up = pltpu.roll(gate, 64, 1)
        sig = jax.nn.sigmoid(gate)
        first = lax.broadcasted_iota(jnp.int32, gate.shape, 1) < 64
        hid[at, full:] = jnp.where(first, gate * sig * up, 0.0).astype(BF16)
        slope[at, full:] = jnp.where(first, up * sig * (1.0 + gate * (1.0 - sig)), 0.0).astype(BF16)
        gain[at, full:] = jnp.where(first, gate * sig, 0.0).astype(BF16)

    copies = [h1_copy, h2_copy]
    for i, (src, dst) in enumerate(((wq, wq_out), (wo, wo_out), (wg, wg_out))):
        copies.append(pltpu.make_async_copy(src, dst, out_sem.at[2 + i]))
        copies[-1].start()
    cots.pass_on()
    cots.arrive()
    gathers[3].arrive()
    copies.append(pltpu.make_async_copy(wd, wd_out, out_sem.at[5]))
    copies[-1].start()
    for copy in copies:
        copy.wait()
    each_dest(p, lambda dest, u, j: small_copy(dest).wait_send())
    for part in (auxes, rowses, tokens, cots, sums, spread, *gathers):
        part.finish()


def forward(count, small, aux, row, tokens, cot, wq, wo, wg, wd):
    size = tokens.shape[0]
    group = TP * size
    wide, pad = wo.shape[2], wd.shape[2]
    any_spec = pl.BlockSpec(memory_space=pl.ANY)
    vmem = pl.BlockSpec(memory_space=pltpu.VMEM)
    dma = pltpu.SemaphoreType.DMA

    def out(*shape, dtype=BF16):
        return jax.ShapeDtypeStruct(shape, dtype)

    weights = [wq, wo, wg, wd]
    return pl.pallas_call(
        functools.partial(forward_kernel, count),
        in_specs=[vmem, vmem, vmem, vmem] + [any_spec] * 5,
        out_specs=[any_spec] * 7 + [vmem] * 8,
        out_shape=[out(D, w.shape[2]) for w in weights]
        + [
            out(group, D),
            out(group, D),
            out(TP, size, D),
            out(TP, size, 128, dtype=F32),
            out(TP, 8, size, dtype=F32),
            out(group, 3 * wide),
            out(group, wide),
            out(group, pad),
            out(2 * group, pad),
            out(size // 2, D, dtype=F32),
            out(16, max(D, 128 * (small.shape[0] - 16)), dtype=F32),
        ],
        scratch_shapes=[pltpu.VMEM((D, w.shape[2]), BF16) for w in weights]
        + [
            pltpu.VMEM((TP, size, D), BF16),
            pltpu.VMEM((group, D), BF16),
            pltpu.VMEM((group, D), BF16),
            pltpu.VMEM((count,) + small.shape, BF16),
            pltpu.VMEM((TP, size, 128), F32),
            pltpu.VMEM((TP, 8, size), F32),
            pltpu.VMEM((2, size, D), BF16),
            pltpu.VMEM((2, size, D), BF16),
            pltpu.VMEM((2, size, D), BF16),
            pltpu.VMEM((size, D), F32),
            pltpu.VMEM((3, size // 2, D), BF16),
            dma((4, count)),
            dma((4, 2)),
            dma((count + 1,)),
            dma((2, 4)),
            dma((2, 4)),
            dma((2, 4)),
            dma((2, 4)),
            dma((2, 2)),
            dma((2, 4)),
            dma((2, 4)),
            dma((2, 4)),
            dma((6,)),
        ],
        compiler_params=pltpu.CompilerParams(
            collective_id=0, has_side_effects=True, vmem_limit_bytes=60 * 1024 * 1024
        ),
        cost_estimate=pl.CostEstimate(flops=12 * 10**9, bytes_accessed=80 * 10**6, transcendentals=10**7),
        name="forward",
    )(small, aux, row, tokens, cot, *weights)


class GradScatter:
    def __init__(self, place, index, grad, out, far, send_sem, recv_sem, far_sem):
        self.place, self.grad, self.out, self.far = place, grad, out, far
        self.send_sem, self.recv_sem, self.far_sem = send_sem.at[index], recv_sem.at[index], far_sem.at[index]
        self.rows = out.shape[2]

    def copy(self, dest, u, j):
        p = self.place
        block = self.grad.at[pl.ds(dest * self.rows, self.rows)]
        far = 0
        if p.lines == 4:
            far = (((p.u == 0) & (u == 2)) | ((p.u == 3) & (u == 1))).astype(jnp.int32)
        return remote(block, self.out.at[p.u, p.j], self.send_sem.at[dest], self.recv_sem.at[far], dest, p.t)

    def outer(self):
        p = self.place
        size = TP * self.rows
        chunk = self.grad.at[pl.ds(jnp.where(p.u == 0, 3, 0) * size, size)]
        dest = p.me + jnp.where(p.u == 0, TP, -TP)
        return remote(chunk, self.far, self.send_sem.at[p.me], self.far_sem, dest, p.t)

    def ends(self):
        return (self.place.u == 0) | (self.place.u == 3)

    def later(self, u):
        p = self.place
        return ((p.u == 1) & (u == 3)) | ((p.u == 2) & (u == 0))

    def start(self):
        p = self.place
        if p.lines == 4:
            pl.when(self.ends())(lambda: self.outer().start())
        own = self.grad.at[pl.ds(p.me * self.rows, self.rows)]

        def act(dest, u, j):
            if p.lines == 4:
                pl.when((jnp.abs(p.u - u) < 3) & ~self.later(u))(lambda: self.copy(dest, u, j).start())
            else:
                self.copy(dest, u, j).start()

        each_dest(p, act)
        pltpu.make_async_copy(own, self.out.at[p.u, p.j], self.recv_sem.at[0]).start()

    def combine(self):
        p = self.place
        if p.lines != 4:
            return
        size = TP * self.rows

        @pl.when(~self.ends())
        def _():
            u = jnp.where(p.u == 1, 3, 0)
            wait_bytes(self.far, self.far_sem)

            @pl.loop(0, size // 32)
            def _(i):
                here = pl.ds(pl.multiple_of(i * 32, 32), 32)
                at = pl.ds(pl.multiple_of(u * size + i * 32, 32), 32)
                total = self.grad[at, :].astype(F32) + self.far[here, :].astype(F32)
                self.grad[at, :] = total.astype(BF16)

            @pl.loop(0, TP)
            def _(q):
                j = (p.j + q) % TP
                self.copy(u * TP + j, u, j).start()

    def arrive(self):
        p = self.place
        if p.lines == 4:
            wait_bytes(self.out.at[pl.ds(0, 3)], self.recv_sem.at[0])
            pl.when(~self.ends())(lambda: wait_bytes(self.out.at[0], self.recv_sem.at[1]))
        else:
            wait_bytes(self.out, self.recv_sem.at[0])

    def finish(self):
        p = self.place

        def act(dest, u, j):
            if p.lines == 4:
                pl.when(jnp.abs(p.u - u) < 3)(lambda: self.copy(dest, u, j).wait_send())
            else:
                self.copy(dest, u, j).wait_send()

        each_dest(p, act)
        if p.lines == 4:
            pl.when(self.ends())(lambda: self.outer().wait_send())


def norm_stats(values):
    centre = values - jnp.mean(values, axis=-1, keepdims=True)
    inverse = lax.rsqrt(jnp.mean(centre * centre, axis=-1, keepdims=True) + 1e-05)
    return centre * inverse, inverse


def backward_kernel(
    count,
    aux, row, tok, resid, norms, hid_in, cot_in, slopes_in, wd_in, wg_in, wo_in, wq_in, h2_in, h1_in, qkv_in, att_in,
    rs_q, rs_o, rs_g, rs_d, block_out, input_out, norm_out, bias_out,
    wd, wg, wo, cot, hid, slopes, hh, qkv, att, dgate, gd, gg, go, far_d, far_g, far_o, far_q,
    to_core, from_core, low, own, parts, grad, block, gains, biases, small_all, bias_all, small_t,
    load_sem, rs_send, rs_recv, rs_far, core_sem, part_sem, free_sem, part2_sem, core2_sem,
    swap_sem, small_sem, bias_sem, rank_sem, t_sem,
):
    p = Place(count)
    size = tok.shape[0]
    half = size // 2
    group = TP * size
    wide = att.shape[1]
    full = hid.shape[1] - 128
    loads = {}
    for i, (name, src, dst) in enumerate(
        (
            ("wd", wd_in, wd), ("cot", cot_in, cot), ("slopes", slopes_in, slopes.at[: 2 * group, : hid.shape[1]]),
            ("hid", hid_in, hid), ("wg", wg_in, wg), ("h2", h2_in, hh), ("wo", wo_in, wo), ("att", att_in, att),
            ("qkv", qkv_in, qkv),
        )
    ):
        loads[name] = pltpu.make_async_copy(src, dst, load_sem.at[i])
        loads[name].start()
    greet(p)
    gq = slopes.at[:D, : 3 * wide]
    wq = wg.at[:, : 3 * wide]
    scatter_q, scatter_o, scatter_g, scatter_d = [
        GradScatter(p, i, g, out, far, rs_send, rs_recv, rs_far)
        for i, (g, out, far) in enumerate(
            ((gq, rs_q, far_q), (go, rs_o, far_o), (gg, rs_g, far_g), (gd, rs_d, far_d))
        )
    ]
    sums = GroupSum(p, to_core, from_core, low, own, parts, core_sem, part_sem, free_sem)

    def rows_of(s):
        return pl.ds(pl.multiple_of(s * size, size), size)

    for name in ("wd", "cot", "slopes"):
        loads[name].wait()

    @pl.loop(0, TP)
    def _(s):
        at = rows_of(s)
        dhid = dot(cot[at, :], wd[...], 1, 0)
        slope = dhid * slopes[at, : hid.shape[1]].astype(F32)
        gain = dhid * slopes[pl.ds(pl.multiple_of(group + s * size, size), size), : hid.shape[1]].astype(F32)
        dgate[at, :full] = slope[:, :full].astype(BF16)
        dgate[at, full : 2 * full] = gain[:, :full].astype(BF16)
        last = slope[:, full:] + pltpu.roll(gain[:, full:], 64, 1)
        dgate[at, 2 * full :] = last.astype(BF16)

    step = min(256, D)

    def weight_grad(left, right, out):
        @pl.loop(0, D // step)
        def _(n):
            at = pl.ds(pl.multiple_of(n * step, step), step)
            out[at, :] = dot(left[:, at], right[...], 0, 0).astype(BF16)

    loads["hid"].wait()
    weight_grad(cot, hid, gd)
    scatter_d.start()

    loads["wg"].wait()
    sums.start(
        lambda s, n, step: dot(dgate[rows_of(s), :], wg[pl.ds(pl.multiple_of(n * step, step), step), :], 1, 1)
    )
    load_wq = pltpu.make_async_copy(wq_in, wq, load_sem.at[9])
    load_wq.start()
    loads["h2"].wait()
    weight_grad(hh, dgate, gg)
    scatter_g.start()
    load_h1 = pltpu.make_async_copy(h1_in, hh, load_sem.at[10])
    load_h1.start()
    scatter_d.combine()
    sums.arrive()

    gains[...] = jnp.zeros_like(gains)

    @pl.loop(0, half // 32)
    def _(i):
        at = pl.multiple_of(i * 32, 32)
        scaled, inverse = norm_stats(resid[pl.ds(at, 32), :])
        grad_in = sums.total(at, 32)
        part, gain, shift = norm_back(grad_in, scaled, inverse, norms[2:3, :D])
        gains[2:3, :] += gain[None]
        gains[3:4, :] += shift[None]
        mine = pl.ds(pl.multiple_of((p.j * 2 + p.t) * half + at, 32), 32)
        total = cot[mine, :].astype(F32) + part
        grad[pl.ds(at, 32), :] = total
        cot[mine, :] = total.astype(BF16)

    sums.release()
    spread = GroupGather(p, cot, size, part2_sem, core2_sem)
    spread.run()
    scatter_g.combine()

    for name in ("wo", "att", "qkv"):
        loads[name].wait()
    biases[...] = jnp.zeros_like(biases)

    @pl.loop(0, TP)
    def _(s):
        at = rows_of(s)
        grad_out = dot(cot[at, :], wo[...], 1, 0).astype(BF16)
        allowed = mask_of(aux[s][:, ROT : ROT + 1], row[s, 0:1, :], size)
        tables = tables_of(aux[s], wide)
        three = attend_back_values(
            qkv[at, :wide], qkv[at, wide : 2 * wide], qkv[at, 2 * wide :], grad_out, allowed, tables
        )
        for k, value in enumerate(three):
            lanes = slice(k * wide, (k + 1) * wide)
            qkv[at, lanes] = value
            biases[0:1, lanes] += jnp.sum(value.astype(F32), axis=0, keepdims=True)

    load_h1.wait()
    weight_grad(hh, qkv, gq)
    scatter_q.start()
    weight_grad(cot, att, go)
    scatter_o.start()

    bias_all[p.u] = biases[...]

    def bias_copy(k):
        u = (p.u + k) % p.lines
        return remote(biases, bias_all.at[p.u], bias_sem.at[k], bias_sem.at[p.lines + k], u * TP + p.j, p.t)

    for k in range(1, p.lines):
        bias_copy(k).start()

    load_wq.wait()
    sums.acquire()
    sums.start(
        lambda s, n, step: dot(qkv[rows_of(s), :], wq[pl.ds(pl.multiple_of(n * step, step), step), :], 1, 1)
    )
    scatter_q.combine()
    scatter_o.combine()
    sums.arrive()

    @pl.loop(0, half // 32)
    def _(i):
        at = pl.multiple_of(i * 32, 32)
        values = tok[pl.ds(pl.multiple_of(p.t * half + at, 32), 32), :].astype(F32)
        scaled, inverse = norm_stats(values)
        part, gain, shift = norm_back(sums.total(at, 32), scaled, inverse, norms[0:1, :D])
        gains[0:1, :] += gain[None]
        gains[1:2, :] += shift[None]
        grad[pl.ds(at, 32), :] += part

    sums.release()
    mine = pl.ds(pl.multiple_of(p.t * half, half), half)

    def give(index, value, out):
        here = pltpu.make_async_copy(value, out.at[mine], swap_sem.at[index, 0])
        there = remote(value, out.at[mine], swap_sem.at[index, 1], swap_sem.at[index, 2], p.me, 1 - p.t)
        here.start()
        there.start()
        return here, there

    gives = [*give(0, grad, input_out)]

    rows = rs_q.shape[2]

    def tile_of(d):
        return pl.ds(pl.multiple_of(d * rows // 128 * 128, 128), 128)

    def small_copy(dest):
        return remote(gains.at[:, tile_of(dest)], small_all.at[p.me], small_sem.at[dest], small_sem.at[count], dest, p.t)

    own_small = pltpu.make_async_copy(gains.at[:, tile_of(p.me)], small_all.at[p.me], small_sem.at[count])
    own_small.start()
    each_dest(p, lambda dest, u, j: small_copy(dest).start())

    for k in range(1, p.lines):
        bias_copy(k).wait_recv()
    total = bias_all[0]
    for k in range(1, p.lines):
        total = total + bias_all[k]
    bias_out[p.j] = total

    def rank_copy(q):
        j = (p.j + q) % TP
        return remote(bias_out.at[p.j], bias_out.at[p.j], rank_sem.at[q], rank_sem.at[TP + q], p.u * TP + j, p.t)

    for q in range(1, TP):
        rank_copy(q).start()

    sums.acquire()
    sums.start(lambda s, n, step: dot(hid[rows_of(s), :], wd[pl.ds(pl.multiple_of(n * step, step), step), :], 1, 1))
    sums.arrive()

    @pl.loop(0, half // 32)
    def _(i):
        at = pl.multiple_of(i * 32, 32)
        block[pl.ds(at, 32), :] = resid[pl.ds(at, 32), :] + sums.total(at, 32)

    gives += give(1, block, block_out)

    wait_bytes(small_all, small_sem.at[count])
    total = small_all[0]
    for d in range(1, count):
        total = total + small_all[d]
    small_t[0] = total
    swap = remote(small_t.at[0], small_t.at[1], t_sem.at[0], t_sem.at[1], p.me, 1 - p.t)
    swap.start()
    swap.wait()
    norm_out[...] = small_t[0] + small_t[1]
    for q in range(1, TP):
        rank_copy(q).wait()
    for k in range(1, p.lines):
        bias_copy(k).wait_send()
    each_dest(p, lambda dest, u, j: small_copy(dest).wait_send())
    for copy in gives:
        copy.wait()
    sums.finish()
    spread.finish()
    for scatter in (scatter_d, scatter_g, scatter_q, scatter_o):
        scatter.arrive()
        scatter.finish()


def backward(count, aux, row, tok, resid, norms, hid, cot, slopes, wd, wg, wo, wq, h2, h1, qkv, att):
    size = tok.shape[0]
    half = size // 2
    group = TP * size
    wide, pad = wo.shape[1], wd.shape[1]
    lines, rows = count // TP, D // count
    any_spec = pl.BlockSpec(memory_space=pl.ANY)
    vmem = pl.BlockSpec(memory_space=pltpu.VMEM)
    dma = pltpu.SemaphoreType.DMA

    def out(*shape, dtype=BF16):
        return jax.ShapeDtypeStruct(shape, dtype)

    def far(width):
        return pltpu.VMEM((TP * rows if lines == 4 else 16, width), BF16)

    return pl.pallas_call(
        functools.partial(backward_kernel, count),
        in_specs=[vmem] * 5 + [any_spec] * 11,
        out_specs=[any_spec] * 6 + [vmem] * 2,
        out_shape=[
            out(lines, TP, rows, 3 * wide),
            out(lines, TP, rows, wide),
            out(lines, TP, rows, wg.shape[1]),
            out(lines, TP, rows, pad),
            out(size, D, dtype=F32),
            out(size, D, dtype=F32),
            out(8, 128, dtype=F32),
            out(TP, 8, 3 * wide, dtype=F32),
        ],
        scratch_shapes=[
            pltpu.VMEM((D, pad), BF16),
            pltpu.VMEM((D, wg.shape[1]), BF16),
            pltpu.VMEM((D, wide), BF16),
            pltpu.VMEM((group, D), BF16),
            pltpu.VMEM((group, pad), BF16),
            pltpu.VMEM((max(2 * group, D), max(pad, 3 * wide)), BF16),
            pltpu.VMEM((group, D), BF16),
            pltpu.VMEM((group, 3 * wide), BF16),
            pltpu.VMEM((group, wide), BF16),
            pltpu.VMEM((group, wg.shape[1]), BF16),
            pltpu.VMEM((D, pad), BF16),
            pltpu.VMEM((D, wg.shape[1]), BF16),
            pltpu.VMEM((D, wide), BF16),
            far(pad),
            far(wg.shape[1]),
            far(wide),
            far(3 * wide),
            pltpu.VMEM((2, size, D), BF16),
            pltpu.VMEM((2, size, D), BF16),
            pltpu.VMEM((2, size, D), BF16),
            pltpu.VMEM((size, D), F32),
            pltpu.VMEM((3, half, D), BF16),
            pltpu.VMEM((half, D), F32),
            pltpu.VMEM((half, D), F32),
            pltpu.VMEM((8, D), F32),
            pltpu.VMEM((8, 3 * wide), F32),
            pltpu.VMEM((count, 8, 128), F32),
            pltpu.VMEM((lines, 8, 3 * wide), F32),
            pltpu.VMEM((2, 8, 128), F32),
            dma((11,)),
            dma((4, count)),
            dma((4, 2)),
            dma((4,)),
            dma((2, 2)),
            dma((2, 4)),
            pltpu.SemaphoreType.REGULAR((4,)),
            dma((2, 4)),
            dma((2, 4)),
            dma((2, 3)),
            dma((count + 1,)),
            dma((2 * lines,)),
            dma((2 * TP,)),
            dma((2,)),
        ],
        compiler_params=pltpu.CompilerParams(
            collective_id=1, has_side_effects=True, vmem_limit_bytes=62 * 1024 * 1024
        ),
        cost_estimate=pl.CostEstimate(flops=27 * 10**9, bytes_accessed=120 * 10**6, transcendentals=10**7),
        name="backward",
    )(aux, row, tok, resid, norms, hid, cot, slopes, wd, wg, wo, wq, h2, h1, qkv, att)


def per_device(
    count,
    tokens_in,
    segment_ids,
    d_out,
    qkv_weight,
    qkv_bias,
    out_weight,
    gating_weight,
    down_weight,
    norm_params,
    qkv_first,
    qkv_second,
    bias_first,
    bias_second,
    out_first,
    out_second,
    gating_first,
    gating_second,
    down_first,
    down_second,
    norm_first,
    norm_second,
):
    place = lax.axis_index("dp")
    rows = norm_params.shape[1]
    seq_len = tokens_in.shape[1]
    head_local = qkv_weight.shape[2]
    hidden_local = gating_weight.shape[2]
    wide = head_local // TP
    hid = hidden_local // TP
    full = hid // 128 * 128

    def cut(shard):
        return shard.astype(BF16).transpose(1, 0, 2)

    gates = gating_weight.astype(BF16).reshape(rows, 2, TP, hid)
    gates = jnp.concatenate(
        [gates[:, 0, :, :full], gates[:, 1, :, :full], gates[:, 0, :, full:], gates[:, 1, :, full:]], axis=2
    )
    downs = jnp.pad(down_weight.T.reshape(rows, TP, hid), ((0, 0), (0, 0), (0, -hid % 128)))
    weights = (
        cut(qkv_weight.reshape(rows, 3, TP, wide).transpose(0, 2, 1, 3).reshape(rows, TP, 3 * wide)),
        cut(out_weight.T.reshape(rows, TP, wide)),
        gates.transpose(1, 0, 2),
        cut(downs),
    )
    bias_here = qkv_bias.shape[1]
    small_norm = lax.dynamic_update_slice(jnp.zeros((16, 128), F32), norm_params, (0, (place * rows) % 128))
    small_bias = lax.dynamic_update_slice(jnp.zeros((3 * head_local,), F32), qkv_bias[0], (place * bias_here,))
    small = jnp.concatenate([small_norm, small_bias.reshape(-1, 128)]).astype(BF16)
    segments = segment_ids[0]
    earlier = jnp.sum((segments[None, :] < segments[:, None]).astype(jnp.int32), axis=1)
    positions = (jnp.arange(seq_len, dtype=jnp.int32) - earlier).astype(F32)
    frequency = 10000.0 ** (-2.0 * jnp.arange(ROT // 2, dtype=F32) / ROT)
    angles = positions[:, None] * frequency[None, :]
    aux = jnp.concatenate([jnp.cos(angles), jnp.sin(angles), segments[:, None].astype(F32)], axis=1)
    aux = jnp.pad(aux, ((0, 0), (0, 128 - aux.shape[1])))
    row = jnp.broadcast_to(segments.astype(F32)[None], (8, seq_len))

    wq, wo, wg, wd, h1, h2, cot, aux_all, row_all, qkv, att, hidden, slopes, resid, norms = forward(
        count, small, aux, row, tokens_in[0], d_out[0], *weights
    )
    cot = cot.reshape(TP * seq_len, D)
    rs_q, rs_o, rs_g, rs_d, block_out, input_grad, norm_sum, bias_sum = backward(
        count, aux_all, row_all, tokens_in[0], resid, norms, hidden, cot, slopes, wd, wg, wo, wq, h2, h1, qkv, att
    )

    lines = count // TP
    line = place // TP

    def total(parts):
        summed = 0.0
        for u in range(lines):
            piece = parts[u].astype(F32)
            if lines == 4 and u in (0, 3):
                piece = jnp.where(line == 3 - u, 0.0, piece)
            summed = summed + piece
        return summed.transpose(1, 0, 2)

    gating_parts = total(rs_g)
    gate_parts = jnp.concatenate([gating_parts[..., :full], gating_parts[..., 2 * full : full + hid]], axis=2)
    up_parts = jnp.concatenate([gating_parts[..., full : 2 * full], gating_parts[..., full + hid :]], axis=2)
    gating_shard = jnp.stack([gate_parts, up_parts], axis=1).reshape(gating_weight.shape)
    qkv_shard = total(rs_q).reshape(rows, TP, 3, wide).transpose(0, 2, 1, 3).reshape(qkv_weight.shape)
    out_shard = total(rs_o).reshape(rows, head_local).T
    down_shard = total(rs_d)[..., :hid].reshape(rows, hidden_local).T
    norm_grad = lax.dynamic_slice_in_dim(norm_sum[:4], (place * rows) % 128, rows, 1)
    bias_grad = bias_sum[:, 0].reshape(TP, 3, wide).transpose(1, 0, 2).reshape(1, 3 * head_local)
    bias_grad = lax.dynamic_slice_in_dim(bias_grad, place * bias_here, bias_here, 1)
    return (
        block_out[None],
        input_grad[None],
        *adamw_update(qkv_weight, qkv_shard, qkv_first, qkv_second, D ** (-0.5), 0.1),
        *adamw_update(qkv_bias, bias_grad, bias_first, bias_second, 0.3, 0.0),
        *adamw_update(out_weight, out_shard, out_first, out_second, (H * HD // 16) ** (-0.5), 0.1),
        *adamw_update(gating_weight, gating_shard, gating_first, gating_second, D ** (-0.5), 0.1),
        *adamw_update(down_weight, down_shard, down_first, down_second, FF ** (-0.5), 0.1),
        *adamw_update(norm_params, norm_grad, norm_first, norm_second, 0.25, 0.0),
    )


def solution(mesh):
    tokens = P("dp", None, None)
    qkv = P("dp", None, "tensor")
    rest = P("tensor", "dp")
    norm = P(None, "dp")
    weights = (qkv, rest, rest, qkv, rest, norm)
    states = (qkv, qkv, rest, rest, rest, rest, qkv, qkv, rest, rest, norm, norm)
    return jax.shard_map(
        functools.partial(per_device, mesh.shape["dp"]),
        mesh=mesh,
        in_specs=(tokens, P("dp", None), tokens, *weights, *states),
        out_specs=(tokens, tokens, *(spec for spec in weights for _ in range(3))),
        check_vma=False,
    )
```

```python
import functools

import jax
import jax.numpy as jnp
from jax import lax
from jax.experimental import pallas as pl
from jax.experimental.pallas import tpu as pltpu
from jax.sharding import PartitionSpec as P

D = 2048
H = 32
HD = 64
ROT = 16
FF = 5632
STEP = 10
TP = 4

F32 = jnp.float32
BF16 = jnp.bfloat16


def layer_norm(values, scale_row, shift_row):
    centre = values - jnp.mean(values, axis=-1, keepdims=True)
    spread = jnp.mean(centre * centre, axis=-1, keepdims=True)
    inverse = lax.rsqrt(spread + 1e-05)
    scaled = centre * inverse
    return (scaled * scale_row + shift_row, scaled, inverse)


def norm_back(grad_in, scaled, inverse, scale_row):
    grad_scaled = grad_in * scale_row
    mean_first = jnp.mean(grad_scaled, axis=-1, keepdims=True)
    mean_second = jnp.mean(grad_scaled * scaled, axis=-1, keepdims=True)
    grad_values = inverse * (grad_scaled - mean_first - scaled * mean_second)
    return (grad_values, jnp.sum(grad_in * scaled, axis=0), jnp.sum(grad_in, axis=0))


def adamw_update(weight_old, gradient, first_old, second_old, step_rate, decay_rate):
    first_new = 0.9 * first_old + 0.1 * gradient
    second_new = 0.95 * second_old + 0.05 * gradient * gradient
    corrected = first_new / (1.0 - 0.9**STEP) / (jnp.sqrt(second_new / (1.0 - 0.95**STEP)) + 1e-08)
    return (weight_old - step_rate * (corrected + decay_rate * weight_old), first_new, second_new)


def dot(a, b, ca, cb):
    return lax.dot_general(a, b, (((ca,), (cb,)), ((), ())), preferred_element_type=F32)


def spin(values, cos_t, lower_t, upper_t):
    wide = values.shape[1]
    return (
        values * cos_t
        + pltpu.roll(values, wide - ROT // 2, 1) * lower_t
        + pltpu.roll(values, ROT // 2, 1) * upper_t
    )


def spin_back(values, cos_t, lower_t, upper_t):
    wide = values.shape[1]
    return (
        values * cos_t
        + pltpu.roll(values * lower_t, ROT // 2, 1)
        + pltpu.roll(values * upper_t, wide - ROT // 2, 1)
    )


def mask_of(seg_col, seg_row, size):
    rows = lax.broadcasted_iota(jnp.int32, (size, size), 0)
    cols = lax.broadcasted_iota(jnp.int32, (size, size), 1)
    return (seg_col == seg_row) & (cols <= rows)


def attend_back_values(query, key, value, grad, allowed, tables):
    head_of = lax.broadcasted_iota(jnp.int32, query.shape, 1) // HD
    zero = jnp.zeros_like(query)
    dq = jnp.zeros(query.shape, F32)
    dk = jnp.zeros(query.shape, F32)
    dv = jnp.zeros(query.shape, F32)
    for head in range(query.shape[1] // HD):
        mine = head_of == head
        query_h = jnp.where(mine, query, zero)
        grad_h = jnp.where(mine, grad, zero)
        scores = dot(query_h, key, 1, 1) * HD ** (-0.5)
        scores = jnp.where(allowed, scores, -1e30)
        weights = jnp.exp(scores - jnp.max(scores, axis=1, keepdims=True))
        prob = weights / jnp.sum(weights, axis=1, keepdims=True)
        dv = dv + dot(prob.astype(BF16), grad_h, 0, 0)
        dprob = dot(grad_h, value, 1, 1)
        delta = jnp.sum(prob * dprob, axis=1, keepdims=True)
        dscore = (prob * (dprob - delta)).astype(BF16)
        dq = jnp.where(mine, dot(dscore, key, 1, 0), dq)
        dk = dk + dot(dscore, query_h, 0, 0)
    dq = spin_back(dq * HD ** (-0.5), *tables).astype(BF16)
    dk = spin_back(dk * HD ** (-0.5), *tables).astype(BF16)
    return dq, dk, dv.astype(BF16)


class Place:
    def __init__(self, count):
        self.count = count
        self.lines = count // TP
        self.me = lax.axis_index("dp")
        self.t = lax.axis_index("tensor")
        self.u = self.me // TP
        self.j = self.me % TP
        self.x = self.j // 2
        self.c = self.j % 2
        self.core_peer = self.me + 1 - 2 * self.c
        self.x_peer = self.me + 2 - 4 * self.x

    def group(self, k):
        x = (self.x + k // 2) % 2
        return self.u * TP + x * 2 + self.c, (self.t + k % 2) % 2, x


def remote(src, dst, send_sem, recv_sem, dp, t):
    return pltpu.make_async_remote_copy(
        src_ref=src,
        dst_ref=dst,
        send_sem=send_sem,
        recv_sem=recv_sem,
        device_id=(dp, t),
        device_id_type=pl.DeviceIdType.MESH,
    )


def wait_bytes(ref, sem):
    pltpu.make_async_copy(ref, ref, sem).wait()


def greet(place):
    barrier = pltpu.get_barrier_semaphore()

    @pl.loop(1, place.count)
    def _(k):
        pl.semaphore_signal(
            barrier,
            inc=1,
            device_id=((place.me + k) % place.count, place.t),
            device_id_type=pl.DeviceIdType.MESH,
        )

    for k in (1, 3):
        dp, t, _ = place.group(k)
        pl.semaphore_signal(barrier, inc=1, device_id=(dp, t), device_id_type=pl.DeviceIdType.MESH)
    pl.semaphore_wait(barrier, place.count + 1)


def each_dest(place, act):
    if place.lines == 4:

        @pl.loop(1, TP)
        def _(q):
            j = (place.j + q) % TP
            act(place.u * TP + j, place.u, j)

        @pl.loop(0, TP)
        def _(q):
            j = (place.j + q) % TP
            for dz in (2, 1, 3):
                u = (place.u + dz) % 4
                act(u * TP + j, u, j)

    else:

        @pl.loop(1, place.count)
        def _(k):
            dest = (place.me + k) % place.count
            act(dest, dest // TP, dest % TP)


class WeightGather:
    def __init__(self, place, index, src, dst, send_sem, recv_sem):
        self.place, self.src, self.dst = place, src, dst
        self.send_sem, self.recv_sem = send_sem.at[index], recv_sem.at[index]
        self.rows = src.shape[1]

    def group_copy(self, q):
        p = self.place
        j = (p.j + q) % TP
        mine = self.dst.at[pl.ds(p.me * self.rows, self.rows)]
        return remote(self.src.at[j], mine, self.send_sem.at[q], self.recv_sem.at[2], p.u * TP + j, p.t)

    def chunk(self, u):
        size = TP * self.rows
        return self.dst.at[pl.ds(u * size, size)]

    def line_copy(self, k):
        p = self.place
        u = (p.u + k) % p.lines
        far = 0
        if p.lines == 4:
            far = (((p.u == 0) & (u == 2)) | ((p.u == 3) & (u == 1))).astype(jnp.int32)
        mine = self.chunk(p.u)
        return remote(mine, mine, self.send_sem.at[TP + k], self.recv_sem.at[far], u * TP + p.j, p.t)

    def line_each(self, act):
        p = self.place
        if p.lines == 4:
            for k in (2, 1, 3):
                pl.when(jnp.abs(p.u - (p.u + k) % 4) < 3)(lambda k=k: act(k))
        else:
            for k in range(1, p.lines):
                act(k)

    def start(self):
        p = self.place
        for q in (2, 3, 1):
            self.group_copy(q).start()
        mine = self.dst.at[pl.ds(p.me * self.rows, self.rows)]
        pltpu.make_async_copy(self.src.at[p.j], mine, self.recv_sem.at[2]).start()

    def pass_on(self):
        wait_bytes(self.chunk(0), self.recv_sem.at[2])
        self.line_each(lambda k: self.line_copy(k).start())

    def middle(self):
        return (self.place.u == 1) | (self.place.u == 2)

    def forward(self):
        p = self.place
        chunk = self.chunk(jnp.where(p.u == 2, 0, 3))
        dest = p.me + jnp.where(p.u == 2, TP, -TP)
        return remote(chunk, chunk, self.send_sem.at[TP], self.recv_sem.at[1], dest, p.t)

    def relay(self):
        if self.place.lines == 4:

            @pl.when(self.middle())
            def _():
                wait_bytes(self.chunk(0), self.recv_sem.at[1])
                self.forward().start()

    def arrive(self):
        p = self.place
        size = TP * self.rows
        wait_bytes(self.dst.at[pl.ds(0, size * (2 if p.lines == 4 else p.lines - 1))], self.recv_sem.at[0])
        if p.lines == 4:
            pl.when(~self.middle())(lambda: wait_bytes(self.chunk(0), self.recv_sem.at[1]))

    def finish(self):
        for q in range(1, TP):
            self.group_copy(q).wait_send()
        self.line_each(lambda k: self.line_copy(k).wait_send())
        if self.place.lines == 4:
            pl.when(self.middle())(lambda: self.forward().wait_send())


class GroupSum:
    def __init__(self, place, to_core, from_core, low, own, parts, core_sem, part_sem, free_sem=None):
        self.place = place
        self.to_core, self.from_core, self.low, self.own, self.parts = to_core, from_core, low, own, parts
        self.core_sem, self.part_sem, self.free_sem = core_sem, part_sem, free_sem

    def core_copy(self, i):
        p = self.place
        return remote(
            self.to_core.at[i], self.from_core.at[i], self.core_sem.at[0, i], self.core_sem.at[1, i], p.core_peer, p.t
        )

    def part_copy(self, k):
        p = self.place
        half = self.parts.shape[1]
        dp, t, _ = p.group(k)
        block = self.low.at[0 if k >= 2 else 1, pl.ds(pl.multiple_of(t * half, half), half)]
        return remote(block, self.parts.at[k - 1], self.part_sem.at[0, k], self.part_sem.at[1, k], dp, t)

    def start(self, product):
        p = self.place
        step = min(512, D)
        other = [(p.x + 1) % 2, p.x]
        for i in range(2):

            @pl.loop(0, D // step)
            def _(n):
                at = pl.ds(pl.multiple_of(n * step, step), step)
                self.to_core[i, :, at] = product(other[i] * 2 + 1 - p.c, n, step).astype(BF16)

            self.core_copy(i).start()
        for i in range(2):
            self.core_copy(i).wait_recv()

            @pl.loop(0, D // step)
            def _(n):
                at = pl.ds(pl.multiple_of(n * step, step), step)
                total = product(other[i] * 2 + p.c, n, step) + self.from_core[i, :, at].astype(F32)
                self.low[i, :, at] = total.astype(BF16)
                if i == 1:
                    half = self.own.shape[0]

                    @pl.when(p.t == 0)
                    def _():
                        self.own[:, at] = total[:half]

                    @pl.when(p.t == 1)
                    def _():
                        self.own[:, at] = total[half:]

            for k in (3, 2) if i == 0 else (1,):
                self.part_copy(k).start()

    def arrive(self):
        for k in (3, 2, 1):
            self.part_copy(k).wait_recv()

    def total(self, at, rows):
        value = self.own[pl.ds(pl.multiple_of(at, 32), rows), :]
        for k in range(3):
            value = value + self.parts[k, pl.ds(pl.multiple_of(at, 32), rows), :].astype(F32)
        return value

    def finish(self):
        for i in range(2):
            self.core_copy(i).wait_send()
        for k in (1, 2, 3):
            self.part_copy(k).wait_send()

    def release(self):
        p = self.place
        pl.semaphore_signal(
            self.free_sem.at[0], inc=1, device_id=(p.core_peer, p.t), device_id_type=pl.DeviceIdType.MESH
        )
        for k in (1, 2, 3):
            dp, t, _ = p.group(k)
            pl.semaphore_signal(
                self.free_sem.at[k], inc=1, device_id=(dp, t), device_id_type=pl.DeviceIdType.MESH
            )

    def acquire(self):
        self.finish()
        for k in range(4):
            pl.semaphore_wait(self.free_sem.at[k], 1)


class GroupGather:
    def __init__(self, place, out, size, part_sem, core_sem):
        self.place, self.out, self.half = place, out, size // 2
        self.part_sem, self.core_sem = part_sem, core_sem

    def block(self, x, t):
        p = self.place
        start = ((x * 2 + p.c) * 2 + t) * self.half
        return self.out.at[pl.ds(pl.multiple_of(start, self.half), self.half)]

    def part_copy(self, k):
        p = self.place
        dp, t, _ = p.group(k)
        mine = self.block(p.x, p.t)
        return remote(mine, mine, self.part_sem.at[0, k], self.part_sem.at[1, k], dp, t)

    def core_copy(self, k):
        p = self.place
        _, t, x = p.group(k)
        block = self.block(x, t)
        return remote(block, block, self.core_sem.at[0, k], self.core_sem.at[1, k], p.core_peer, p.t)

    def start(self):
        for k in (3, 2, 1):
            self.part_copy(k).start()
        self.core_copy(0).start()

    def arrive(self):
        for k in (1, 2, 3):
            self.part_copy(k).wait_recv()
            self.core_copy(k).start()
        for k in range(4):
            self.core_copy(k).wait_recv()

    def finish(self):
        for k in (1, 2, 3):
            self.part_copy(k).wait_send()
        for k in range(4):
            self.core_copy(k).wait_send()


class GroupPieces:
    def __init__(self, place, src, out, sem, size=0):
        self.place, self.src, self.out, self.sem, self.size = place, src, out, sem, size

    def at(self, j):
        if self.size:
            return self.out.at[pl.ds(pl.multiple_of(j * self.size, self.size), self.size)]
        return self.out.at[j]

    def own(self):
        return pltpu.make_async_copy(self.src, self.at(self.place.j), self.sem.at[0, 0])

    def near(self, k):
        p = self.place
        dest = p.core_peer if k == 1 else p.x_peer
        return remote(self.src, self.at(p.j), self.sem.at[0, k], self.sem.at[1, k], dest, p.t)

    def relay(self):
        p = self.place
        block = self.at((p.j + 2) % TP)
        return remote(block, block, self.sem.at[0, 3], self.sem.at[1, 3], p.core_peer, p.t)

    def start(self):
        self.near(2).start()
        self.near(1).start()
        self.own().start()

    def pass_on(self):
        self.near(2).wait_recv()
        self.relay().start()

    def arrive(self):
        self.near(1).wait_recv()
        self.relay().wait_recv()
        self.own().wait()

    def finish(self):
        self.near(1).wait_send()
        self.near(2).wait_send()
        self.relay().wait_send()


def tables_of(aux, wide):
    half = ROT // 2
    line = lax.broadcasted_iota(jnp.int32, (aux.shape[1], wide), 0)
    lane = lax.broadcasted_iota(jnp.int32, (aux.shape[1], wide), 1) % HD
    first = lane < half
    second = (lane >= half) & (lane < ROT)

    def spread(pick, sign):
        table = jnp.where(pick, sign, 0.0).astype(F32)
        return lax.dot_general(
            aux, table, (((1,), (0,)), ((), ())), precision=lax.Precision.HIGHEST, preferred_element_type=F32
        )

    rest = lax.broadcasted_iota(jnp.int32, (aux.shape[0], wide), 1) % HD >= ROT
    cos_t = spread((line == lane % half) & (first | second), 1.0) + jnp.where(rest, 1.0, 0.0)
    low_t = spread((line == lane + half) & first, -1.0)
    upp_t = spread((line == lane) & second, 1.0)
    return cos_t, low_t, upp_t


def attend_values(query, key, value, allowed):
    head_of = lax.broadcasted_iota(jnp.int32, query.shape, 1) // HD
    total = jnp.zeros(query.shape, F32)
    for head in range(query.shape[1] // HD):
        mine = head_of == head
        scores = dot(jnp.where(mine, query, jnp.zeros_like(query)), key, 1, 1) * HD ** (-0.5)
        scores = jnp.where(allowed, scores, -1e30)
        weights = jnp.exp(scores - jnp.max(scores, axis=1, keepdims=True))
        prob = weights / jnp.sum(weights, axis=1, keepdims=True)
        total = jnp.where(mine, dot(prob.astype(BF16), value, 1, 0), total)
    return total


class GradScatter:
    def __init__(self, place, index, grad, slots, out, send_sem, recv_sem, free_sem=None):
        self.place, self.grad, self.slots, self.out = place, grad, slots, out
        self.send_sem, self.recv_sem, self.free_sem = send_sem.at[index], recv_sem.at[index], free_sem
        self.rows = out.shape[1]
        self.size = TP * self.rows

    def chunk(self, ref, u):
        return ref.at[pl.ds(u * self.size, self.size)]

    def near(self, u):
        return jnp.abs(self.place.u - u) < 3 if self.place.lines == 4 else None

    def line_each(self, act, picked=lambda u: True):
        p = self.place
        for k in (2, 1, 3) if p.lines == 4 else range(1, p.lines):
            u = (p.u + k) % p.lines
            if p.lines == 4:
                pl.when(self.near(u) & picked(u))(lambda k=k, u=u: act(k, u))
            else:
                act(k, u)

    def line_copy(self, k, u):
        p = self.place
        far = 0
        if p.lines == 4:
            far = (((p.u == 0) & (u == 2)) | ((p.u == 3) & (u == 1))).astype(jnp.int32)
        return remote(
            self.chunk(self.grad, u), self.chunk(self.slots, p.u), self.send_sem.at[TP + k], self.recv_sem.at[far],
            u * TP + p.j, p.t,
        )

    def outer(self):
        p = self.place
        first = p.u == 0
        src, dst = self.chunk(self.grad, jnp.where(first, 3, 0)), self.chunk(self.slots, jnp.where(first, 1, 2))
        return remote(src, dst, self.send_sem.at[TP], self.recv_sem.at[2], p.me + jnp.where(first, TP, -TP), p.t)

    def ends(self):
        return (self.place.u == 0) | (self.place.u == 3)

    def later(self, u):
        p = self.place
        return ((p.u == 1) & (u == 3)) | ((p.u == 2) & (u == 0))

    def allow(self):
        p = self.place
        self.line_each(
            lambda k, u: pl.semaphore_signal(
                self.free_sem.at[p.u], inc=1, device_id=(u * TP + p.j, p.t), device_id_type=pl.DeviceIdType.MESH
            )
        )

    def start(self):
        if self.free_sem is not None:
            self.line_each(lambda k, u: pl.semaphore_wait(self.free_sem.at[u], 1))
        if self.place.lines == 4:
            pl.when(self.ends())(lambda: self.outer().start())
            self.line_each(lambda k, u: self.line_copy(k, u).start(), lambda u: ~self.later(u))
        else:
            self.line_each(lambda k, u: self.line_copy(k, u).start())

    def add(self, u, sources):
        p = self.place

        @pl.loop(0, self.size // 32)
        def _(i):
            at = pl.ds(pl.multiple_of(u * self.size + i * 32, 32), 32)
            total = self.grad[at, :].astype(F32)
            for slot in sources:
                here = pl.ds(pl.multiple_of(slot * self.size + i * 32, 32), 32)
                total = total + self.slots[here, :].astype(F32)
            self.grad[at, :] = total.astype(BF16)

    def combine(self):
        p = self.place
        if p.lines != 4:
            return

        @pl.when(~self.ends())
        def _():
            wait_bytes(self.chunk(self.slots, 0), self.recv_sem.at[2])
            self.add(jnp.where(p.u == 1, 3, 0), [p.u])
            self.line_each(lambda k, u: self.line_copy(k, u).start(), self.later)

    def group_copy(self, q):
        p = self.place
        j = (p.j + q) % TP
        block = self.grad.at[pl.ds((p.u * TP + j) * self.rows, self.rows)]
        return remote(block, self.out.at[p.j], self.send_sem.at[q], self.recv_sem.at[3], p.u * TP + j, p.t)

    def reduce(self):
        p = self.place
        if p.lines == 4:
            wait_bytes(self.slots.at[pl.ds(0, 2 * self.size)], self.recv_sem.at[0])
            pl.when(~self.ends())(lambda: wait_bytes(self.chunk(self.slots, 0), self.recv_sem.at[1]))
            pl.when(self.ends())(lambda: self.add(p.u, [1, 2]))
            pl.when(p.u == 1)(lambda: self.add(p.u, [0, 2, 3]))
            pl.when(p.u == 2)(lambda: self.add(p.u, [0, 1, 3]))
        else:
            wait_bytes(self.slots.at[pl.ds(0, (p.lines - 1) * self.size)], self.recv_sem.at[0])
            for k in range(1, p.lines):
                self.add(p.u, [(p.u + k) % p.lines])
        for q in (2, 3, 1):
            self.group_copy(q).start()
        own = self.grad.at[pl.ds(p.me * self.rows, self.rows)]
        pltpu.make_async_copy(own, self.out.at[p.j], self.recv_sem.at[3]).start()

    def finish(self):
        wait_bytes(self.out, self.recv_sem.at[3])
        for q in range(1, TP):
            self.group_copy(q).wait_send()
        self.line_each(lambda k, u: self.line_copy(k, u).wait_send())
        if self.place.lines == 4:
            pl.when(self.ends())(lambda: self.outer().wait_send())


def norm_stats(values):
    centre = values - jnp.mean(values, axis=-1, keepdims=True)
    inverse = lax.rsqrt(jnp.mean(centre * centre, axis=-1, keepdims=True) + 1e-05)
    return centre * inverse, inverse


def layer_kernel(
    count,
    small_src, aux_src, row_src, tok_src, cot_src, wq_src, wo_src, wg_src, wd_src,
    rs_q, rs_o, rs_g, rs_d, block_out, input_out, h1_out, norm_out, bias_out,
    wq, wo, wg, wd, cot, hh, qkv, att, hid, slopes, dgate, gd, gg, go, slots_d, slots_o,
    to_core, from_core, low, own, parts, grad, resid, block, gains, biases, norms,
    small, aux_all, row_all, small_all, bias_all, small_t,
    w_send, w_recv, small_sem, aux_sem, row_sem, tok_sem, cot_sem, h1_sem,
    rs_send, rs_recv, free_g, free_d, core_sem, part_sem, free_sem, part2_sem, core2_sem, part3_sem, core3_sem,
    swap_sem, gain_sem, bias_sem, rank_sem, t_sem,
):
    p = Place(count)
    size = tok_src.shape[0]
    half = size // 2
    group = TP * size
    wide = att.shape[1]
    rows = wq_src.shape[1]
    full = hid.shape[1] - 128
    greet(p)

    def rows_of(s):
        return pl.ds(pl.multiple_of(s * size, size), size)

    def columns(n, step):
        return pl.ds(pl.multiple_of(n * step, step), step)

    gathers = [
        WeightGather(p, i, src, dst, w_send, w_recv)
        for i, (src, dst) in enumerate(((wq_src, wq), (wo_src, wo), (wg_src, wg), (wd_src, wd)))
    ]
    gather_q, gather_o, gather_g, gather_d = gathers
    tok = cot
    auxes = GroupPieces(p, aux_src, aux_all, aux_sem)
    rowses = GroupPieces(p, row_src, row_all, row_sem)
    tokens = GroupPieces(p, tok_src, tok, tok_sem, size)
    cots = GroupPieces(p, cot_src, cot, cot_sem, size)
    sums = GroupSum(p, to_core, from_core, low, own, parts, core_sem, part_sem, free_sem)
    spread_h = GroupGather(p, hh, size, part2_sem, core2_sem)
    spread_r = GroupGather(p, cot, size, part3_sem, core3_sem)
    gq = slopes.at[:D, : 3 * wide]
    scatter_q, scatter_o, scatter_g, scatter_d = [
        GradScatter(p, i, g, slots, out, rs_send, rs_recv, free)
        for i, (g, slots, out, free) in enumerate(
            (
                (gq, slots_d.at[:, : 3 * wide], rs_q, free_d),
                (go, slots_o, rs_o, None),
                (gg, wg, rs_g, free_g),
                (gd, slots_d.at[:, : hid.shape[1]], rs_d, None),
            )
        )
    ]

    def small_copy(dest):
        return remote(small_src, small.at[p.me], small_sem.at[dest], small_sem.at[count], dest, p.t)

    gather_q.start()
    auxes.start()
    rowses.start()
    gather_o.start()
    gather_g.start()
    gather_d.start()
    tokens.start()
    pltpu.make_async_copy(small_src, small.at[p.me], small_sem.at[count]).start()
    gather_q.pass_on()
    each_dest(p, lambda dest, u, j: small_copy(dest).start())
    gather_o.pass_on()
    gather_g.pass_on()
    auxes.pass_on()
    rowses.pass_on()
    gather_d.pass_on()
    tokens.pass_on()

    wait_bytes(small, small_sem.at[count])
    per_tile = 128 // rows
    for m in range(D // 128):
        tile = jnp.zeros((8, 128), F32)
        for i in range(per_tile):
            tile = tile + small[m * per_tile + i].astype(F32)[0:8]
        norms[0:8, m * 128 : (m + 1) * 128] = tile
    bias_rows = small.shape[1] - 16
    total = jnp.zeros((bias_rows, 128), F32)
    for d in range(count):
        total = total + small[d].astype(F32)[16:]
    for i in range(bias_rows):
        norms[8:9, i * 128 : (i + 1) * 128] = total[i : i + 1]
    auxes.arrive()
    rowses.arrive()
    gather_q.relay()
    tokens.arrive()

    @pl.loop(0, group // 32)
    def _(i):
        at = pl.ds(pl.multiple_of(i * 32, 32), 32)
        normed, _, _ = layer_norm(tok[at, :].astype(F32), norms[0:1, :D], norms[1:2, :D])
        hh[at, :] = normed.astype(BF16)

    tokens.finish()
    keep_h1 = pltpu.make_async_copy(hh, h1_out, h1_sem.at[0])
    keep_h1.start()
    gather_q.arrive()
    gather_o.relay()
    head_wide = (bias_rows * 128) // 3

    @pl.loop(0, TP)
    def _(s):
        at = rows_of(s)
        proj = dot(hh[at, :], wq[...], 1, 0)
        tables = tables_of(aux_all[s], wide)

        def part(k):
            lanes = pl.ds(pl.multiple_of(k * head_wide + p.j * wide, 128), wide)
            return proj[:, k * wide : (k + 1) * wide] + norms[8:9, lanes]

        query = spin(part(0), *tables).astype(BF16)
        key = spin(part(1), *tables).astype(BF16)
        value = part(2).astype(BF16)
        qkv[at, :wide] = query
        qkv[at, wide : 2 * wide] = key
        qkv[at, 2 * wide :] = value
        allowed = mask_of(aux_all[s][:, ROT : ROT + 1], row_all[s, 0:1, :], size)
        att[at, :] = attend_values(query, key, value, allowed).astype(BF16)

    gather_o.arrive()
    keep_h1.wait()
    sums.start(lambda s, n, step: dot(att[rows_of(s), :], wo[columns(n, step), :], 1, 1))
    gather_g.relay()
    sums.arrive()

    @pl.loop(0, half // 32)
    def _(i):
        at = pl.multiple_of(i * 32, 32)
        values = tok_src[pl.ds(pl.multiple_of(p.t * half + at, 32), 32), :].astype(F32)
        values = values + sums.total(at, 32)
        resid[pl.ds(at, 32), :] = values
        normed, _, _ = layer_norm(values, norms[2:3, :D], norms[3:4, :D])
        start = (p.j * 2 + p.t) * half + at
        hh[pl.ds(pl.multiple_of(start, 32), 32), :] = normed.astype(BF16)

    sums.release()
    spread_h.start()
    cots.start()
    spread_h.arrive()
    cots.pass_on()
    gather_g.arrive()
    gather_d.relay()

    @pl.loop(0, TP)
    def _(s):
        at = rows_of(s)
        late = pl.ds(pl.multiple_of(group + s * size, size), size)
        rows_in = hh[at, :]
        gate = dot(rows_in, wg[:, :full], 1, 0)
        up = dot(rows_in, wg[:, full : 2 * full], 1, 0)
        sig = jax.nn.sigmoid(gate)
        hid[at, :full] = (gate * sig * up).astype(BF16)
        slopes[at, :full] = (up * sig * (1.0 + gate * (1.0 - sig))).astype(BF16)
        slopes[late, :full] = (gate * sig).astype(BF16)
        gate = dot(rows_in, wg[:, 2 * full :], 1, 0)
        up = pltpu.roll(gate, 64, 1)
        sig = jax.nn.sigmoid(gate)
        first = lax.broadcasted_iota(jnp.int32, gate.shape, 1) < 64
        tail = slice(full, full + 128)
        hid[at, tail] = jnp.where(first, gate * sig * up, 0.0).astype(BF16)
        slopes[at, tail] = jnp.where(first, up * sig * (1.0 + gate * (1.0 - sig)), 0.0).astype(BF16)
        slopes[late, tail] = jnp.where(first, gate * sig, 0.0).astype(BF16)

    cots.arrive()
    step = min(256, D)

    def weight_grad(left, right, out):
        @pl.loop(0, D // step)
        def _(n):
            at = columns(n, step)
            out[at, :] = dot(left[:, at], right[...], 0, 0).astype(BF16)

    weight_grad(cot, hid, gd)
    scatter_d.start()

    gather_d.arrive()

    @pl.loop(0, TP)
    def _(s):
        at = rows_of(s)
        late = pl.ds(pl.multiple_of(group + s * size, size), size)
        dhid = dot(cot[at, :], wd[...], 1, 0)
        slope = dhid * slopes[at, : hid.shape[1]].astype(F32)
        gain = dhid * slopes[late, : hid.shape[1]].astype(F32)
        dgate[at, :full] = slope[:, :full].astype(BF16)
        dgate[at, full : 2 * full] = gain[:, :full].astype(BF16)
        last = slope[:, full:] + pltpu.roll(gain[:, full:], 64, 1)
        dgate[at, 2 * full :] = last.astype(BF16)

    cots.finish()
    sums.acquire()
    sums.start(lambda s, n, step: dot(dgate[rows_of(s), :], wg[columns(n, step), :], 1, 1))
    gather_g.finish()
    scatter_g.allow()
    weight_grad(hh, dgate, gg)
    scatter_g.start()
    spread_h.finish()
    load_h1 = pltpu.make_async_copy(h1_out, hh, h1_sem.at[1])
    load_h1.start()
    scatter_d.combine()
    sums.arrive()

    gains[...] = jnp.zeros_like(gains)

    @pl.loop(0, half // 32)
    def _(i):
        at = pl.multiple_of(i * 32, 32)
        scaled, inverse = norm_stats(resid[pl.ds(at, 32), :])
        part, gain, shift = norm_back(sums.total(at, 32), scaled, inverse, norms[2:3, :D])
        gains[2:3, :] += gain[None]
        gains[3:4, :] += shift[None]
        mine = pl.ds(pl.multiple_of((p.j * 2 + p.t) * half + at, 32), 32)
        total = cot[mine, :].astype(F32) + part
        grad[pl.ds(at, 32), :] = total
        cot[mine, :] = total.astype(BF16)

    sums.release()
    spread_r.start()
    scatter_g.combine()
    scatter_d.reduce()
    scatter_q.allow()
    spread_r.arrive()

    biases[...] = jnp.zeros_like(biases)

    @pl.loop(0, TP)
    def _(s):
        at = rows_of(s)
        grad_out = dot(cot[at, :], wo[...], 1, 0).astype(BF16)
        allowed = mask_of(aux_all[s][:, ROT : ROT + 1], row_all[s, 0:1, :], size)
        tables = tables_of(aux_all[s], wide)
        three = attend_back_values(
            qkv[at, :wide], qkv[at, wide : 2 * wide], qkv[at, 2 * wide :], grad_out, allowed, tables
        )
        for k, value in enumerate(three):
            lanes = slice(k * wide, (k + 1) * wide)
            qkv[at, lanes] = value
            biases[0:1, lanes] += jnp.sum(value.astype(F32), axis=0, keepdims=True)

    load_h1.wait()
    weight_grad(hh, qkv, gq)
    scatter_q.start()
    weight_grad(cot, att, go)
    scatter_o.start()

    bias_all[p.u] = biases[...]

    def bias_copy(k):
        u = (p.u + k) % p.lines
        return remote(biases, bias_all.at[p.u], bias_sem.at[k], bias_sem.at[p.lines + k], u * TP + p.j, p.t)

    for k in range(1, p.lines):
        bias_copy(k).start()

    sums.acquire()
    sums.start(lambda s, n, step: dot(qkv[rows_of(s), :], wq[columns(n, step), :], 1, 1))
    scatter_q.combine()
    scatter_o.combine()
    sums.arrive()

    @pl.loop(0, half // 32)
    def _(i):
        at = pl.multiple_of(i * 32, 32)
        values = tok_src[pl.ds(pl.multiple_of(p.t * half + at, 32), 32), :].astype(F32)
        scaled, inverse = norm_stats(values)
        part, gain, shift = norm_back(sums.total(at, 32), scaled, inverse, norms[0:1, :D])
        gains[0:1, :] += gain[None]
        gains[1:2, :] += shift[None]
        grad[pl.ds(at, 32), :] += part

    sums.release()
    mine = pl.ds(pl.multiple_of(p.t * half, half), half)

    def give(index, value, out):
        here = pltpu.make_async_copy(value, out.at[mine], swap_sem.at[index, 0])
        there = remote(value, out.at[mine], swap_sem.at[index, 1], swap_sem.at[index, 2], p.me, 1 - p.t)
        here.start()
        there.start()
        return here, there

    gives = [*give(0, grad, input_out)]

    def tile_of(d):
        return pl.ds(pl.multiple_of(d * rows // 128 * 128, 128), 128)

    def gain_copy(dest):
        return remote(gains.at[:, tile_of(dest)], small_all.at[p.me], gain_sem.at[dest], gain_sem.at[count], dest, p.t)

    pltpu.make_async_copy(gains.at[:, tile_of(p.me)], small_all.at[p.me], gain_sem.at[count]).start()
    each_dest(p, lambda dest, u, j: gain_copy(dest).start())

    for k in range(1, p.lines):
        bias_copy(k).wait_recv()
    total = bias_all[0]
    for k in range(1, p.lines):
        total = total + bias_all[k]
    bias_out[p.j] = total

    def rank_copy(q):
        j = (p.j + q) % TP
        return remote(bias_out.at[p.j], bias_out.at[p.j], rank_sem.at[q], rank_sem.at[TP + q], p.u * TP + j, p.t)

    for q in range(1, TP):
        rank_copy(q).start()

    sums.acquire()
    sums.start(lambda s, n, step: dot(hid[rows_of(s), :], wd[columns(n, step), :], 1, 1))
    sums.arrive()

    @pl.loop(0, half // 32)
    def _(i):
        at = pl.multiple_of(i * 32, 32)
        block[pl.ds(at, 32), :] = resid[pl.ds(at, 32), :] + sums.total(at, 32)

    gives += give(1, block, block_out)
    scatter_g.reduce()

    wait_bytes(small_all, gain_sem.at[count])
    total = small_all[0]
    for d in range(1, count):
        total = total + small_all[d]
    small_t[0] = total
    swap = remote(small_t.at[0], small_t.at[1], t_sem.at[0], t_sem.at[1], p.me, 1 - p.t)
    swap.start()
    scatter_q.reduce()
    scatter_o.reduce()
    swap.wait()
    norm_out[...] = small_t[0] + small_t[1]
    for q in range(1, TP):
        rank_copy(q).wait()
    for k in range(1, p.lines):
        bias_copy(k).wait_send()
    each_dest(p, lambda dest, u, j: small_copy(dest).wait_send())
    each_dest(p, lambda dest, u, j: gain_copy(dest).wait_send())
    for copy in gives:
        copy.wait()
    for part in (auxes, rowses, sums, spread_r, gather_q, gather_o, gather_d):
        part.finish()
    for scatter in (scatter_d, scatter_g, scatter_q, scatter_o):
        scatter.finish()


def layer(count, small, aux, row, tokens, cot, wq, wo, wg, wd):
    size = tokens.shape[0]
    half = size // 2
    group = TP * size
    lines, rows = count // TP, wq.shape[1]
    wide, pad, gates = wo.shape[2], wd.shape[2], wg.shape[2]
    any_spec = pl.BlockSpec(memory_space=pl.ANY)
    vmem = pl.BlockSpec(memory_space=pltpu.VMEM)
    dma = pltpu.SemaphoreType.DMA
    regular = pltpu.SemaphoreType.REGULAR

    def out(*shape, dtype=BF16):
        return jax.ShapeDtypeStruct(shape, dtype)

    return pl.pallas_call(
        functools.partial(layer_kernel, count),
        in_specs=[vmem, vmem, vmem, vmem] + [any_spec] * 5,
        out_specs=[any_spec] * 7 + [vmem] * 2,
        out_shape=[
            out(TP, rows, 3 * wide),
            out(TP, rows, wide),
            out(TP, rows, gates),
            out(TP, rows, pad),
            out(size, D, dtype=F32),
            out(size, D, dtype=F32),
            out(group, D),
            out(8, 128, dtype=F32),
            out(TP, 8, 3 * wide, dtype=F32),
        ],
        scratch_shapes=[
            pltpu.VMEM((D, 3 * wide), BF16),
            pltpu.VMEM((D, wide), BF16),
            pltpu.VMEM((D, gates), BF16),
            pltpu.VMEM((D, pad), BF16),
            pltpu.VMEM((group, D), BF16),
            pltpu.VMEM((group, D), BF16),
            pltpu.VMEM((group, 3 * wide), BF16),
            pltpu.VMEM((group, wide), BF16),
            pltpu.VMEM((group, pad), BF16),
            pltpu.VMEM((max(2 * group, D), max(pad, 3 * wide)), BF16),
            pltpu.VMEM((group, gates), BF16),
            pltpu.VMEM((D, pad), BF16),
            pltpu.VMEM((D, gates), BF16),
            pltpu.VMEM((D, wide), BF16),
            pltpu.VMEM((D, max(pad, 3 * wide)), BF16),
            pltpu.VMEM((D, wide), BF16),
            pltpu.VMEM((2, size, D), BF16),
            pltpu.VMEM((2, size, D), BF16),
            pltpu.VMEM((2, size, D), BF16),
            pltpu.VMEM((half, D), F32),
            pltpu.VMEM((3, half, D), BF16),
            pltpu.VMEM((half, D), F32),
            pltpu.VMEM((half, D), F32),
            pltpu.VMEM((half, D), F32),
            pltpu.VMEM((8, D), F32),
            pltpu.VMEM((8, 3 * wide), F32),
            pltpu.VMEM((16, max(D, 128 * (small.shape[0] - 16))), F32),
            pltpu.VMEM((count,) + small.shape, BF16),
            pltpu.VMEM((TP, size, 128), F32),
            pltpu.VMEM((TP, 8, size), F32),
            pltpu.VMEM((count, 8, 128), F32),
            pltpu.VMEM((lines, 8, 3 * wide), F32),
            pltpu.VMEM((2, 8, 128), F32),
            dma((4, TP + lines)),
            dma((4, 3)),
            dma((count + 1,)),
            dma((2, 4)),
            dma((2, 4)),
            dma((2, 4)),
            dma((2, 4)),
            dma((2,)),
            dma((4, TP + lines)),
            dma((4, 4)),
            regular((lines,)),
            regular((lines,)),
            dma((2, 2)),
            dma((2, 4)),
            regular((4,)),
            dma((2, 4)),
            dma((2, 4)),
            dma((2, 4)),
            dma((2, 4)),
            dma((2, 3)),
            dma((count + 1,)),
            dma((2 * lines,)),
            dma((2 * TP,)),
            dma((2,)),
        ],
        compiler_params=pltpu.CompilerParams(
            collective_id=0, has_side_effects=True, vmem_limit_bytes=63 * 1024 * 1024
        ),
        cost_estimate=pl.CostEstimate(flops=40 * 10**9, bytes_accessed=60 * 10**6, transcendentals=10**7),
        name="layer",
    )(small, aux, row, tokens, cot, wq, wo, wg, wd)


def per_device(
    count,
    tokens_in,
    segment_ids,
    d_out,
    qkv_weight,
    qkv_bias,
    out_weight,
    gating_weight,
    down_weight,
    norm_params,
    qkv_first,
    qkv_second,
    bias_first,
    bias_second,
    out_first,
    out_second,
    gating_first,
    gating_second,
    down_first,
    down_second,
    norm_first,
    norm_second,
):
    place = lax.axis_index("dp")
    rows = norm_params.shape[1]
    seq_len = tokens_in.shape[1]
    head_local = qkv_weight.shape[2]
    hidden_local = gating_weight.shape[2]
    wide = head_local // TP
    hid = hidden_local // TP
    full = hid // 128 * 128

    def cut(shard):
        return shard.astype(BF16).transpose(1, 0, 2)

    gates = gating_weight.astype(BF16).reshape(rows, 2, TP, hid)
    gates = jnp.concatenate(
        [gates[:, 0, :, :full], gates[:, 1, :, :full], gates[:, 0, :, full:], gates[:, 1, :, full:]], axis=2
    )
    downs = jnp.pad(down_weight.T.reshape(rows, TP, hid), ((0, 0), (0, 0), (0, -hid % 128)))
    weights = (
        cut(qkv_weight.reshape(rows, 3, TP, wide).transpose(0, 2, 1, 3).reshape(rows, TP, 3 * wide)),
        cut(out_weight.T.reshape(rows, TP, wide)),
        gates.transpose(1, 0, 2),
        cut(downs),
    )
    bias_here = qkv_bias.shape[1]
    small_norm = lax.dynamic_update_slice(jnp.zeros((16, 128), F32), norm_params, (0, (place * rows) % 128))
    small_bias = lax.dynamic_update_slice(jnp.zeros((3 * head_local,), F32), qkv_bias[0], (place * bias_here,))
    small = jnp.concatenate([small_norm, small_bias.reshape(-1, 128)]).astype(BF16)
    segments = segment_ids[0]
    earlier = jnp.sum((segments[None, :] < segments[:, None]).astype(jnp.int32), axis=1)
    positions = (jnp.arange(seq_len, dtype=jnp.int32) - earlier).astype(F32)
    frequency = 10000.0 ** (-2.0 * jnp.arange(ROT // 2, dtype=F32) / ROT)
    angles = positions[:, None] * frequency[None, :]
    aux = jnp.concatenate([jnp.cos(angles), jnp.sin(angles), segments[:, None].astype(F32)], axis=1)
    aux = jnp.pad(aux, ((0, 0), (0, 128 - aux.shape[1])))
    row = jnp.broadcast_to(segments.astype(F32)[None], (8, seq_len))

    rs_q, rs_o, rs_g, rs_d, block_out, input_grad, _, norm_sum, bias_sum = layer(
        count, small, aux, row, tokens_in[0], d_out[0], *weights
    )

    def total(parts):
        return parts.transpose(1, 0, 2).astype(F32)

    gating_parts = total(rs_g)
    gate_parts = jnp.concatenate([gating_parts[..., :full], gating_parts[..., 2 * full : full + hid]], axis=2)
    up_parts = jnp.concatenate([gating_parts[..., full : 2 * full], gating_parts[..., full + hid :]], axis=2)
    gating_shard = jnp.stack([gate_parts, up_parts], axis=1).reshape(gating_weight.shape)
    qkv_shard = total(rs_q).reshape(rows, TP, 3, wide).transpose(0, 2, 1, 3).reshape(qkv_weight.shape)
    out_shard = total(rs_o).reshape(rows, head_local).T
    down_shard = total(rs_d)[..., :hid].reshape(rows, hidden_local).T
    norm_grad = lax.dynamic_slice_in_dim(norm_sum[:4], (place * rows) % 128, rows, 1)
    bias_grad = bias_sum[:, 0].reshape(TP, 3, wide).transpose(1, 0, 2).reshape(1, 3 * head_local)
    bias_grad = lax.dynamic_slice_in_dim(bias_grad, place * bias_here, bias_here, 1)
    return (
        block_out[None],
        input_grad[None],
        *adamw_update(qkv_weight, qkv_shard, qkv_first, qkv_second, D ** (-0.5), 0.1),
        *adamw_update(qkv_bias, bias_grad, bias_first, bias_second, 0.3, 0.0),
        *adamw_update(out_weight, out_shard, out_first, out_second, (H * HD // 16) ** (-0.5), 0.1),
        *adamw_update(gating_weight, gating_shard, gating_first, gating_second, D ** (-0.5), 0.1),
        *adamw_update(down_weight, down_shard, down_first, down_second, FF ** (-0.5), 0.1),
        *adamw_update(norm_params, norm_grad, norm_first, norm_second, 0.25, 0.0),
    )


def solution(mesh):
    tokens = P("dp", None, None)
    qkv = P("dp", None, "tensor")
    rest = P("tensor", "dp")
    norm = P(None, "dp")
    weights = (qkv, rest, rest, qkv, rest, norm)
    states = (qkv, qkv, rest, rest, rest, rest, qkv, qkv, rest, rest, norm, norm)
    return jax.shard_map(
        functools.partial(per_device, mesh.shape["dp"]),
        mesh=mesh,
        in_specs=(tokens, P("dp", None), tokens, *weights, *states),
        out_specs=(tokens, tokens, *(spec for spec in weights for _ in range(3))),
        check_vma=False,
    )
```

```python
import functools

import jax
import jax.numpy as jnp
from jax import lax
from jax.experimental import pallas as pl
from jax.experimental.layout import Layout, with_layout_constraint
from jax.experimental.pallas import tpu as pltpu
from jax.sharding import PartitionSpec as P

D = 2048
H = 32
HD = 64
ROT = 16
FF = 5632
STEP = 10
TP = 4

F32 = jnp.float32
BF16 = jnp.bfloat16


def layer_norm(values, scale_row, shift_row):
    centre = values - jnp.mean(values, axis=-1, keepdims=True)
    spread = jnp.mean(centre * centre, axis=-1, keepdims=True)
    inverse = lax.rsqrt(spread + 1e-05)
    scaled = centre * inverse
    return (scaled * scale_row + shift_row, scaled, inverse)


def norm_back(grad_in, scaled, inverse, scale_row):
    grad_scaled = grad_in * scale_row
    mean_first = jnp.mean(grad_scaled, axis=-1, keepdims=True)
    mean_second = jnp.mean(grad_scaled * scaled, axis=-1, keepdims=True)
    grad_values = inverse * (grad_scaled - mean_first - scaled * mean_second)
    return (grad_values, jnp.sum(grad_in * scaled, axis=0), jnp.sum(grad_in, axis=0))


def adamw_update(weight_old, gradient, first_old, second_old, step_rate, decay_rate):
    first_new = 0.9 * first_old + 0.1 * gradient
    second_new = 0.95 * second_old + 0.05 * gradient * gradient
    corrected = first_new / (1.0 - 0.9**STEP) / (jnp.sqrt(second_new / (1.0 - 0.95**STEP)) + 1e-08)
    return (weight_old - step_rate * (corrected + decay_rate * weight_old), first_new, second_new)


def dot(a, b, ca, cb):
    return lax.dot_general(a, b, (((ca,), (cb,)), ((), ())), preferred_element_type=F32)


def spin(values, cos_t, lower_t, upper_t):
    wide = values.shape[1]
    return (
        values * cos_t
        + pltpu.roll(values, wide - ROT // 2, 1) * lower_t
        + pltpu.roll(values, ROT // 2, 1) * upper_t
    )


def spin_back(values, cos_t, lower_t, upper_t):
    wide = values.shape[1]
    return (
        values * cos_t
        + pltpu.roll(values * lower_t, ROT // 2, 1)
        + pltpu.roll(values * upper_t, wide - ROT // 2, 1)
    )


def mask_of(seg_col, seg_row, size):
    rows = lax.broadcasted_iota(jnp.int32, (size, size), 0)
    cols = lax.broadcasted_iota(jnp.int32, (size, size), 1)
    return (seg_col == seg_row) & (cols <= rows)


def attend_back_values(query, key, value, grad, allowed, tables):
    head_of = lax.broadcasted_iota(jnp.int32, query.shape, 1) // HD
    zero = jnp.zeros_like(query)
    dq = jnp.zeros(query.shape, F32)
    dk = jnp.zeros(query.shape, F32)
    dv = jnp.zeros(query.shape, F32)
    for head in range(query.shape[1] // HD):
        mine = head_of == head
        query_h = jnp.where(mine, query, zero)
        grad_h = jnp.where(mine, grad, zero)
        scores = dot(query_h, key, 1, 1) * HD ** (-0.5)
        scores = jnp.where(allowed, scores, -1e30)
        weights = jnp.exp(scores - jnp.max(scores, axis=1, keepdims=True))
        prob = weights / jnp.sum(weights, axis=1, keepdims=True)
        dv = dv + dot(prob.astype(BF16), grad_h, 0, 0)
        dprob = dot(grad_h, value, 1, 1)
        delta = jnp.sum(prob * dprob, axis=1, keepdims=True)
        dscore = (prob * (dprob - delta)).astype(BF16)
        dq = jnp.where(mine, dot(dscore, key, 1, 0), dq)
        dk = dk + dot(dscore, query_h, 0, 0)
    dq = spin_back(dq * HD ** (-0.5), *tables).astype(BF16)
    dk = spin_back(dk * HD ** (-0.5), *tables).astype(BF16)
    return dq, dk, dv.astype(BF16)


class Place:
    def __init__(self, count):
        self.count = count
        self.lines = count // TP
        self.me = lax.axis_index("dp")
        self.t = lax.axis_index("tensor")
        self.u = self.me // TP
        self.j = self.me % TP
        self.x = self.j // 2
        self.c = self.j % 2
        self.core_peer = self.me + 1 - 2 * self.c
        self.x_peer = self.me + 2 - 4 * self.x

    def group(self, k):
        x = (self.x + k // 2) % 2
        return self.u * TP + x * 2 + self.c, (self.t + k % 2) % 2, x


def remote(src, dst, send_sem, recv_sem, dp, t):
    return pltpu.make_async_remote_copy(
        src_ref=src,
        dst_ref=dst,
        send_sem=send_sem,
        recv_sem=recv_sem,
        device_id=(dp, t),
        device_id_type=pl.DeviceIdType.MESH,
    )


def wait_bytes(ref, sem):
    pltpu.make_async_copy(ref, ref, sem).wait()


def greet(place):
    barrier = pltpu.get_barrier_semaphore()

    @pl.loop(1, place.count)
    def _(k):
        pl.semaphore_signal(
            barrier,
            inc=1,
            device_id=((place.me + k) % place.count, place.t),
            device_id_type=pl.DeviceIdType.MESH,
        )

    for k in (1, 3):
        dp, t, _ = place.group(k)
        pl.semaphore_signal(barrier, inc=1, device_id=(dp, t), device_id_type=pl.DeviceIdType.MESH)
    pl.semaphore_wait(barrier, place.count + 1)


def each_dest(place, act):
    if place.lines == 4:

        @pl.loop(1, TP)
        def _(q):
            j = (place.j + q) % TP
            act(place.u * TP + j, place.u, j)

        @pl.loop(0, TP)
        def _(q):
            j = (place.j + q) % TP
            for dz in (2, 1, 3):
                u = (place.u + dz) % 4
                act(u * TP + j, u, j)

    else:

        @pl.loop(1, place.count)
        def _(k):
            dest = (place.me + k) % place.count
            act(dest, dest // TP, dest % TP)


class WeightGather:
    def __init__(self, place, index, src, dst, send_sem, recv_sem):
        self.place, self.src, self.dst = place, src, dst
        self.send_sem, self.recv_sem = send_sem.at[index], recv_sem.at[index]
        self.rows = src.shape[1]

    def group_copy(self, q):
        p = self.place
        j = (p.j + q) % TP
        mine = self.dst.at[pl.ds(p.me * self.rows, self.rows)]
        return remote(self.src.at[j], mine, self.send_sem.at[q], self.recv_sem.at[2], p.u * TP + j, p.t)

    def chunk(self, u):
        size = TP * self.rows
        return self.dst.at[pl.ds(u * size, size)]

    def line_copy(self, k):
        p = self.place
        u = (p.u + k) % p.lines
        far = 0
        if p.lines == 4:
            far = (((p.u == 0) & (u == 2)) | ((p.u == 3) & (u == 1))).astype(jnp.int32)
        mine = self.chunk(p.u)
        return remote(mine, mine, self.send_sem.at[TP + k], self.recv_sem.at[far], u * TP + p.j, p.t)

    def line_each(self, act):
        p = self.place
        if p.lines == 4:
            for k in (2, 1, 3):
                pl.when(jnp.abs(p.u - (p.u + k) % 4) < 3)(lambda k=k: act(k))
        else:
            for k in range(1, p.lines):
                act(k)

    def start(self):
        p = self.place
        for q in (2, 3, 1):
            self.group_copy(q).start()
        mine = self.dst.at[pl.ds(p.me * self.rows, self.rows)]
        pltpu.make_async_copy(self.src.at[p.j], mine, self.recv_sem.at[2]).start()

    def pass_on(self):
        wait_bytes(self.chunk(0), self.recv_sem.at[2])
        self.line_each(lambda k: self.line_copy(k).start())

    def middle(self):
        return (self.place.u == 1) | (self.place.u == 2)

    def forward(self):
        p = self.place
        chunk = self.chunk(jnp.where(p.u == 2, 0, 3))
        dest = p.me + jnp.where(p.u == 2, TP, -TP)
        return remote(chunk, chunk, self.send_sem.at[TP], self.recv_sem.at[1], dest, p.t)

    def relay(self):
        if self.place.lines == 4:

            @pl.when(self.middle())
            def _():
                wait_bytes(self.chunk(0), self.recv_sem.at[1])
                self.forward().start()

    def arrive(self):
        p = self.place
        size = TP * self.rows
        wait_bytes(self.dst.at[pl.ds(0, size * (2 if p.lines == 4 else p.lines - 1))], self.recv_sem.at[0])
        if p.lines == 4:
            pl.when(~self.middle())(lambda: wait_bytes(self.chunk(0), self.recv_sem.at[1]))

    def finish(self):
        for q in range(1, TP):
            self.group_copy(q).wait_send()
        self.line_each(lambda k: self.line_copy(k).wait_send())
        if self.place.lines == 4:
            pl.when(self.middle())(lambda: self.forward().wait_send())


class GroupSum:
    def __init__(self, place, to_core, from_core, low, own, parts, core_sem, part_sem, free_sem=None):
        self.place = place
        self.to_core, self.from_core, self.low, self.own, self.parts = to_core, from_core, low, own, parts
        self.core_sem, self.part_sem, self.free_sem = core_sem, part_sem, free_sem

    def core_copy(self, i):
        p = self.place
        return remote(
            self.to_core.at[i], self.from_core.at[i], self.core_sem.at[0, i], self.core_sem.at[1, i], p.core_peer, p.t
        )

    def part_copy(self, k):
        p = self.place
        half = self.parts.shape[1]
        dp, t, _ = p.group(k)
        block = self.low.at[0 if k >= 2 else 1, pl.ds(pl.multiple_of(t * half, half), half)]
        return remote(block, self.parts.at[k - 1], self.part_sem.at[0, k], self.part_sem.at[1, k], dp, t)

    def start(self, product):
        p = self.place
        step = min(512, D)
        other = [(p.x + 1) % 2, p.x]
        for i in range(2):

            @pl.loop(0, D // step)
            def _(n):
                at = pl.ds(pl.multiple_of(n * step, step), step)
                self.to_core[i, :, at] = product(other[i] * 2 + 1 - p.c, n, step).astype(BF16)

            self.core_copy(i).start()
        for i in range(2):
            self.core_copy(i).wait_recv()

            @pl.loop(0, D // step)
            def _(n):
                at = pl.ds(pl.multiple_of(n * step, step), step)
                total = product(other[i] * 2 + p.c, n, step) + self.from_core[i, :, at].astype(F32)
                self.low[i, :, at] = total.astype(BF16)
                if i == 1:
                    half = self.own.shape[0]

                    @pl.when(p.t == 0)
                    def _():
                        self.own[:, at] = total[:half]

                    @pl.when(p.t == 1)
                    def _():
                        self.own[:, at] = total[half:]

            for k in (3, 2) if i == 0 else (1,):
                self.part_copy(k).start()

    def arrive(self):
        for k in (3, 2, 1):
            self.part_copy(k).wait_recv()

    def total(self, at, rows):
        value = self.own[pl.ds(pl.multiple_of(at, 32), rows), :]
        for k in range(3):
            value = value + self.parts[k, pl.ds(pl.multiple_of(at, 32), rows), :].astype(F32)
        return value

    def finish(self):
        for i in range(2):
            self.core_copy(i).wait_send()
        for k in (1, 2, 3):
            self.part_copy(k).wait_send()

    def release(self):
        p = self.place
        pl.semaphore_signal(
            self.free_sem.at[0], inc=1, device_id=(p.core_peer, p.t), device_id_type=pl.DeviceIdType.MESH
        )
        for k in (1, 2, 3):
            dp, t, _ = p.group(k)
            pl.semaphore_signal(
                self.free_sem.at[k], inc=1, device_id=(dp, t), device_id_type=pl.DeviceIdType.MESH
            )

    def acquire(self):
        self.finish()
        for k in range(4):
            pl.semaphore_wait(self.free_sem.at[k], 1)


class GroupGather:
    def __init__(self, place, out, size, part_sem, core_sem):
        self.place, self.out, self.half = place, out, size // 2
        self.part_sem, self.core_sem = part_sem, core_sem

    def block(self, x, t):
        p = self.place
        start = ((x * 2 + p.c) * 2 + t) * self.half
        return self.out.at[pl.ds(pl.multiple_of(start, self.half), self.half)]

    def part_copy(self, k):
        p = self.place
        dp, t, _ = p.group(k)
        mine = self.block(p.x, p.t)
        return remote(mine, mine, self.part_sem.at[0, k], self.part_sem.at[1, k], dp, t)

    def core_copy(self, k):
        p = self.place
        _, t, x = p.group(k)
        block = self.block(x, t)
        return remote(block, block, self.core_sem.at[0, k], self.core_sem.at[1, k], p.core_peer, p.t)

    def start(self):
        for k in (3, 2, 1):
            self.part_copy(k).start()
        self.core_copy(0).start()

    def arrive(self):
        for k in (1, 2, 3):
            self.part_copy(k).wait_recv()
            self.core_copy(k).start()
        for k in range(4):
            self.core_copy(k).wait_recv()

    def finish(self):
        for k in (1, 2, 3):
            self.part_copy(k).wait_send()
        for k in range(4):
            self.core_copy(k).wait_send()


class GroupPieces:
    def __init__(self, place, src, out, sem, size=0):
        self.place, self.src, self.out, self.sem, self.size = place, src, out, sem, size

    def at(self, j):
        if self.size:
            return self.out.at[pl.ds(pl.multiple_of(j * self.size, self.size), self.size)]
        return self.out.at[j]

    def own(self):
        return pltpu.make_async_copy(self.src, self.at(self.place.j), self.sem.at[0, 0])

    def near(self, k):
        p = self.place
        dest = p.core_peer if k == 1 else p.x_peer
        return remote(self.src, self.at(p.j), self.sem.at[0, k], self.sem.at[1, k], dest, p.t)

    def relay(self):
        p = self.place
        block = self.at((p.j + 2) % TP)
        return remote(block, block, self.sem.at[0, 3], self.sem.at[1, 3], p.core_peer, p.t)

    def start(self):
        self.near(2).start()
        self.near(1).start()
        self.own().start()

    def pass_on(self):
        self.near(2).wait_recv()
        self.relay().start()

    def arrive(self):
        self.near(1).wait_recv()
        self.relay().wait_recv()
        self.own().wait()

    def finish(self):
        self.near(1).wait_send()
        self.near(2).wait_send()
        self.relay().wait_send()


def tables_of(aux, wide):
    half = ROT // 2
    line = lax.broadcasted_iota(jnp.int32, (aux.shape[1], wide), 0)
    lane = lax.broadcasted_iota(jnp.int32, (aux.shape[1], wide), 1) % HD
    first = lane < half
    second = (lane >= half) & (lane < ROT)

    def spread(pick, sign):
        table = jnp.where(pick, sign, 0.0).astype(F32)
        return lax.dot_general(
            aux, table, (((1,), (0,)), ((), ())), precision=lax.Precision.HIGHEST, preferred_element_type=F32
        )

    rest = lax.broadcasted_iota(jnp.int32, (aux.shape[0], wide), 1) % HD >= ROT
    cos_t = spread((line == lane % half) & (first | second), 1.0) + jnp.where(rest, 1.0, 0.0)
    low_t = spread((line == lane + half) & first, -1.0)
    upp_t = spread((line == lane) & second, 1.0)
    return cos_t, low_t, upp_t


def attend_values(query, key, value, allowed):
    head_of = lax.broadcasted_iota(jnp.int32, query.shape, 1) // HD
    total = jnp.zeros(query.shape, F32)
    for head in range(query.shape[1] // HD):
        mine = head_of == head
        scores = dot(jnp.where(mine, query, jnp.zeros_like(query)), key, 1, 1) * HD ** (-0.5)
        scores = jnp.where(allowed, scores, -1e30)
        weights = jnp.exp(scores - jnp.max(scores, axis=1, keepdims=True))
        prob = weights / jnp.sum(weights, axis=1, keepdims=True)
        total = jnp.where(mine, dot(prob.astype(BF16), value, 1, 0), total)
    return total


class GradScatter:
    def __init__(self, place, index, grad, slots, out, send_sem, recv_sem, free_sem=None):
        self.place, self.grad, self.slots, self.out = place, grad, slots, out
        self.send_sem, self.recv_sem, self.free_sem = send_sem.at[index], recv_sem.at[index], free_sem
        self.rows = out.shape[1]
        self.size = TP * self.rows

    def chunk(self, ref, u):
        return ref.at[pl.ds(u * self.size, self.size)]

    def near(self, u):
        return jnp.abs(self.place.u - u) < 3 if self.place.lines == 4 else None

    def line_each(self, act, picked=lambda u: True):
        p = self.place
        for k in (2, 1, 3) if p.lines == 4 else range(1, p.lines):
            u = (p.u + k) % p.lines
            if p.lines == 4:
                pl.when(self.near(u) & picked(u))(lambda k=k, u=u: act(k, u))
            else:
                act(k, u)

    def line_copy(self, k, u):
        p = self.place
        far = 0
        if p.lines == 4:
            far = (((p.u == 0) & (u == 2)) | ((p.u == 3) & (u == 1))).astype(jnp.int32)
        return remote(
            self.chunk(self.grad, u), self.chunk(self.slots, p.u), self.send_sem.at[TP + k], self.recv_sem.at[far],
            u * TP + p.j, p.t,
        )

    def outer(self):
        p = self.place
        first = p.u == 0
        src, dst = self.chunk(self.grad, jnp.where(first, 3, 0)), self.chunk(self.slots, jnp.where(first, 1, 2))
        return remote(src, dst, self.send_sem.at[TP], self.recv_sem.at[2], p.me + jnp.where(first, TP, -TP), p.t)

    def ends(self):
        return (self.place.u == 0) | (self.place.u == 3)

    def later(self, u):
        p = self.place
        return ((p.u == 1) & (u == 3)) | ((p.u == 2) & (u == 0))

    def allow(self):
        p = self.place
        self.line_each(
            lambda k, u: pl.semaphore_signal(
                self.free_sem.at[p.u], inc=1, device_id=(u * TP + p.j, p.t), device_id_type=pl.DeviceIdType.MESH
            )
        )

    def start(self):
        self.start_outer()
        self.start_rest()

    def start_outer(self):
        if self.free_sem is not None:
            self.line_each(lambda k, u: pl.semaphore_wait(self.free_sem.at[u], 1))
        if self.place.lines == 4:
            pl.when(self.ends())(lambda: self.outer().start())

    def start_rest(self):
        if self.place.lines == 4:
            self.line_each(lambda k, u: self.line_copy(k, u).start(), lambda u: ~self.later(u))
        else:
            self.line_each(lambda k, u: self.line_copy(k, u).start())

    def add(self, u, sources):
        p = self.place

        @pl.loop(0, self.size // 32)
        def _(i):
            at = pl.ds(pl.multiple_of(u * self.size + i * 32, 32), 32)
            total = self.grad[at, :].astype(F32)
            for slot in sources:
                here = pl.ds(pl.multiple_of(slot * self.size + i * 32, 32), 32)
                total = total + self.slots[here, :].astype(F32)
            self.grad[at, :] = total.astype(BF16)

    def combine(self):
        p = self.place
        if p.lines != 4:
            return

        @pl.when(~self.ends())
        def _():
            wait_bytes(self.chunk(self.slots, 0), self.recv_sem.at[2])
            self.add(jnp.where(p.u == 1, 3, 0), [p.u])
            self.line_each(lambda k, u: self.line_copy(k, u).start(), self.later)

    def group_copy(self, q):
        p = self.place
        j = (p.j + q) % TP
        block = self.grad.at[pl.ds((p.u * TP + j) * self.rows, self.rows)]
        return remote(block, self.out.at[p.j], self.send_sem.at[q], self.recv_sem.at[3], p.u * TP + j, p.t)

    def reduce(self):
        p = self.place
        if p.lines == 4:
            wait_bytes(self.slots.at[pl.ds(0, 2 * self.size)], self.recv_sem.at[0])
            pl.when(~self.ends())(lambda: wait_bytes(self.chunk(self.slots, 0), self.recv_sem.at[1]))
            pl.when(self.ends())(lambda: self.add(p.u, [1, 2]))
            pl.when(p.u == 1)(lambda: self.add(p.u, [0, 2, 3]))
            pl.when(p.u == 2)(lambda: self.add(p.u, [0, 1, 3]))
        else:
            wait_bytes(self.slots.at[pl.ds(0, (p.lines - 1) * self.size)], self.recv_sem.at[0])
            for k in range(1, p.lines):
                self.add(p.u, [(p.u + k) % p.lines])
        for q in (2, 3, 1):
            self.group_copy(q).start()
        own = self.grad.at[pl.ds(p.me * self.rows, self.rows)]
        pltpu.make_async_copy(own, self.out.at[p.j], self.recv_sem.at[3]).start()

    def finish(self):
        wait_bytes(self.out, self.recv_sem.at[3])
        for q in range(1, TP):
            self.group_copy(q).wait_send()
        self.line_each(lambda k, u: self.line_copy(k, u).wait_send())
        if self.place.lines == 4:
            pl.when(self.ends())(lambda: self.outer().wait_send())


def norm_stats(values):
    centre = values - jnp.mean(values, axis=-1, keepdims=True)
    inverse = lax.rsqrt(jnp.mean(centre * centre, axis=-1, keepdims=True) + 1e-05)
    return centre * inverse, inverse


def layer_kernel(
    count,
    small_src, aux_src, row_src, tok_src, cot_src, wq_src, wo_src, wg_src, wd_src,
    rs_q, rs_o, rs_g, rs_d, block_out, input_out, h1_out, norm_out, bias_out,
    wq, wo, wg, wd, cot, hh, qkv, att, hid, slopes, dgate, gd, gg, go, slots_d, slots_o,
    to_core, from_core, low, own, parts, grad, resid, block, gains, biases, norms,
    small, aux_all, row_all, small_all, bias_all, small_t,
    w_send, w_recv, small_sem, aux_sem, row_sem, tok_sem, cot_sem, h1_sem,
    rs_send, rs_recv, free_g, free_d, core_sem, part_sem, free_sem, part2_sem, core2_sem, part3_sem, core3_sem,
    swap_sem, gain_sem, bias_sem, rank_sem, t_sem,
):
    p = Place(count)
    size = tok_src.shape[0]
    half = size // 2
    group = TP * size
    wide = att.shape[1]
    rows = wq_src.shape[1]
    full = hid.shape[1] - 128
    greet(p)

    def rows_of(s):
        return pl.ds(pl.multiple_of(s * size, size), size)

    def columns(n, step):
        return pl.ds(pl.multiple_of(n * step, step), step)

    gathers = [
        WeightGather(p, i, src, dst, w_send, w_recv)
        for i, (src, dst) in enumerate(((wq_src, wq), (wo_src, wo), (wg_src, wg), (wd_src, wd)))
    ]
    gather_q, gather_o, gather_g, gather_d = gathers
    tok = cot
    auxes = GroupPieces(p, aux_src, aux_all, aux_sem)
    rowses = GroupPieces(p, row_src, row_all, row_sem)
    tokens = GroupPieces(p, tok_src, tok, tok_sem, size)
    cots = GroupPieces(p, cot_src, cot, cot_sem, size)
    sums = GroupSum(p, to_core, from_core, low, own, parts, core_sem, part_sem, free_sem)
    spread_h = GroupGather(p, hh, size, part2_sem, core2_sem)
    spread_r = GroupGather(p, cot, size, part3_sem, core3_sem)
    gq = slopes.at[:D, : 3 * wide]
    scatter_q, scatter_o, scatter_g, scatter_d = [
        GradScatter(p, i, g, slots, out, rs_send, rs_recv, free)
        for i, (g, slots, out, free) in enumerate(
            (
                (gq, slots_d.at[:, : 3 * wide], rs_q, free_d),
                (go, slots_o, rs_o, None),
                (gg, wg, rs_g, free_g),
                (gd, slots_d.at[:, : hid.shape[1]], rs_d, None),
            )
        )
    ]

    def small_copy(dest):
        return remote(small_src, small.at[p.me], small_sem.at[dest], small_sem.at[count], dest, p.t)

    pltpu.make_async_copy(small_src, small.at[p.me], small_sem.at[count]).start()
    each_dest(p, lambda dest, u, j: small_copy(dest).start())
    gather_q.start()
    auxes.start()
    rowses.start()
    gather_o.start()
    gather_g.start()
    gather_d.start()
    tokens.start()
    gather_q.pass_on()
    gather_o.pass_on()
    gather_g.pass_on()
    auxes.pass_on()
    rowses.pass_on()
    tokens.pass_on()

    wait_bytes(small, small_sem.at[count])
    per_tile = 128 // rows
    for m in range(D // 128):
        tile = jnp.zeros((8, 128), F32)
        for i in range(per_tile):
            tile = tile + small[m * per_tile + i].astype(F32)[0:8]
        norms[0:8, m * 128 : (m + 1) * 128] = tile
    bias_rows = small.shape[1] - 16
    total = jnp.zeros((bias_rows, 128), F32)
    for d in range(count):
        total = total + small[d].astype(F32)[16:]
    for i in range(bias_rows):
        norms[8:9, i * 128 : (i + 1) * 128] = total[i : i + 1]
    auxes.arrive()
    rowses.arrive()
    gather_q.relay()
    tokens.arrive()

    @pl.loop(0, group // 32)
    def _(i):
        at = pl.ds(pl.multiple_of(i * 32, 32), 32)
        normed, _, _ = layer_norm(tok[at, :].astype(F32), norms[0:1, :D], norms[1:2, :D])
        hh[at, :] = normed.astype(BF16)

    tokens.finish()
    keep_h1 = pltpu.make_async_copy(hh, h1_out, h1_sem.at[0])
    keep_h1.start()
    gather_q.arrive()
    gather_d.pass_on()
    gather_o.relay()
    head_wide = (bias_rows * 128) // 3

    @pl.loop(0, TP)
    def _(s):
        at = rows_of(s)
        proj = dot(hh[at, :], wq[...], 1, 0)
        tables = tables_of(aux_all[s], wide)

        def part(k):
            lanes = pl.ds(pl.multiple_of(k * head_wide + p.j * wide, 128), wide)
            return proj[:, k * wide : (k + 1) * wide] + norms[8:9, lanes]

        query = spin(part(0), *tables).astype(BF16)
        key = spin(part(1), *tables).astype(BF16)
        value = part(2).astype(BF16)
        qkv[at, :wide] = query
        qkv[at, wide : 2 * wide] = key
        qkv[at, 2 * wide :] = value
        allowed = mask_of(aux_all[s][:, ROT : ROT + 1], row_all[s, 0:1, :], size)
        att[at, :] = attend_values(query, key, value, allowed).astype(BF16)

    gather_o.arrive()
    keep_h1.wait()
    sums.start(lambda s, n, step: dot(att[rows_of(s), :], wo[columns(n, step), :], 1, 1))
    gather_g.relay()
    sums.arrive()

    @pl.loop(0, half // 32)
    def _(i):
        at = pl.multiple_of(i * 32, 32)
        values = tok_src[pl.ds(pl.multiple_of(p.t * half + at, 32), 32), :].astype(F32)
        values = values + sums.total(at, 32)
        resid[pl.ds(at, 32), :] = values
        normed, _, _ = layer_norm(values, norms[2:3, :D], norms[3:4, :D])
        start = (p.j * 2 + p.t) * half + at
        hh[pl.ds(pl.multiple_of(start, 32), 32), :] = normed.astype(BF16)

    sums.release()
    spread_h.start()
    cots.start()
    spread_h.arrive()
    cots.pass_on()
    gather_g.arrive()
    gather_d.relay()

    @pl.loop(0, TP)
    def _(s):
        at = rows_of(s)
        late = pl.ds(pl.multiple_of(group + s * size, size), size)
        rows_in = hh[at, :]
        gate = dot(rows_in, wg[:, :full], 1, 0)
        up = dot(rows_in, wg[:, full : 2 * full], 1, 0)
        sig = jax.nn.sigmoid(gate)
        hid[at, :full] = (gate * sig * up).astype(BF16)
        slopes[at, :full] = (up * sig * (1.0 + gate * (1.0 - sig))).astype(BF16)
        slopes[late, :full] = (gate * sig).astype(BF16)
        gate = dot(rows_in, wg[:, 2 * full :], 1, 0)
        up = pltpu.roll(gate, 64, 1)
        sig = jax.nn.sigmoid(gate)
        first = lax.broadcasted_iota(jnp.int32, gate.shape, 1) < 64
        tail = slice(full, full + 128)
        hid[at, tail] = jnp.where(first, gate * sig * up, 0.0).astype(BF16)
        slopes[at, tail] = jnp.where(first, up * sig * (1.0 + gate * (1.0 - sig)), 0.0).astype(BF16)
        slopes[late, tail] = jnp.where(first, gate * sig, 0.0).astype(BF16)

    cots.arrive()
    step = min(256, D)

    def weight_grad(left, right, out):
        @pl.loop(0, D // step)
        def _(n):
            at = columns(n, step)
            out[at, :] = dot(left[:, at], right[...], 0, 0).astype(BF16)

    weight_grad(cot, hid, gd)
    scatter_d.start()

    gather_d.arrive()

    @pl.loop(0, TP)
    def _(s):
        at = rows_of(s)
        late = pl.ds(pl.multiple_of(group + s * size, size), size)
        dhid = dot(cot[at, :], wd[...], 1, 0)
        slope = dhid * slopes[at, : hid.shape[1]].astype(F32)
        gain = dhid * slopes[late, : hid.shape[1]].astype(F32)
        dgate[at, :full] = slope[:, :full].astype(BF16)
        dgate[at, full : 2 * full] = gain[:, :full].astype(BF16)
        last = slope[:, full:] + pltpu.roll(gain[:, full:], 64, 1)
        dgate[at, 2 * full :] = last.astype(BF16)

    cots.finish()
    sums.acquire()
    sums.start(lambda s, n, step: dot(dgate[rows_of(s), :], wg[columns(n, step), :], 1, 1))
    gather_g.finish()
    scatter_g.allow()
    weight_grad(hh, dgate, gg)
    scatter_g.start()
    spread_h.finish()
    load_h1 = pltpu.make_async_copy(h1_out, hh, h1_sem.at[1])
    load_h1.start()
    scatter_d.combine()
    sums.arrive()

    gains[...] = jnp.zeros_like(gains)

    @pl.loop(0, half // 32)
    def _(i):
        at = pl.multiple_of(i * 32, 32)
        scaled, inverse = norm_stats(resid[pl.ds(at, 32), :])
        part, gain, shift = norm_back(sums.total(at, 32), scaled, inverse, norms[2:3, :D])
        gains[2:3, :] += gain[None]
        gains[3:4, :] += shift[None]
        mine = pl.ds(pl.multiple_of((p.j * 2 + p.t) * half + at, 32), 32)
        total = cot[mine, :].astype(F32) + part
        grad[pl.ds(at, 32), :] = total
        cot[mine, :] = total.astype(BF16)

    sums.release()
    spread_r.start()
    spread_r.arrive()

    biases[...] = jnp.zeros_like(biases)

    @pl.loop(0, TP)
    def _(s):
        at = rows_of(s)
        grad_out = dot(cot[at, :], wo[...], 1, 0).astype(BF16)
        allowed = mask_of(aux_all[s][:, ROT : ROT + 1], row_all[s, 0:1, :], size)
        tables = tables_of(aux_all[s], wide)
        three = attend_back_values(
            qkv[at, :wide], qkv[at, wide : 2 * wide], qkv[at, 2 * wide :], grad_out, allowed, tables
        )
        for k, value in enumerate(three):
            lanes = slice(k * wide, (k + 1) * wide)
            qkv[at, lanes] = value
            biases[0:1, lanes] += jnp.sum(value.astype(F32), axis=0, keepdims=True)

    bias_all[p.u] = biases[...]

    def bias_copy(k):
        u = (p.u + k) % p.lines
        return remote(biases, bias_all.at[p.u], bias_sem.at[k], bias_sem.at[p.lines + k], u * TP + p.j, p.t)

    for k in range(1, p.lines):
        bias_copy(k).start()

    scatter_d.reduce()
    scatter_q.allow()
    load_h1.wait()
    weight_grad(hh, qkv, gq)
    scatter_q.start_outer()
    weight_grad(cot, att, go)
    scatter_o.start_outer()
    scatter_q.start_rest()
    scatter_o.start_rest()
    scatter_g.combine()

    sums.acquire()
    sums.start(lambda s, n, step: dot(qkv[rows_of(s), :], wq[columns(n, step), :], 1, 1))
    sums.arrive()

    @pl.loop(0, half // 32)
    def _(i):
        at = pl.multiple_of(i * 32, 32)
        values = tok_src[pl.ds(pl.multiple_of(p.t * half + at, 32), 32), :].astype(F32)
        scaled, inverse = norm_stats(values)
        part, gain, shift = norm_back(sums.total(at, 32), scaled, inverse, norms[0:1, :D])
        gains[0:1, :] += gain[None]
        gains[1:2, :] += shift[None]
        grad[pl.ds(at, 32), :] += part

    sums.release()
    mine = pl.ds(pl.multiple_of(p.t * half, half), half)

    def give(index, value, out):
        here = pltpu.make_async_copy(value, out.at[mine], swap_sem.at[index, 0])
        there = remote(value, out.at[mine], swap_sem.at[index, 1], swap_sem.at[index, 2], p.me, 1 - p.t)
        here.start()
        there.start()
        return here, there

    gives = [*give(0, grad, input_out)]

    def tile_of(d):
        return pl.ds(pl.multiple_of(d * rows // 128 * 128, 128), 128)

    def gain_copy(dest):
        return remote(gains.at[:, tile_of(dest)], small_all.at[p.me], gain_sem.at[dest], gain_sem.at[count], dest, p.t)

    pltpu.make_async_copy(gains.at[:, tile_of(p.me)], small_all.at[p.me], gain_sem.at[count]).start()
    each_dest(p, lambda dest, u, j: gain_copy(dest).start())

    sums.acquire()
    sums.start(lambda s, n, step: dot(hid[rows_of(s), :], wd[columns(n, step), :], 1, 1))
    sums.arrive()

    @pl.loop(0, half // 32)
    def _(i):
        at = pl.multiple_of(i * 32, 32)
        block[pl.ds(at, 32), :] = resid[pl.ds(at, 32), :] + sums.total(at, 32)

    gives += give(1, block, block_out)
    scatter_g.reduce()
    scatter_q.combine()
    scatter_o.combine()

    for k in range(1, p.lines):
        bias_copy(k).wait_recv()
    total = bias_all[0]
    for k in range(1, p.lines):
        total = total + bias_all[k]
    bias_out[p.j] = total

    def rank_copy(q):
        j = (p.j + q) % TP
        return remote(bias_out.at[p.j], bias_out.at[p.j], rank_sem.at[q], rank_sem.at[TP + q], p.u * TP + j, p.t)

    for q in range(1, TP):
        rank_copy(q).start()

    wait_bytes(small_all, gain_sem.at[count])
    total = small_all[0]
    for d in range(1, count):
        total = total + small_all[d]
    small_t[0] = total
    swap = remote(small_t.at[0], small_t.at[1], t_sem.at[0], t_sem.at[1], p.me, 1 - p.t)
    swap.start()
    scatter_q.reduce()
    scatter_o.reduce()
    swap.wait()
    norm_out[...] = small_t[0] + small_t[1]
    for q in range(1, TP):
        rank_copy(q).wait()
    for k in range(1, p.lines):
        bias_copy(k).wait_send()
    each_dest(p, lambda dest, u, j: small_copy(dest).wait_send())
    each_dest(p, lambda dest, u, j: gain_copy(dest).wait_send())
    for copy in gives:
        copy.wait()
    for part in (auxes, rowses, sums, spread_r, gather_q, gather_o, gather_d):
        part.finish()
    for scatter in (scatter_d, scatter_g, scatter_q, scatter_o):
        scatter.finish()


def layer(count, small, aux, row, tokens, cot, wq, wo, wg, wd):
    size = tokens.shape[0]
    half = size // 2
    group = TP * size
    lines, rows = count // TP, wq.shape[1]
    wide, pad, gates = wo.shape[2], wd.shape[2], wg.shape[2]
    any_spec = pl.BlockSpec(memory_space=pl.ANY)
    vmem = pl.BlockSpec(memory_space=pltpu.VMEM)
    dma = pltpu.SemaphoreType.DMA
    regular = pltpu.SemaphoreType.REGULAR

    def out(*shape, dtype=BF16):
        return jax.ShapeDtypeStruct(shape, dtype)

    return pl.pallas_call(
        functools.partial(layer_kernel, count),
        in_specs=[vmem, vmem, vmem, vmem] + [any_spec] * 5,
        out_specs=[any_spec] * 7 + [vmem] * 2,
        out_shape=[
            out(TP, rows, 3 * wide),
            out(TP, rows, wide),
            out(TP, rows, gates),
            out(TP, rows, pad),
            out(size, D, dtype=F32),
            out(size, D, dtype=F32),
            out(group, D),
            out(8, 128, dtype=F32),
            out(TP, 8, 3 * wide, dtype=F32),
        ],
        scratch_shapes=[
            pltpu.VMEM((D, 3 * wide), BF16),
            pltpu.VMEM((D, wide), BF16),
            pltpu.VMEM((D, gates), BF16),
            pltpu.VMEM((D, pad), BF16),
            pltpu.VMEM((group, D), BF16),
            pltpu.VMEM((group, D), BF16),
            pltpu.VMEM((group, 3 * wide), BF16),
            pltpu.VMEM((group, wide), BF16),
            pltpu.VMEM((group, pad), BF16),
            pltpu.VMEM((max(2 * group, D), max(pad, 3 * wide)), BF16),
            pltpu.VMEM((group, gates), BF16),
            pltpu.VMEM((D, pad), BF16),
            pltpu.VMEM((D, gates), BF16),
            pltpu.VMEM((D, wide), BF16),
            pltpu.VMEM((D, max(pad, 3 * wide)), BF16),
            pltpu.VMEM((D, wide), BF16),
            pltpu.VMEM((2, size, D), BF16),
            pltpu.VMEM((2, size, D), BF16),
            pltpu.VMEM((2, size, D), BF16),
            pltpu.VMEM((half, D), F32),
            pltpu.VMEM((3, half, D), BF16),
            pltpu.VMEM((half, D), F32),
            pltpu.VMEM((half, D), F32),
            pltpu.VMEM((half, D), F32),
            pltpu.VMEM((8, D), F32),
            pltpu.VMEM((8, 3 * wide), F32),
            pltpu.VMEM((16, max(D, 128 * (small.shape[0] - 16))), F32),
            pltpu.VMEM((count,) + small.shape, BF16),
            pltpu.VMEM((TP, size, 128), F32),
            pltpu.VMEM((TP, 8, size), F32),
            pltpu.VMEM((count, 8, 128), F32),
            pltpu.VMEM((lines, 8, 3 * wide), F32),
            pltpu.VMEM((2, 8, 128), F32),
            dma((4, TP + lines)),
            dma((4, 3)),
            dma((count + 1,)),
            dma((2, 4)),
            dma((2, 4)),
            dma((2, 4)),
            dma((2, 4)),
            dma((2,)),
            dma((4, TP + lines)),
            dma((4, 4)),
            regular((lines,)),
            regular((lines,)),
            dma((2, 2)),
            dma((2, 4)),
            regular((4,)),
            dma((2, 4)),
            dma((2, 4)),
            dma((2, 4)),
            dma((2, 4)),
            dma((2, 3)),
            dma((count + 1,)),
            dma((2 * lines,)),
            dma((2 * TP,)),
            dma((2,)),
        ],
        compiler_params=pltpu.CompilerParams(
            collective_id=0, has_side_effects=True, vmem_limit_bytes=63 * 1024 * 1024
        ),
        cost_estimate=pl.CostEstimate(flops=40 * 10**9, bytes_accessed=60 * 10**6, transcendentals=10**7),
        name="layer",
    )(small, aux, row, tokens, cot, wq, wo, wg, wd)


def laid_out(values):
    return with_layout_constraint(values, Layout(tuple(range(values.ndim))))


def per_device(
    count,
    tokens_in,
    segment_ids,
    d_out,
    qkv_weight,
    qkv_bias,
    out_weight,
    gating_weight,
    down_weight,
    norm_params,
    qkv_first,
    qkv_second,
    bias_first,
    bias_second,
    out_first,
    out_second,
    gating_first,
    gating_second,
    down_first,
    down_second,
    norm_first,
    norm_second,
):
    place = lax.axis_index("dp")
    rows = norm_params.shape[1]
    seq_len = tokens_in.shape[1]
    head_local = qkv_weight.shape[2]
    hidden_local = gating_weight.shape[2]
    wide = head_local // TP
    hid = hidden_local // TP
    full = hid // 128 * 128

    low_gates = laid_out(gating_weight.astype(BF16))
    heads_part, tails_part = low_gates[:, :, : TP * full], low_gates[:, :, TP * full :]
    spare = hid - full
    weights = (
        jnp.stack(
            [
                jnp.concatenate([qkv_weight[:, k, j * wide : (j + 1) * wide] for k in range(3)], axis=1)
                for j in range(TP)
            ]
        ).astype(BF16),
        out_weight.astype(BF16).reshape(TP, wide, rows).transpose(0, 2, 1),
        jnp.stack(
            [
                jnp.concatenate(
                    [heads_part[:, k, j * full : (j + 1) * full] for k in range(2)]
                    + [tails_part[:, k, j * spare : (j + 1) * spare] for k in range(2)],
                    axis=1,
                )
                for j in range(TP)
            ]
        ),
        jnp.concatenate(
            [
                down_weight[: TP * full].astype(BF16).reshape(TP, full, rows),
                down_weight[TP * full :].astype(BF16).reshape(TP, spare, rows),
                jnp.zeros((TP, -hid % 128, rows), BF16),
            ],
            axis=1,
        ).transpose(0, 2, 1),
    )
    bias_here = qkv_bias.shape[1]
    small_norm = lax.dynamic_update_slice(jnp.zeros((16, 128), F32), norm_params, (0, (place * rows) % 128))
    small_bias = lax.dynamic_update_slice(jnp.zeros((3 * head_local,), F32), qkv_bias[0], (place * bias_here,))
    small = jnp.concatenate([small_norm, small_bias.reshape(-1, 128)]).astype(BF16)
    segments = segment_ids[0]
    earlier = jnp.sum((segments[None, :] < segments[:, None]).astype(jnp.int32), axis=1)
    positions = (jnp.arange(seq_len, dtype=jnp.int32) - earlier).astype(F32)
    frequency = 10000.0 ** (-2.0 * jnp.arange(ROT // 2, dtype=F32) / ROT)
    angles = positions[:, None] * frequency[None, :]
    aux = jnp.concatenate([jnp.cos(angles), jnp.sin(angles), segments[:, None].astype(F32)], axis=1)
    aux = jnp.pad(aux, ((0, 0), (0, 128 - aux.shape[1])))
    row = jnp.broadcast_to(segments.astype(F32)[None], (8, seq_len))

    rs_q, rs_o, rs_g, rs_d, block_out, input_grad, _, norm_sum, bias_sum = layer(
        count, small, aux, row, tokens_in[0], d_out[0], *weights
    )

    gate_parts = [
        jnp.concatenate(
            [rs_g[j, :, k * full : (k + 1) * full] for j in range(TP)]
            + [rs_g[j, :, 2 * full + k * spare : 2 * full + (k + 1) * spare] for j in range(TP)],
            axis=1,
        )
        for k in range(2)
    ]
    gating_shard = lax.optimization_barrier(laid_out(jnp.stack(gate_parts, axis=1))).astype(F32)
    qkv_shard = jnp.stack(
        [
            jnp.concatenate([rs_q[j, :, k * wide : (k + 1) * wide] for j in range(TP)], axis=1)
            for k in range(3)
        ],
        axis=1,
    ).astype(F32)
    out_shard = laid_out(rs_o.transpose(0, 2, 1).reshape(head_local, rows)).astype(F32)
    down_parts = rs_d.transpose(0, 2, 1)
    down_shard = laid_out(
        jnp.concatenate(
            [down_parts[:, :full].reshape(TP * full, rows), down_parts[:, full:hid].reshape(TP * spare, rows)]
        )
    ).astype(F32)
    norm_grad = lax.dynamic_slice_in_dim(norm_sum[:4], (place * rows) % 128, rows, 1)
    bias_grad = bias_sum[:, 0].reshape(TP, 3, wide).transpose(1, 0, 2).reshape(1, 3 * head_local)
    bias_grad = lax.dynamic_slice_in_dim(bias_grad, place * bias_here, bias_here, 1)
    return (
        block_out[None],
        input_grad[None],
        *adamw_update(qkv_weight, qkv_shard, qkv_first, qkv_second, D ** (-0.5), 0.1),
        *adamw_update(qkv_bias, bias_grad, bias_first, bias_second, 0.3, 0.0),
        *adamw_update(out_weight, out_shard, out_first, out_second, (H * HD // 16) ** (-0.5), 0.1),
        *adamw_update(gating_weight, gating_shard, gating_first, gating_second, D ** (-0.5), 0.1),
        *adamw_update(down_weight, down_shard, down_first, down_second, FF ** (-0.5), 0.1),
        *adamw_update(norm_params, norm_grad, norm_first, norm_second, 0.25, 0.0),
    )


def solution(mesh):
    tokens = P("dp", None, None)
    qkv = P("dp", None, "tensor")
    rest = P("tensor", "dp")
    norm = P(None, "dp")
    weights = (qkv, rest, rest, qkv, rest, norm)
    states = (qkv, qkv, rest, rest, rest, rest, qkv, qkv, rest, rest, norm, norm)
    return jax.shard_map(
        functools.partial(per_device, mesh.shape["dp"]),
        mesh=mesh,
        in_specs=(tokens, P("dp", None), tokens, *weights, *states),
        out_specs=(tokens, tokens, *(spec for spec in weights for _ in range(3))),
        check_vma=False,
    )
```

```python
import functools

import jax
import jax.numpy as jnp
from jax import lax
from jax.experimental import pallas as pl
from jax.experimental.layout import Layout, with_layout_constraint
from jax.experimental.pallas import tpu as pltpu
from jax.sharding import PartitionSpec as P

D = 2048
H = 32
HD = 64
ROT = 16
FF = 5632
STEP = 10
TP = 4

F32 = jnp.float32
BF16 = jnp.bfloat16


def layer_norm(values, scale_row, shift_row):
    centre = values - jnp.mean(values, axis=-1, keepdims=True)
    spread = jnp.mean(centre * centre, axis=-1, keepdims=True)
    inverse = lax.rsqrt(spread + 1e-05)
    scaled = centre * inverse
    return (scaled * scale_row + shift_row, scaled, inverse)


def norm_back(grad_in, scaled, inverse, scale_row):
    grad_scaled = grad_in * scale_row
    mean_first = jnp.mean(grad_scaled, axis=-1, keepdims=True)
    mean_second = jnp.mean(grad_scaled * scaled, axis=-1, keepdims=True)
    grad_values = inverse * (grad_scaled - mean_first - scaled * mean_second)
    return (grad_values, jnp.sum(grad_in * scaled, axis=0), jnp.sum(grad_in, axis=0))


def adamw_update(weight_old, gradient, first_old, second_old, step_rate, decay_rate):
    first_new = 0.9 * first_old + 0.1 * gradient
    second_new = 0.95 * second_old + 0.05 * gradient * gradient
    corrected = first_new / (1.0 - 0.9**STEP) / (jnp.sqrt(second_new / (1.0 - 0.95**STEP)) + 1e-08)
    return (weight_old - step_rate * (corrected + decay_rate * weight_old), first_new, second_new)


def dot(a, b, ca, cb):
    return lax.dot_general(a, b, (((ca,), (cb,)), ((), ())), preferred_element_type=F32)


def spin(values, cos_t, lower_t, upper_t):
    wide = values.shape[1]
    return (
        values * cos_t
        + pltpu.roll(values, wide - ROT // 2, 1) * lower_t
        + pltpu.roll(values, ROT // 2, 1) * upper_t
    )


def spin_back(values, cos_t, lower_t, upper_t):
    wide = values.shape[1]
    return (
        values * cos_t
        + pltpu.roll(values * lower_t, ROT // 2, 1)
        + pltpu.roll(values * upper_t, wide - ROT // 2, 1)
    )


def mask_of(seg_col, seg_row, size):
    rows = lax.broadcasted_iota(jnp.int32, (size, size), 0)
    cols = lax.broadcasted_iota(jnp.int32, (size, size), 1)
    return (seg_col == seg_row) & (cols <= rows)


def attend_back_values(query, key, value, grad, allowed, tables):
    head_of = lax.broadcasted_iota(jnp.int32, query.shape, 1) // HD
    zero = jnp.zeros_like(query)
    dq = jnp.zeros(query.shape, F32)
    dk = jnp.zeros(query.shape, F32)
    dv = jnp.zeros(query.shape, F32)
    for head in range(query.shape[1] // HD):
        mine = head_of == head
        query_h = jnp.where(mine, query, zero)
        grad_h = jnp.where(mine, grad, zero)
        scores = dot(query_h, key, 1, 1) * HD ** (-0.5)
        scores = jnp.where(allowed, scores, -1e30)
        weights = jnp.exp(scores - jnp.max(scores, axis=1, keepdims=True))
        prob = weights / jnp.sum(weights, axis=1, keepdims=True)
        dv = dv + dot(prob.astype(BF16), grad_h, 0, 0)
        dprob = dot(grad_h, value, 1, 1)
        delta = jnp.sum(prob * dprob, axis=1, keepdims=True)
        dscore = (prob * (dprob - delta)).astype(BF16)
        dq = jnp.where(mine, dot(dscore, key, 1, 0), dq)
        dk = dk + dot(dscore, query_h, 0, 0)
    dq = spin_back(dq * HD ** (-0.5), *tables).astype(BF16)
    dk = spin_back(dk * HD ** (-0.5), *tables).astype(BF16)
    return dq, dk, dv.astype(BF16)


class Place:
    def __init__(self, count):
        self.count = count
        self.lines = count // TP
        self.me = lax.axis_index("dp")
        self.t = lax.axis_index("tensor")
        self.u = self.me // TP
        self.j = self.me % TP
        self.x = self.j // 2
        self.c = self.j % 2
        self.core_peer = self.me + 1 - 2 * self.c
        self.x_peer = self.me + 2 - 4 * self.x

    def group(self, k):
        x = (self.x + k // 2) % 2
        return self.u * TP + x * 2 + self.c, (self.t + k % 2) % 2, x


def remote(src, dst, send_sem, recv_sem, dp, t):
    return pltpu.make_async_remote_copy(
        src_ref=src,
        dst_ref=dst,
        send_sem=send_sem,
        recv_sem=recv_sem,
        device_id=(dp, t),
        device_id_type=pl.DeviceIdType.MESH,
    )


def wait_bytes(ref, sem):
    pltpu.make_async_copy(ref, ref, sem).wait()


def greet(place):
    barrier = pltpu.get_barrier_semaphore()

    @pl.loop(1, place.count)
    def _(k):
        pl.semaphore_signal(
            barrier,
            inc=1,
            device_id=((place.me + k) % place.count, place.t),
            device_id_type=pl.DeviceIdType.MESH,
        )

    for k in (1, 3):
        dp, t, _ = place.group(k)
        pl.semaphore_signal(barrier, inc=1, device_id=(dp, t), device_id_type=pl.DeviceIdType.MESH)
    pl.semaphore_wait(barrier, place.count + 1)


def each_dest(place, act):
    if place.lines == 4:

        @pl.loop(1, TP)
        def _(q):
            j = (place.j + q) % TP
            act(place.u * TP + j, place.u, j)

        @pl.loop(0, TP)
        def _(q):
            j = (place.j + q) % TP
            for dz in (2, 1, 3):
                u = (place.u + dz) % 4
                act(u * TP + j, u, j)

    else:

        @pl.loop(1, place.count)
        def _(k):
            dest = (place.me + k) % place.count
            act(dest, dest // TP, dest % TP)


class WeightGather:
    def __init__(self, place, index, src, dst, send_sem, recv_sem):
        self.place, self.src, self.dst = place, src, dst
        self.send_sem, self.recv_sem = send_sem.at[index], recv_sem.at[index]
        self.rows = src.shape[1]

    def group_copy(self, q):
        p = self.place
        j = (p.j + q) % TP
        mine = self.dst.at[pl.ds(p.me * self.rows, self.rows)]
        return remote(self.src.at[j], mine, self.send_sem.at[q], self.recv_sem.at[2], p.u * TP + j, p.t)

    def chunk(self, u):
        size = TP * self.rows
        return self.dst.at[pl.ds(u * size, size)]

    def line_copy(self, k):
        p = self.place
        u = (p.u + k) % p.lines
        sem = 0
        if p.lines == 4:
            sem = jnp.where(self.middle(), jnp.where(p.u + u == 3, 3, 0), jnp.where(jnp.abs(p.u - u) == 2, 1, 0))
        mine = self.chunk(p.u)
        return remote(mine, mine, self.send_sem.at[TP + k], self.recv_sem.at[sem], u * TP + p.j, p.t)

    def line_each(self, act):
        p = self.place
        if p.lines == 4:
            for k in (2, 1, 3):
                gap = jnp.abs(p.u - (p.u + k) % 4)
                pl.when((gap == 1) | ((gap == 2) & ~self.middle()))(lambda k=k: act(k))
        else:
            for k in range(1, p.lines):
                act(k)

    def start(self):
        p = self.place
        for q in (2, 3, 1):
            self.group_copy(q).start()
        mine = self.dst.at[pl.ds(p.me * self.rows, self.rows)]
        pltpu.make_async_copy(self.src.at[p.j], mine, self.recv_sem.at[2]).start()

    def pass_on(self):
        wait_bytes(self.chunk(0), self.recv_sem.at[2])
        self.line_each(lambda k: self.line_copy(k).start())

    def middle(self):
        return (self.place.u == 1) | (self.place.u == 2)

    def forward(self, which):
        p = self.place
        up = p.u == 2
        chunk = self.chunk(jnp.where(up, which, 3 - which))
        sem = self.send_sem.at[TP + 2 * which]
        return remote(chunk, chunk, sem, self.recv_sem.at[1], p.me + jnp.where(up, TP, -TP), p.t)

    def relay(self):
        if self.place.lines == 4:

            @pl.when(self.middle())
            def _():
                wait_bytes(self.chunk(0), self.recv_sem.at[3])
                self.forward(1).start()
                wait_bytes(self.chunk(0), self.recv_sem.at[1])
                self.forward(0).start()

    def arrive(self):
        p = self.place
        size = TP * self.rows
        if p.lines == 4:
            wait_bytes(self.chunk(0), self.recv_sem.at[0])
            pl.when(~self.middle())(lambda: wait_bytes(self.dst.at[pl.ds(0, 2 * size)], self.recv_sem.at[1]))
        else:
            wait_bytes(self.dst.at[pl.ds(0, size * (p.lines - 1))], self.recv_sem.at[0])

    def finish(self):
        for q in range(1, TP):
            self.group_copy(q).wait_send()
        self.line_each(lambda k: self.line_copy(k).wait_send())
        if self.place.lines == 4:

            @pl.when(self.middle())
            def _():
                self.forward(1).wait_send()
                self.forward(0).wait_send()


class GroupSum:
    def __init__(self, place, to_core, from_core, low, own, parts, core_sem, part_sem, free_sem=None):
        self.place = place
        self.to_core, self.from_core, self.low, self.own, self.parts = to_core, from_core, low, own, parts
        self.core_sem, self.part_sem, self.free_sem = core_sem, part_sem, free_sem

    def core_copy(self, i):
        p = self.place
        return remote(
            self.to_core.at[i], self.from_core.at[i], self.core_sem.at[0, i], self.core_sem.at[1, i], p.core_peer, p.t
        )

    def part_copy(self, k):
        p = self.place
        half = self.parts.shape[1]
        dp, t, _ = p.group(k)
        block = self.low.at[0 if k >= 2 else 1, pl.ds(pl.multiple_of(t * half, half), half)]
        return remote(block, self.parts.at[k - 1], self.part_sem.at[0, k], self.part_sem.at[1, k], dp, t)

    def start(self, product):
        p = self.place
        step = min(512, D)
        other = [(p.x + 1) % 2, p.x]
        for i in range(2):

            @pl.loop(0, D // step)
            def _(n):
                at = pl.ds(pl.multiple_of(n * step, step), step)
                self.to_core[i, :, at] = product(other[i] * 2 + 1 - p.c, n, step).astype(BF16)

            self.core_copy(i).start()
        for i in range(2):
            self.core_copy(i).wait_recv()

            @pl.loop(0, D // step)
            def _(n):
                at = pl.ds(pl.multiple_of(n * step, step), step)
                total = product(other[i] * 2 + p.c, n, step) + self.from_core[i, :, at].astype(F32)
                self.low[i, :, at] = total.astype(BF16)
                if i == 1:
                    half = self.own.shape[0]

                    @pl.when(p.t == 0)
                    def _():
                        self.own[:, at] = total[:half]

                    @pl.when(p.t == 1)
                    def _():
                        self.own[:, at] = total[half:]

            for k in (3, 2) if i == 0 else (1,):
                self.part_copy(k).start()

    def arrive(self):
        for k in (3, 2, 1):
            self.part_copy(k).wait_recv()

    def total(self, at, rows):
        value = self.own[pl.ds(pl.multiple_of(at, 32), rows), :]
        for k in range(3):
            value = value + self.parts[k, pl.ds(pl.multiple_of(at, 32), rows), :].astype(F32)
        return value

    def finish(self):
        for i in range(2):
            self.core_copy(i).wait_send()
        for k in (1, 2, 3):
            self.part_copy(k).wait_send()

    def release(self):
        p = self.place
        pl.semaphore_signal(
            self.free_sem.at[0], inc=1, device_id=(p.core_peer, p.t), device_id_type=pl.DeviceIdType.MESH
        )
        for k in (1, 2, 3):
            dp, t, _ = p.group(k)
            pl.semaphore_signal(
                self.free_sem.at[k], inc=1, device_id=(dp, t), device_id_type=pl.DeviceIdType.MESH
            )

    def acquire(self):
        self.finish()
        for k in range(4):
            pl.semaphore_wait(self.free_sem.at[k], 1)


class GroupGather:
    def __init__(self, place, out, size, part_sem, core_sem):
        self.place, self.out, self.half = place, out, size // 2
        self.part_sem, self.core_sem = part_sem, core_sem

    def block(self, x, t):
        p = self.place
        start = ((x * 2 + p.c) * 2 + t) * self.half
        return self.out.at[pl.ds(pl.multiple_of(start, self.half), self.half)]

    def part_copy(self, k):
        p = self.place
        dp, t, _ = p.group(k)
        mine = self.block(p.x, p.t)
        return remote(mine, mine, self.part_sem.at[0, k], self.part_sem.at[1, k], dp, t)

    def core_copy(self, k):
        p = self.place
        _, t, x = p.group(k)
        block = self.block(x, t)
        return remote(block, block, self.core_sem.at[0, k], self.core_sem.at[1, k], p.core_peer, p.t)

    def start(self):
        for k in (3, 2, 1):
            self.part_copy(k).start()
        self.core_copy(0).start()

    def arrive(self):
        for k in (1, 2, 3):
            self.part_copy(k).wait_recv()
            self.core_copy(k).start()
        for k in range(4):
            self.core_copy(k).wait_recv()

    def finish(self):
        for k in (1, 2, 3):
            self.part_copy(k).wait_send()
        for k in range(4):
            self.core_copy(k).wait_send()


class GroupPieces:
    def __init__(self, place, src, out, sem, size=0):
        self.place, self.src, self.out, self.sem, self.size = place, src, out, sem, size

    def at(self, j):
        if self.size:
            return self.out.at[pl.ds(pl.multiple_of(j * self.size, self.size), self.size)]
        return self.out.at[j]

    def own(self):
        return pltpu.make_async_copy(self.src, self.at(self.place.j), self.sem.at[0, 0])

    def near(self, k):
        p = self.place
        dest = p.core_peer if k == 1 else p.x_peer
        return remote(self.src, self.at(p.j), self.sem.at[0, k], self.sem.at[1, k], dest, p.t)

    def relay(self):
        p = self.place
        block = self.at((p.j + 2) % TP)
        return remote(block, block, self.sem.at[0, 3], self.sem.at[1, 3], p.core_peer, p.t)

    def start(self):
        self.near(2).start()
        self.near(1).start()
        self.own().start()

    def pass_on(self):
        self.near(2).wait_recv()
        self.relay().start()

    def arrive(self):
        self.near(1).wait_recv()
        self.relay().wait_recv()
        self.own().wait()

    def finish(self):
        self.near(1).wait_send()
        self.near(2).wait_send()
        self.relay().wait_send()


def tables_of(aux, wide):
    half = ROT // 2
    line = lax.broadcasted_iota(jnp.int32, (aux.shape[1], wide), 0)
    lane = lax.broadcasted_iota(jnp.int32, (aux.shape[1], wide), 1) % HD
    first = lane < half
    second = (lane >= half) & (lane < ROT)

    def spread(pick, sign):
        table = jnp.where(pick, sign, 0.0).astype(F32)
        return lax.dot_general(
            aux, table, (((1,), (0,)), ((), ())), precision=lax.Precision.HIGHEST, preferred_element_type=F32
        )

    rest = lax.broadcasted_iota(jnp.int32, (aux.shape[0], wide), 1) % HD >= ROT
    cos_t = spread((line == lane % half) & (first | second), 1.0) + jnp.where(rest, 1.0, 0.0)
    low_t = spread((line == lane + half) & first, -1.0)
    upp_t = spread((line == lane) & second, 1.0)
    return cos_t, low_t, upp_t


def attend_values(query, key, value, allowed):
    head_of = lax.broadcasted_iota(jnp.int32, query.shape, 1) // HD
    total = jnp.zeros(query.shape, F32)
    for head in range(query.shape[1] // HD):
        mine = head_of == head
        scores = dot(jnp.where(mine, query, jnp.zeros_like(query)), key, 1, 1) * HD ** (-0.5)
        scores = jnp.where(allowed, scores, -1e30)
        weights = jnp.exp(scores - jnp.max(scores, axis=1, keepdims=True))
        prob = weights / jnp.sum(weights, axis=1, keepdims=True)
        total = jnp.where(mine, dot(prob.astype(BF16), value, 1, 0), total)
    return total


class GradScatter:
    def __init__(self, place, index, grad, slots, out, send_sem, recv_sem, free_sem=None):
        self.place, self.grad, self.slots, self.out = place, grad, slots, out
        self.send_sem, self.recv_sem, self.free_sem = send_sem.at[index], recv_sem.at[index], free_sem
        self.rows = out.shape[1]
        self.size = TP * self.rows

    def chunk(self, ref, u):
        return ref.at[pl.ds(u * self.size, self.size)]

    def near(self, u):
        return jnp.abs(self.place.u - u) < 3 if self.place.lines == 4 else None

    def line_each(self, act, picked=lambda u: True):
        p = self.place
        for k in (2, 1, 3) if p.lines == 4 else range(1, p.lines):
            u = (p.u + k) % p.lines
            if p.lines == 4:
                pl.when(self.near(u) & picked(u))(lambda k=k, u=u: act(k, u))
            else:
                act(k, u)

    def line_copy(self, k, u):
        p = self.place
        far = 0
        if p.lines == 4:
            far = (((p.u == 0) & (u == 2)) | ((p.u == 3) & (u == 1))).astype(jnp.int32)
        return remote(
            self.chunk(self.grad, u), self.chunk(self.slots, p.u), self.send_sem.at[TP + k], self.recv_sem.at[far],
            u * TP + p.j, p.t,
        )

    def outer(self):
        p = self.place
        first = p.u == 0
        src, dst = self.chunk(self.grad, jnp.where(first, 3, 0)), self.chunk(self.slots, jnp.where(first, 1, 2))
        return remote(src, dst, self.send_sem.at[TP], self.recv_sem.at[2], p.me + jnp.where(first, TP, -TP), p.t)

    def ends(self):
        return (self.place.u == 0) | (self.place.u == 3)

    def later(self, u):
        p = self.place
        return ((p.u == 1) & (u == 3)) | ((p.u == 2) & (u == 0))

    def allow(self):
        p = self.place
        self.line_each(
            lambda k, u: pl.semaphore_signal(
                self.free_sem.at[p.u], inc=1, device_id=(u * TP + p.j, p.t), device_id_type=pl.DeviceIdType.MESH
            )
        )

    def start(self):
        self.start_outer()
        self.start_rest()

    def start_outer(self):
        if self.free_sem is not None:
            self.line_each(lambda k, u: pl.semaphore_wait(self.free_sem.at[u], 1))
        if self.place.lines == 4:
            pl.when(self.ends())(lambda: self.outer().start())

    def start_rest(self):
        if self.place.lines == 4:
            self.line_each(lambda k, u: self.line_copy(k, u).start(), lambda u: ~self.later(u))
        else:
            self.line_each(lambda k, u: self.line_copy(k, u).start())

    def add(self, u, sources):
        p = self.place

        @pl.loop(0, self.size // 32)
        def _(i):
            at = pl.ds(pl.multiple_of(u * self.size + i * 32, 32), 32)
            total = self.grad[at, :].astype(F32)
            for slot in sources:
                here = pl.ds(pl.multiple_of(slot * self.size + i * 32, 32), 32)
                total = total + self.slots[here, :].astype(F32)
            self.grad[at, :] = total.astype(BF16)

    def combine(self):
        p = self.place
        if p.lines != 4:
            return

        @pl.when(~self.ends())
        def _():
            wait_bytes(self.chunk(self.slots, 0), self.recv_sem.at[2])
            self.add(jnp.where(p.u == 1, 3, 0), [p.u])
            self.line_each(lambda k, u: self.line_copy(k, u).start(), self.later)

    def group_copy(self, q):
        p = self.place
        j = (p.j + q) % TP
        block = self.grad.at[pl.ds((p.u * TP + j) * self.rows, self.rows)]
        return remote(block, self.out.at[p.j], self.send_sem.at[q], self.recv_sem.at[3], p.u * TP + j, p.t)

    def reduce(self):
        p = self.place
        if p.lines == 4:
            wait_bytes(self.slots.at[pl.ds(0, 2 * self.size)], self.recv_sem.at[0])
            pl.when(~self.ends())(lambda: wait_bytes(self.chunk(self.slots, 0), self.recv_sem.at[1]))
            pl.when(self.ends())(lambda: self.add(p.u, [1, 2]))
            pl.when(p.u == 1)(lambda: self.add(p.u, [0, 2, 3]))
            pl.when(p.u == 2)(lambda: self.add(p.u, [0, 1, 3]))
        else:
            wait_bytes(self.slots.at[pl.ds(0, (p.lines - 1) * self.size)], self.recv_sem.at[0])
            for k in range(1, p.lines):
                self.add(p.u, [(p.u + k) % p.lines])
        for q in (2, 3, 1):
            self.group_copy(q).start()
        own = self.grad.at[pl.ds(p.me * self.rows, self.rows)]
        pltpu.make_async_copy(own, self.out.at[p.j], self.recv_sem.at[3]).start()

    def finish(self):
        wait_bytes(self.out, self.recv_sem.at[3])
        for q in range(1, TP):
            self.group_copy(q).wait_send()
        self.line_each(lambda k, u: self.line_copy(k, u).wait_send())
        if self.place.lines == 4:
            pl.when(self.ends())(lambda: self.outer().wait_send())


def norm_stats(values):
    centre = values - jnp.mean(values, axis=-1, keepdims=True)
    inverse = lax.rsqrt(jnp.mean(centre * centre, axis=-1, keepdims=True) + 1e-05)
    return centre * inverse, inverse


def layer_kernel(
    count,
    small_src, aux_src, row_src, tok_src, cot_src, wq_src, wo_src, wga_src, wda_src, wgb_src, wdb_src,
    rs_q, rs_o, rs_ga, rs_da, rs_gb, rs_db, block_out, input_out, h1_out, norm_out, bias_out,
    wq, wo, wga, wda, wgb, wdb, cot, hh, qkv, att, hid, slopes, dga, dgb, gda, gga, gdb, ggb, go,
    slots_ga, slots_da, slots_db, slots_o,
    to_core, from_core, low, own, parts, grad, resid, gains, biases, norms,
    small, aux_all, row_all, small_all, bias_all, gains_t,
    w_send, w_recv, small_sem, aux_sem, row_sem, tok_sem, cot_sem, h1_sem,
    rs_send, rs_recv, free_g, free_q, core_sem, part_sem, free_sem, part2_sem, core2_sem, part3_sem, core3_sem,
    swap_sem, gain_sem, bias_sem, rank_sem, t_sem,
):
    p = Place(count)
    size = tok_src.shape[0]
    half = size // 2
    group = TP * size
    wide = att.shape[1]
    rows = wq_src.shape[1]
    first = wda.shape[1]
    second = hid.shape[1] - 128 - first
    greet(p)

    def rows_of(s):
        return pl.ds(pl.multiple_of(s * size, size), size)

    def columns(n, step):
        return pl.ds(pl.multiple_of(n * step, step), step)

    gathers = [
        WeightGather(p, i, src, dst, w_send, w_recv)
        for i, (src, dst) in enumerate(
            ((wq_src, wq), (wo_src, wo), (wga_src, wga), (wda_src, wda), (wgb_src, wgb), (wdb_src, wdb))
        )
    ]
    gather_q, gather_o, gather_ga, gather_da, gather_gb, gather_db = gathers
    tok = cot
    auxes = GroupPieces(p, aux_src, aux_all, aux_sem)
    rowses = GroupPieces(p, row_src, row_all, row_sem)
    tokens = GroupPieces(p, tok_src, tok, tok_sem, size)
    cots = GroupPieces(p, cot_src, cot, cot_sem, size)
    sums = GroupSum(p, to_core, from_core, low, own, parts, core_sem, part_sem, free_sem)
    spread_h = GroupGather(p, hh, size, part2_sem, core2_sem)
    spread_r = GroupGather(p, cot, size, part3_sem, core3_sem)
    gq = slopes.at[:D, : 3 * wide]
    scatters = [
        GradScatter(p, i, g, slots, out, rs_send, rs_recv, free)
        for i, (g, slots, out, free) in enumerate(
            (
                (gq, wga.at[:, : 3 * wide], rs_q, free_q),
                (go, slots_o, rs_o, None),
                (gga, slots_ga, rs_ga, None),
                (gda, slots_da, rs_da, None),
                (ggb, wgb, rs_gb, free_g),
                (gdb, slots_db, rs_db, None),
            )
        )
    ]
    scatter_q, scatter_o, scatter_ga, scatter_da, scatter_gb, scatter_db = scatters

    def small_copy(dest):
        return remote(small_src, small.at[p.me], small_sem.at[dest], small_sem.at[count], dest, p.t)

    pltpu.make_async_copy(small_src, small.at[p.me], small_sem.at[count]).start()
    each_dest(p, lambda dest, u, j: small_copy(dest).start())
    gather_q.start()
    auxes.start()
    rowses.start()
    gather_o.start()
    for part in gathers[2:4]:
        part.start()
    tokens.start()
    for part in gathers[4:]:
        part.start()
    for part in gathers[:4]:
        part.pass_on()
    auxes.pass_on()
    rowses.pass_on()
    tokens.pass_on()

    wait_bytes(small, small_sem.at[count])
    per_tile = 128 // rows
    for m in range(D // 128):
        tile = jnp.zeros((8, 128), F32)
        for i in range(per_tile):
            tile = tile + small[m * per_tile + i].astype(F32)[0:8]
        norms[0:8, m * 128 : (m + 1) * 128] = tile
    bias_rows = small.shape[1] - 16
    total = jnp.zeros((bias_rows, 128), F32)
    for d in range(count):
        total = total + small[d].astype(F32)[16:]
    for i in range(bias_rows):
        norms[8:9, i * 128 : (i + 1) * 128] = total[i : i + 1]
    auxes.arrive()
    rowses.arrive()
    gather_q.relay()
    tokens.arrive()

    @pl.loop(0, group // 32)
    def _(i):
        at = pl.ds(pl.multiple_of(i * 32, 32), 32)
        normed, _, _ = layer_norm(tok[at, :].astype(F32), norms[0:1, :D], norms[1:2, :D])
        hh[at, :] = normed.astype(BF16)

    tokens.finish()
    keep_h1 = pltpu.make_async_copy(hh, h1_out, h1_sem.at[0])
    keep_h1.start()
    gather_q.arrive()
    gather_gb.pass_on()
    gather_db.pass_on()
    gather_o.relay()
    head_wide = (bias_rows * 128) // 3

    @pl.loop(0, TP)
    def _(s):
        at = rows_of(s)
        proj = dot(hh[at, :], wq[...], 1, 0)
        tables = tables_of(aux_all[s], wide)

        def part(k):
            lanes = pl.ds(pl.multiple_of(k * head_wide + p.j * wide, 128), wide)
            return proj[:, k * wide : (k + 1) * wide] + norms[8:9, lanes]

        query = spin(part(0), *tables).astype(BF16)
        key = spin(part(1), *tables).astype(BF16)
        value = part(2).astype(BF16)
        qkv[at, :wide] = query
        qkv[at, wide : 2 * wide] = key
        qkv[at, 2 * wide :] = value
        allowed = mask_of(aux_all[s][:, ROT : ROT + 1], row_all[s, 0:1, :], size)
        att[at, :] = attend_values(query, key, value, allowed).astype(BF16)

    gather_o.arrive()
    keep_h1.wait()
    sums.start(lambda s, n, step: dot(att[rows_of(s), :], wo[columns(n, step), :], 1, 1))
    gather_ga.relay()
    sums.arrive()

    @pl.loop(0, half // 32)
    def _(i):
        at = pl.multiple_of(i * 32, 32)
        values = tok_src[pl.ds(pl.multiple_of(p.t * half + at, 32), 32), :].astype(F32)
        values = values + sums.total(at, 32)
        resid[pl.ds(at, 32), :] = values
        normed, _, _ = layer_norm(values, norms[2:3, :D], norms[3:4, :D])
        start = (p.j * 2 + p.t) * half + at
        hh[pl.ds(pl.multiple_of(start, 32), 32), :] = normed.astype(BF16)

    sums.release()
    spread_h.start()
    cots.start()
    spread_h.arrive()
    cots.pass_on()
    gather_da.relay()
    gather_gb.relay()
    gather_db.relay()
    step = min(256, D)

    def weight_grad(left, right, out):
        @pl.loop(0, D // step)
        def _(n):
            at = columns(n, step)
            out[at, :] = dot(left[:, at], right, 0, 0).astype(BF16)

    def late_rows(s):
        return pl.ds(pl.multiple_of(group + s * size, size), size)

    def hidden_part(weights, base, width, mixed):
        @pl.loop(0, TP)
        def _(s):
            at, late = rows_of(s), late_rows(s)
            rows_in = hh[at, :]
            lanes = slice(base, base + width)
            gate = dot(rows_in, weights[:, :width], 1, 0)
            up = dot(rows_in, weights[:, width : 2 * width], 1, 0)
            sig = jax.nn.sigmoid(gate)
            hid[at, lanes] = (gate * sig * up).astype(BF16)
            slopes[at, lanes] = (up * sig * (1.0 + gate * (1.0 - sig))).astype(BF16)
            slopes[late, lanes] = (gate * sig).astype(BF16)
            if mixed:
                gate = dot(rows_in, weights[:, 2 * width :], 1, 0)
                up = pltpu.roll(gate, 64, 1)
                sig = jax.nn.sigmoid(gate)
                left = lax.broadcasted_iota(jnp.int32, gate.shape, 1) < 64
                lanes = slice(base + width, base + width + 128)
                hid[at, lanes] = jnp.where(left, gate * sig * up, 0.0).astype(BF16)
                slopes[at, lanes] = jnp.where(left, up * sig * (1.0 + gate * (1.0 - sig)), 0.0).astype(BF16)
                slopes[late, lanes] = jnp.where(left, gate * sig, 0.0).astype(BF16)

    def gates_part(weights, base, width, mixed, out):
        @pl.loop(0, TP)
        def _(s):
            at, late = rows_of(s), late_rows(s)
            lanes = slice(base, base + weights.shape[1])
            dhid = dot(cot[at, :], weights[...], 1, 0)
            slope = dhid * slopes[at, lanes].astype(F32)
            gain = dhid * slopes[late, lanes].astype(F32)
            out[at, :width] = slope[:, :width].astype(BF16)
            out[at, width : 2 * width] = gain[:, :width].astype(BF16)
            if mixed:
                last = slope[:, width:] + pltpu.roll(gain[:, width:], 64, 1)
                out[at, 2 * width :] = last.astype(BF16)

    gather_ga.arrive()
    hidden_part(wga, 0, first, False)
    cots.arrive()
    weight_grad(cot, hid[:, :first], gda)
    scatter_da.start()
    gather_da.arrive()
    gates_part(wda, 0, first, False, dga)
    weight_grad(hh, dga[...], gga)
    scatter_ga.start()
    gather_gb.arrive()
    hidden_part(wgb, first, second, True)
    weight_grad(cot, hid[:, first:], gdb)
    scatter_db.start()
    gather_db.arrive()
    gates_part(wdb, first, second, True, dgb)

    cots.finish()
    sums.acquire()
    sums.start(
        lambda s, n, step: dot(dga[rows_of(s), :], wga[columns(n, step), :], 1, 1)
        + dot(dgb[rows_of(s), :], wgb[columns(n, step), :], 1, 1)
    )
    gather_gb.finish()
    gather_ga.finish()
    scatter_gb.allow()
    scatter_q.allow()
    weight_grad(hh, dgb[...], ggb)
    scatter_gb.start()
    spread_h.finish()
    load_h1 = pltpu.make_async_copy(h1_out, hh, h1_sem.at[1])
    load_h1.start()
    scatter_da.combine()
    scatter_ga.combine()
    sums.arrive()

    gains[...] = jnp.zeros_like(gains)

    @pl.loop(0, half // 32)
    def _(i):
        at = pl.multiple_of(i * 32, 32)
        scaled, inverse = norm_stats(resid[pl.ds(at, 32), :])
        part, gain, shift = norm_back(sums.total(at, 32), scaled, inverse, norms[2:3, :D])
        gains[2:3, :] += gain[None]
        gains[3:4, :] += shift[None]
        mine = pl.ds(pl.multiple_of((p.j * 2 + p.t) * half + at, 32), 32)
        total = cot[mine, :].astype(F32) + part
        grad[pl.ds(at, 32), :] = total
        cot[mine, :] = total.astype(BF16)

    sums.release()
    spread_r.start()
    spread_r.arrive()

    sums.acquire()
    sums.start(
        lambda s, n, step: dot(hid[rows_of(s), :first], wda[columns(n, step), :], 1, 1)
        + dot(hid[rows_of(s), first:], wdb[columns(n, step), :], 1, 1)
    )

    biases[...] = jnp.zeros_like(biases)

    @pl.loop(0, TP)
    def _(s):
        at = rows_of(s)
        grad_out = dot(cot[at, :], wo[...], 1, 0).astype(BF16)
        allowed = mask_of(aux_all[s][:, ROT : ROT + 1], row_all[s, 0:1, :], size)
        tables = tables_of(aux_all[s], wide)
        three = attend_back_values(
            qkv[at, :wide], qkv[at, wide : 2 * wide], qkv[at, 2 * wide :], grad_out, allowed, tables
        )
        for k, value in enumerate(three):
            lanes = slice(k * wide, (k + 1) * wide)
            qkv[at, lanes] = value
            biases[0:1, lanes] += jnp.sum(value.astype(F32), axis=0, keepdims=True)

    bias_all[p.u] = biases[...]

    def bias_copy(k):
        u = (p.u + k) % p.lines
        return remote(biases, bias_all.at[p.u], bias_sem.at[k], bias_sem.at[p.lines + k], u * TP + p.j, p.t)

    for k in range(1, p.lines):
        bias_copy(k).start()

    load_h1.wait()
    weight_grad(hh, qkv[...], gq)
    scatter_q.start_outer()
    weight_grad(cot, att[...], go)
    scatter_o.start_outer()
    scatter_q.start_rest()
    scatter_o.start_rest()
    scatter_db.combine()
    scatter_gb.combine()

    sums.arrive()

    @pl.loop(0, half // 32)
    def _(i):
        at = pl.multiple_of(i * 32, 32)
        resid[pl.ds(at, 32), :] += sums.total(at, 32)

    sums.release()
    mine = pl.ds(pl.multiple_of(p.t * half, half), half)

    def give(index, value, out):
        here = pltpu.make_async_copy(value, out.at[mine], swap_sem.at[index, 0])
        there = remote(value, out.at[mine], swap_sem.at[index, 1], swap_sem.at[index, 2], p.me, 1 - p.t)
        here.start()
        there.start()
        return here, there

    gives = [*give(1, resid, block_out)]

    sums.acquire()
    sums.start(lambda s, n, step: dot(qkv[rows_of(s), :], wq[columns(n, step), :], 1, 1))
    sums.arrive()

    @pl.loop(0, half // 32)
    def _(i):
        at = pl.multiple_of(i * 32, 32)
        values = tok_src[pl.ds(pl.multiple_of(p.t * half + at, 32), 32), :].astype(F32)
        scaled, inverse = norm_stats(values)
        part, gain, shift = norm_back(sums.total(at, 32), scaled, inverse, norms[0:1, :D])
        gains[0:1, :] += gain[None]
        gains[1:2, :] += shift[None]
        grad[pl.ds(at, 32), :] += part

    gives += give(0, grad, input_out)

    def tile_of(d):
        return pl.ds(pl.multiple_of(d * rows // 128 * 128, 128), 128)

    def gain_copy(dest):
        return remote(gains.at[:, tile_of(dest)], small_all.at[p.me], gain_sem.at[dest], gain_sem.at[count], dest, p.t)

    swap = remote(gains, gains_t, t_sem.at[0], t_sem.at[1], p.me, 1 - p.t)
    swap.start()
    swap.wait()
    gains[...] = gains[...] + gains_t[...]
    pltpu.make_async_copy(gains.at[:, tile_of(p.me)], small_all.at[p.me], gain_sem.at[count]).start()
    each_dest(p, lambda dest, u, j: gain_copy(dest).start())

    scatter_da.reduce()
    scatter_ga.reduce()
    scatter_db.reduce()
    scatter_gb.reduce()
    scatter_q.combine()
    scatter_o.combine()

    for k in range(1, p.lines):
        bias_copy(k).wait_recv()
    total = bias_all[0]
    for k in range(1, p.lines):
        total = total + bias_all[k]
    bias_out[p.j] = total

    def rank_copy(q):
        j = (p.j + q) % TP
        return remote(bias_out.at[p.j], bias_out.at[p.j], rank_sem.at[q], rank_sem.at[TP + q], p.u * TP + j, p.t)

    for q in range(1, TP):
        rank_copy(q).start()

    scatter_q.reduce()
    scatter_o.reduce()
    wait_bytes(small_all, gain_sem.at[count])
    total = small_all[0]
    for d in range(1, count):
        total = total + small_all[d]
    norm_out[...] = total
    for q in range(1, TP):
        rank_copy(q).wait()
    for k in range(1, p.lines):
        bias_copy(k).wait_send()
    each_dest(p, lambda dest, u, j: small_copy(dest).wait_send())
    each_dest(p, lambda dest, u, j: gain_copy(dest).wait_send())
    for copy in gives:
        copy.wait()
    for part in (auxes, rowses, sums, spread_r, gather_q, gather_o, gather_da, gather_db):
        part.finish()
    for scatter in scatters:
        scatter.finish()


def layer(count, small, aux, row, tokens, cot, *weights):
    size = tokens.shape[0]
    half = size // 2
    group = TP * size
    lines, rows = count // TP, weights[0].shape[1]
    _, wide, gates_a, hid_a, gates_b, hid_b = [w.shape[2] for w in weights]
    pad = hid_a + hid_b
    any_spec = pl.BlockSpec(memory_space=pl.ANY)
    vmem = pl.BlockSpec(memory_space=pltpu.VMEM)
    dma = pltpu.SemaphoreType.DMA
    regular = pltpu.SemaphoreType.REGULAR

    def out(*shape, dtype=BF16):
        return jax.ShapeDtypeStruct(shape, dtype)

    return pl.pallas_call(
        functools.partial(layer_kernel, count),
        in_specs=[vmem, vmem, vmem, vmem] + [any_spec] * 7,
        out_specs=[any_spec] * 9 + [vmem] * 2,
        out_shape=[
            *[out(TP, rows, w.shape[2]) for w in weights],
            out(size, D, dtype=F32),
            out(size, D, dtype=F32),
            out(group, D),
            out(8, 128, dtype=F32),
            out(TP, 8, 3 * wide, dtype=F32),
        ],
        scratch_shapes=[
            *[pltpu.VMEM((D, w.shape[2]), BF16) for w in weights],
            pltpu.VMEM((group, D), BF16),
            pltpu.VMEM((group, D), BF16),
            pltpu.VMEM((group, 3 * wide), BF16),
            pltpu.VMEM((group, wide), BF16),
            pltpu.VMEM((group, pad), BF16),
            pltpu.VMEM((max(2 * group, D), max(pad, 3 * wide)), BF16),
            pltpu.VMEM((group, gates_a), BF16),
            pltpu.VMEM((group, gates_b), BF16),
            pltpu.VMEM((D, hid_a), BF16),
            pltpu.VMEM((D, gates_a), BF16),
            pltpu.VMEM((D, hid_b), BF16),
            pltpu.VMEM((D, gates_b), BF16),
            pltpu.VMEM((D, wide), BF16),
            pltpu.VMEM((D, gates_a), BF16),
            pltpu.VMEM((D, hid_a), BF16),
            pltpu.VMEM((D, hid_b), BF16),
            pltpu.VMEM((D, wide), BF16),
            pltpu.VMEM((2, size, D), BF16),
            pltpu.VMEM((2, size, D), BF16),
            pltpu.VMEM((2, size, D), BF16),
            pltpu.VMEM((half, D), F32),
            pltpu.VMEM((3, half, D), BF16),
            pltpu.VMEM((half, D), F32),
            pltpu.VMEM((half, D), F32),
            pltpu.VMEM((8, D), F32),
            pltpu.VMEM((8, 3 * wide), F32),
            pltpu.VMEM((16, max(D, 128 * (small.shape[0] - 16))), F32),
            pltpu.VMEM((count,) + small.shape, BF16),
            pltpu.VMEM((TP, size, 128), F32),
            pltpu.VMEM((TP, 8, size), F32),
            pltpu.VMEM((count, 8, 128), F32),
            pltpu.VMEM((lines, 8, 3 * wide), F32),
            pltpu.VMEM((8, D), F32),
            dma((6, TP + lines)),
            dma((6, 4)),
            dma((count + 1,)),
            dma((2, 4)),
            dma((2, 4)),
            dma((2, 4)),
            dma((2, 4)),
            dma((2,)),
            dma((6, TP + lines)),
            dma((6, 4)),
            regular((lines,)),
            regular((lines,)),
            dma((2, 2)),
            dma((2, 4)),
            regular((4,)),
            dma((2, 4)),
            dma((2, 4)),
            dma((2, 4)),
            dma((2, 4)),
            dma((2, 3)),
            dma((count + 1,)),
            dma((2 * lines,)),
            dma((2 * TP,)),
            dma((2,)),
        ],
        compiler_params=pltpu.CompilerParams(
            collective_id=0, has_side_effects=True, vmem_limit_bytes=63 * 1024 * 1024
        ),
        cost_estimate=pl.CostEstimate(flops=40 * 10**9, bytes_accessed=60 * 10**6, transcendentals=10**7),
        name="layer",
    )(small, aux, row, tokens, cot, *weights)


def laid_out(values):
    return with_layout_constraint(values, Layout(tuple(range(values.ndim))))


def per_device(
    count,
    tokens_in,
    segment_ids,
    d_out,
    qkv_weight,
    qkv_bias,
    out_weight,
    gating_weight,
    down_weight,
    norm_params,
    qkv_first,
    qkv_second,
    bias_first,
    bias_second,
    out_first,
    out_second,
    gating_first,
    gating_second,
    down_first,
    down_second,
    norm_first,
    norm_second,
):
    place = lax.axis_index("dp")
    rows = norm_params.shape[1]
    seq_len = tokens_in.shape[1]
    head_local = qkv_weight.shape[2]
    hidden_local = gating_weight.shape[2]
    wide = head_local // TP
    hid = hidden_local // TP
    full = hid // 128 * 128

    low_gates = laid_out(gating_weight.astype(BF16))
    first = -(-(full // 2) // 128) * 128
    spare = hid - full

    def gate_cut(k, start, width):
        return [low_gates[:, k, j * width + start : (j + 1) * width + start] for j in range(TP)]

    def ranks(parts):
        return jnp.stack([jnp.concatenate(one, axis=1) for one in zip(*parts, strict=True)])

    low_down = down_weight.astype(BF16)
    down_full = low_down[: TP * full].reshape(TP, full, rows)
    gate_full = [[low_gates[:, k, j * full : (j + 1) * full] for j in range(TP)] for k in range(2)]
    weights = (
        ranks([[qkv_weight[:, k, j * wide : (j + 1) * wide] for j in range(TP)] for k in range(3)]).astype(BF16),
        out_weight.astype(BF16).reshape(TP, wide, rows).transpose(0, 2, 1),
        ranks([[part[:, :first] for part in gate_full[k]] for k in range(2)]),
        down_full[:, :first].transpose(0, 2, 1),
        ranks([[part[:, first:] for part in gate_full[k]] for k in range(2)] + [gate_cut(k, TP * full, spare) for k in range(2)]),
        jnp.concatenate(
            [
                down_full[:, first:],
                low_down[TP * full :].reshape(TP, spare, rows),
                jnp.zeros((TP, -hid % 128, rows), BF16),
            ],
            axis=1,
        ).transpose(0, 2, 1),
    )
    bias_here = qkv_bias.shape[1]
    small_norm = lax.dynamic_update_slice(jnp.zeros((16, 128), F32), norm_params, (0, (place * rows) % 128))
    small_bias = lax.dynamic_update_slice(jnp.zeros((3 * head_local,), F32), qkv_bias[0], (place * bias_here,))
    small = jnp.concatenate([small_norm, small_bias.reshape(-1, 128)]).astype(BF16)
    segments = segment_ids[0]
    earlier = jnp.sum((segments[None, :] < segments[:, None]).astype(jnp.int32), axis=1)
    positions = (jnp.arange(seq_len, dtype=jnp.int32) - earlier).astype(F32)
    frequency = 10000.0 ** (-2.0 * jnp.arange(ROT // 2, dtype=F32) / ROT)
    angles = positions[:, None] * frequency[None, :]
    aux = jnp.concatenate([jnp.cos(angles), jnp.sin(angles), segments[:, None].astype(F32)], axis=1)
    aux = jnp.pad(aux, ((0, 0), (0, 128 - aux.shape[1])))
    row = jnp.broadcast_to(segments.astype(F32)[None], (8, seq_len))

    rs_q, rs_o, rs_ga, rs_da, rs_gb, rs_db, block_out, input_grad, _, norm_sum, bias_sum = layer(
        count, small, aux, row, tokens_in[0], d_out[0], *weights
    )

    second = full - first
    gate_parts = [
        jnp.concatenate(
            [
                part
                for j in range(TP)
                for part in (
                    rs_ga[j, :, k * first : (k + 1) * first],
                    rs_gb[j, :, k * second : (k + 1) * second],
                )
            ]
            + [rs_gb[j, :, 2 * second + k * spare : 2 * second + (k + 1) * spare] for j in range(TP)],
            axis=1,
        )
        for k in range(2)
    ]
    gating_shard = lax.optimization_barrier(laid_out(jnp.stack(gate_parts, axis=1))).astype(F32)
    qkv_shard = jnp.stack(
        [
            jnp.concatenate([rs_q[j, :, k * wide : (k + 1) * wide] for j in range(TP)], axis=1)
            for k in range(3)
        ],
        axis=1,
    ).astype(F32)
    out_shard = laid_out(rs_o.transpose(0, 2, 1).reshape(head_local, rows)).astype(F32)
    down_parts = jnp.concatenate([rs_da, rs_db], axis=2).transpose(0, 2, 1)
    down_shard = laid_out(
        jnp.concatenate(
            [down_parts[:, :full].reshape(TP * full, rows), down_parts[:, full:hid].reshape(TP * spare, rows)]
        )
    ).astype(F32)
    norm_grad = lax.dynamic_slice_in_dim(norm_sum[:4], (place * rows) % 128, rows, 1)
    bias_grad = bias_sum[:, 0].reshape(TP, 3, wide).transpose(1, 0, 2).reshape(1, 3 * head_local)
    bias_grad = lax.dynamic_slice_in_dim(bias_grad, place * bias_here, bias_here, 1)
    return (
        block_out[None],
        input_grad[None],
        *adamw_update(qkv_weight, qkv_shard, qkv_first, qkv_second, D ** (-0.5), 0.1),
        *adamw_update(qkv_bias, bias_grad, bias_first, bias_second, 0.3, 0.0),
        *adamw_update(out_weight, out_shard, out_first, out_second, (H * HD // 16) ** (-0.5), 0.1),
        *adamw_update(gating_weight, gating_shard, gating_first, gating_second, D ** (-0.5), 0.1),
        *adamw_update(down_weight, down_shard, down_first, down_second, FF ** (-0.5), 0.1),
        *adamw_update(norm_params, norm_grad, norm_first, norm_second, 0.25, 0.0),
    )


def solution(mesh):
    tokens = P("dp", None, None)
    qkv = P("dp", None, "tensor")
    rest = P("tensor", "dp")
    norm = P(None, "dp")
    weights = (qkv, rest, rest, qkv, rest, norm)
    states = (qkv, qkv, rest, rest, rest, rest, qkv, qkv, rest, rest, norm, norm)
    return jax.shard_map(
        functools.partial(per_device, mesh.shape["dp"]),
        mesh=mesh,
        in_specs=(tokens, P("dp", None), tokens, *weights, *states),
        out_specs=(tokens, tokens, *(spec for spec in weights for _ in range(3))),
        check_vma=False,
    )
```

```python
import functools

import jax
import jax.numpy as jnp
from jax import lax
from jax.experimental import pallas as pl
from jax.experimental.layout import Layout, with_layout_constraint
from jax.experimental.pallas import tpu as pltpu
from jax.sharding import PartitionSpec as P

D = 2048
H = 32
HD = 64
ROT = 16
FF = 5632
STEP = 10
TP = 4

F32 = jnp.float32
BF16 = jnp.bfloat16


def layer_norm(values, scale_row, shift_row):
    centre = values - jnp.mean(values, axis=-1, keepdims=True)
    spread = jnp.mean(centre * centre, axis=-1, keepdims=True)
    inverse = lax.rsqrt(spread + 1e-05)
    scaled = centre * inverse
    return (scaled * scale_row + shift_row, scaled, inverse)


def norm_back(grad_in, scaled, inverse, scale_row):
    grad_scaled = grad_in * scale_row
    mean_first = jnp.mean(grad_scaled, axis=-1, keepdims=True)
    mean_second = jnp.mean(grad_scaled * scaled, axis=-1, keepdims=True)
    grad_values = inverse * (grad_scaled - mean_first - scaled * mean_second)
    return (grad_values, jnp.sum(grad_in * scaled, axis=0), jnp.sum(grad_in, axis=0))


def adamw_update(weight_old, gradient, first_old, second_old, step_rate, decay_rate):
    first_new = 0.9 * first_old + 0.1 * gradient
    second_new = 0.95 * second_old + 0.05 * gradient * gradient
    corrected = first_new / (1.0 - 0.9**STEP) / (jnp.sqrt(second_new / (1.0 - 0.95**STEP)) + 1e-08)
    return (weight_old - step_rate * (corrected + decay_rate * weight_old), first_new, second_new)


def dot(a, b, ca, cb):
    return lax.dot_general(a, b, (((ca,), (cb,)), ((), ())), preferred_element_type=F32)


def spin(values, cos_t, lower_t, upper_t):
    wide = values.shape[1]
    return (
        values * cos_t
        + pltpu.roll(values, wide - ROT // 2, 1) * lower_t
        + pltpu.roll(values, ROT // 2, 1) * upper_t
    )


def spin_back(values, cos_t, lower_t, upper_t):
    wide = values.shape[1]
    return (
        values * cos_t
        + pltpu.roll(values * lower_t, ROT // 2, 1)
        + pltpu.roll(values * upper_t, wide - ROT // 2, 1)
    )


def mask_of(seg_col, seg_row, size):
    rows = lax.broadcasted_iota(jnp.int32, (size, size), 0)
    cols = lax.broadcasted_iota(jnp.int32, (size, size), 1)
    return (seg_col == seg_row) & (cols <= rows)


def attend_back_values(query, key, value, grad, allowed, tables):
    head_of = lax.broadcasted_iota(jnp.int32, query.shape, 1) // HD
    zero = jnp.zeros_like(query)
    dq = jnp.zeros(query.shape, F32)
    dk = jnp.zeros(query.shape, F32)
    dv = jnp.zeros(query.shape, F32)
    for head in range(query.shape[1] // HD):
        mine = head_of == head
        query_h = jnp.where(mine, query, zero)
        grad_h = jnp.where(mine, grad, zero)
        scores = dot(query_h, key, 1, 1) * HD ** (-0.5)
        scores = jnp.where(allowed, scores, -1e30)
        weights = jnp.exp(scores - jnp.max(scores, axis=1, keepdims=True))
        prob = weights / jnp.sum(weights, axis=1, keepdims=True)
        dv = dv + dot(prob.astype(BF16), grad_h, 0, 0)
        dprob = dot(grad_h, value, 1, 1)
        delta = jnp.sum(prob * dprob, axis=1, keepdims=True)
        dscore = (prob * (dprob - delta)).astype(BF16)
        dq = jnp.where(mine, dot(dscore, key, 1, 0), dq)
        dk = dk + dot(dscore, query_h, 0, 0)
    dq = spin_back(dq * HD ** (-0.5), *tables).astype(BF16)
    dk = spin_back(dk * HD ** (-0.5), *tables).astype(BF16)
    return dq, dk, dv.astype(BF16)


class Place:
    def __init__(self, count):
        self.count = count
        self.lines = count // TP
        self.me = lax.axis_index("dp")
        self.t = lax.axis_index("tensor")
        self.u = self.me // TP
        self.j = self.me % TP
        self.x = self.j // 2
        self.c = self.j % 2
        self.core_peer = self.me + 1 - 2 * self.c
        self.x_peer = self.me + 2 - 4 * self.x

    def group(self, k):
        x = (self.x + k // 2) % 2
        return self.u * TP + x * 2 + self.c, (self.t + k % 2) % 2, x


def remote(src, dst, send_sem, recv_sem, dp, t):
    return pltpu.make_async_remote_copy(
        src_ref=src,
        dst_ref=dst,
        send_sem=send_sem,
        recv_sem=recv_sem,
        device_id=(dp, t),
        device_id_type=pl.DeviceIdType.MESH,
    )


def wait_bytes(ref, sem):
    pltpu.make_async_copy(ref, ref, sem).wait()


def greet(place):
    barrier = pltpu.get_barrier_semaphore()

    @pl.loop(1, place.count)
    def _(k):
        pl.semaphore_signal(
            barrier,
            inc=1,
            device_id=((place.me + k) % place.count, place.t),
            device_id_type=pl.DeviceIdType.MESH,
        )

    for k in (1, 3):
        dp, t, _ = place.group(k)
        pl.semaphore_signal(barrier, inc=1, device_id=(dp, t), device_id_type=pl.DeviceIdType.MESH)
    pl.semaphore_wait(barrier, place.count + 1)


def each_dest(place, act):
    if place.lines == 4:

        @pl.loop(1, TP)
        def _(q):
            j = (place.j + q) % TP
            act(place.u * TP + j, place.u, j)

        @pl.loop(0, TP)
        def _(q):
            j = (place.j + q) % TP
            for dz in (2, 1, 3):
                u = (place.u + dz) % 4
                act(u * TP + j, u, j)

    else:

        @pl.loop(1, place.count)
        def _(k):
            dest = (place.me + k) % place.count
            act(dest, dest // TP, dest % TP)


class WeightGather:
    def __init__(self, place, index, src, dst, send_sem, recv_sem):
        self.place, self.src, self.dst = place, src, dst
        self.send_sem, self.recv_sem = send_sem.at[index], recv_sem.at[index]
        self.rows = src.shape[1]

    def group_copy(self, q):
        p = self.place
        j = (p.j + q) % TP
        mine = self.dst.at[pl.ds(p.me * self.rows, self.rows)]
        return remote(self.src.at[j], mine, self.send_sem.at[q], self.recv_sem.at[2], p.u * TP + j, p.t)

    def chunk(self, u):
        size = TP * self.rows
        return self.dst.at[pl.ds(u * size, size)]

    def line_copy(self, k):
        p = self.place
        u = (p.u + k) % p.lines
        sem = 0
        if p.lines == 4:
            sem = jnp.where(self.middle(), jnp.where(p.u + u == 3, 3, 0), jnp.where(jnp.abs(p.u - u) == 2, 1, 0))
        mine = self.chunk(p.u)
        return remote(mine, mine, self.send_sem.at[TP + k], self.recv_sem.at[sem], u * TP + p.j, p.t)

    def line_each(self, act):
        p = self.place
        if p.lines == 4:
            for k in (2, 1, 3):
                gap = jnp.abs(p.u - (p.u + k) % 4)
                pl.when((gap == 1) | ((gap == 2) & ~self.middle()))(lambda k=k: act(k))
        else:
            for k in range(1, p.lines):
                act(k)

    def start(self):
        p = self.place
        for q in (2, 3, 1):
            self.group_copy(q).start()
        mine = self.dst.at[pl.ds(p.me * self.rows, self.rows)]
        pltpu.make_async_copy(self.src.at[p.j], mine, self.recv_sem.at[2]).start()

    def pass_on(self):
        wait_bytes(self.chunk(0), self.recv_sem.at[2])
        self.line_each(lambda k: self.line_copy(k).start())

    def middle(self):
        return (self.place.u == 1) | (self.place.u == 2)

    def forward(self, which):
        p = self.place
        up = p.u == 2
        chunk = self.chunk(jnp.where(up, which, 3 - which))
        sem = self.send_sem.at[TP + 2 * which]
        return remote(chunk, chunk, sem, self.recv_sem.at[1], p.me + jnp.where(up, TP, -TP), p.t)

    def relay(self):
        if self.place.lines == 4:

            @pl.when(self.middle())
            def _():
                wait_bytes(self.chunk(0), self.recv_sem.at[3])
                self.forward(1).start()
                wait_bytes(self.chunk(0), self.recv_sem.at[1])
                self.forward(0).start()

    def arrive(self):
        p = self.place
        size = TP * self.rows
        if p.lines == 4:
            wait_bytes(self.chunk(0), self.recv_sem.at[0])
            pl.when(~self.middle())(lambda: wait_bytes(self.dst.at[pl.ds(0, 2 * size)], self.recv_sem.at[1]))
        else:
            wait_bytes(self.dst.at[pl.ds(0, size * (p.lines - 1))], self.recv_sem.at[0])

    def finish(self):
        for q in range(1, TP):
            self.group_copy(q).wait_send()
        self.line_each(lambda k: self.line_copy(k).wait_send())
        if self.place.lines == 4:

            @pl.when(self.middle())
            def _():
                self.forward(1).wait_send()
                self.forward(0).wait_send()


class GroupSum:
    def __init__(self, place, to_core, from_core, low, own, parts, core_sem, part_sem, free_sem=None):
        self.place = place
        self.to_core, self.from_core, self.low, self.own, self.parts = to_core, from_core, low, own, parts
        self.core_sem, self.part_sem, self.free_sem = core_sem, part_sem, free_sem

    def core_copy(self, i):
        p = self.place
        return remote(
            self.to_core.at[i], self.from_core.at[i], self.core_sem.at[0, i], self.core_sem.at[1, i], p.core_peer, p.t
        )

    def part_copy(self, k):
        p = self.place
        half = self.parts.shape[1]
        dp, t, _ = p.group(k)
        block = self.low.at[0 if k >= 2 else 1, pl.ds(pl.multiple_of(t * half, half), half)]
        return remote(block, self.parts.at[k - 1], self.part_sem.at[0, k], self.part_sem.at[1, k], dp, t)

    def start(self, product):
        p = self.place
        step = min(512, D)
        other = [(p.x + 1) % 2, p.x]
        for i in range(2):

            @pl.loop(0, D // step)
            def _(n):
                at = pl.ds(pl.multiple_of(n * step, step), step)
                self.to_core[i, :, at] = product(other[i] * 2 + 1 - p.c, n, step).astype(BF16)

            self.core_copy(i).start()
        for i in range(2):
            self.core_copy(i).wait_recv()

            @pl.loop(0, D // step)
            def _(n):
                at = pl.ds(pl.multiple_of(n * step, step), step)
                total = product(other[i] * 2 + p.c, n, step) + self.from_core[i, :, at].astype(F32)
                self.low[i, :, at] = total.astype(BF16)
                if i == 1:
                    half = self.own.shape[0]

                    @pl.when(p.t == 0)
                    def _():
                        self.own[:, at] = total[:half]

                    @pl.when(p.t == 1)
                    def _():
                        self.own[:, at] = total[half:]

            for k in (3, 2) if i == 0 else (1,):
                self.part_copy(k).start()

    def arrive(self):
        for k in (3, 2, 1):
            self.part_copy(k).wait_recv()

    def total(self, at, rows):
        value = self.own[pl.ds(pl.multiple_of(at, 32), rows), :]
        for k in range(3):
            value = value + self.parts[k, pl.ds(pl.multiple_of(at, 32), rows), :].astype(F32)
        return value

    def finish(self):
        for i in range(2):
            self.core_copy(i).wait_send()
        for k in (1, 2, 3):
            self.part_copy(k).wait_send()

    def release(self):
        p = self.place
        pl.semaphore_signal(
            self.free_sem.at[0], inc=1, device_id=(p.core_peer, p.t), device_id_type=pl.DeviceIdType.MESH
        )
        for k in (1, 2, 3):
            dp, t, _ = p.group(k)
            pl.semaphore_signal(
                self.free_sem.at[k], inc=1, device_id=(dp, t), device_id_type=pl.DeviceIdType.MESH
            )

    def acquire(self):
        self.finish()
        for k in range(4):
            pl.semaphore_wait(self.free_sem.at[k], 1)


class GroupGather:
    def __init__(self, place, out, size, part_sem, core_sem):
        self.place, self.out, self.half = place, out, size // 2
        self.part_sem, self.core_sem = part_sem, core_sem

    def block(self, x, t):
        p = self.place
        start = ((x * 2 + p.c) * 2 + t) * self.half
        return self.out.at[pl.ds(pl.multiple_of(start, self.half), self.half)]

    def part_copy(self, k):
        p = self.place
        dp, t, _ = p.group(k)
        mine = self.block(p.x, p.t)
        return remote(mine, mine, self.part_sem.at[0, k], self.part_sem.at[1, k], dp, t)

    def core_copy(self, k):
        p = self.place
        _, t, x = p.group(k)
        block = self.block(x, t)
        return remote(block, block, self.core_sem.at[0, k], self.core_sem.at[1, k], p.core_peer, p.t)

    def start(self):
        for k in (3, 2, 1):
            self.part_copy(k).start()
        self.core_copy(0).start()

    def arrive(self):
        for k in (1, 2, 3):
            self.part_copy(k).wait_recv()
            self.core_copy(k).start()
        for k in range(4):
            self.core_copy(k).wait_recv()

    def finish(self):
        for k in (1, 2, 3):
            self.part_copy(k).wait_send()
        for k in range(4):
            self.core_copy(k).wait_send()


class GroupPieces:
    def __init__(self, place, src, out, sem, size=0):
        self.place, self.src, self.out, self.sem, self.size = place, src, out, sem, size

    def at(self, j):
        if self.size:
            return self.out.at[pl.ds(pl.multiple_of(j * self.size, self.size), self.size)]
        return self.out.at[j]

    def own(self):
        return pltpu.make_async_copy(self.src, self.at(self.place.j), self.sem.at[0, 0])

    def near(self, k):
        p = self.place
        dest = p.core_peer if k == 1 else p.x_peer
        return remote(self.src, self.at(p.j), self.sem.at[0, k], self.sem.at[1, k], dest, p.t)

    def relay(self):
        p = self.place
        block = self.at((p.j + 2) % TP)
        return remote(block, block, self.sem.at[0, 3], self.sem.at[1, 3], p.core_peer, p.t)

    def start(self):
        self.near(2).start()
        self.near(1).start()
        self.own().start()

    def pass_on(self):
        self.near(2).wait_recv()
        self.relay().start()

    def arrive(self):
        self.near(1).wait_recv()
        self.relay().wait_recv()
        self.own().wait()

    def finish(self):
        self.near(1).wait_send()
        self.near(2).wait_send()
        self.relay().wait_send()


def tables_of(aux, wide):
    half = ROT // 2
    line = lax.broadcasted_iota(jnp.int32, (aux.shape[1], wide), 0)
    lane = lax.broadcasted_iota(jnp.int32, (aux.shape[1], wide), 1) % HD
    first = lane < half
    second = (lane >= half) & (lane < ROT)

    def spread(pick, sign):
        table = jnp.where(pick, sign, 0.0).astype(F32)
        return lax.dot_general(
            aux, table, (((1,), (0,)), ((), ())), precision=lax.Precision.HIGHEST, preferred_element_type=F32
        )

    rest = lax.broadcasted_iota(jnp.int32, (aux.shape[0], wide), 1) % HD >= ROT
    cos_t = spread((line == lane % half) & (first | second), 1.0) + jnp.where(rest, 1.0, 0.0)
    low_t = spread((line == lane + half) & first, -1.0)
    upp_t = spread((line == lane) & second, 1.0)
    return cos_t, low_t, upp_t


def attend_values(query, key, value, allowed):
    head_of = lax.broadcasted_iota(jnp.int32, query.shape, 1) // HD
    total = jnp.zeros(query.shape, F32)
    for head in range(query.shape[1] // HD):
        mine = head_of == head
        scores = dot(jnp.where(mine, query, jnp.zeros_like(query)), key, 1, 1) * HD ** (-0.5)
        scores = jnp.where(allowed, scores, -1e30)
        weights = jnp.exp(scores - jnp.max(scores, axis=1, keepdims=True))
        prob = weights / jnp.sum(weights, axis=1, keepdims=True)
        total = jnp.where(mine, dot(prob.astype(BF16), value, 1, 0), total)
    return total


class GradScatter:
    def __init__(self, place, index, grad, slots, out, send_sem, recv_sem, free_sem=None):
        self.place, self.grad, self.slots, self.out = place, grad, slots, out
        self.send_sem, self.recv_sem, self.free_sem = send_sem.at[index], recv_sem.at[index], free_sem
        self.rows = out.shape[1]
        self.size = TP * self.rows

    def chunk(self, ref, u):
        return ref.at[pl.ds(u * self.size, self.size)]

    def near(self, u):
        return jnp.abs(self.place.u - u) < 3 if self.place.lines == 4 else None

    def line_each(self, act, picked=lambda u: True):
        p = self.place
        for k in (2, 1, 3) if p.lines == 4 else range(1, p.lines):
            u = (p.u + k) % p.lines
            if p.lines == 4:
                pl.when(self.near(u) & picked(u))(lambda k=k, u=u: act(k, u))
            else:
                act(k, u)

    def line_copy(self, k, u):
        p = self.place
        far = 0
        if p.lines == 4:
            far = (((p.u == 0) & (u == 2)) | ((p.u == 3) & (u == 1))).astype(jnp.int32)
        return remote(
            self.chunk(self.grad, u), self.chunk(self.slots, p.u), self.send_sem.at[TP + k], self.recv_sem.at[far],
            u * TP + p.j, p.t,
        )

    def outer(self):
        p = self.place
        first = p.u == 0
        src, dst = self.chunk(self.grad, jnp.where(first, 3, 0)), self.chunk(self.slots, jnp.where(first, 1, 2))
        return remote(src, dst, self.send_sem.at[TP], self.recv_sem.at[2], p.me + jnp.where(first, TP, -TP), p.t)

    def ends(self):
        return (self.place.u == 0) | (self.place.u == 3)

    def later(self, u):
        p = self.place
        return ((p.u == 1) & (u == 3)) | ((p.u == 2) & (u == 0))

    def allow(self):
        p = self.place
        self.line_each(
            lambda k, u: pl.semaphore_signal(
                self.free_sem.at[p.u], inc=1, device_id=(u * TP + p.j, p.t), device_id_type=pl.DeviceIdType.MESH
            )
        )

    def start(self):
        self.start_outer()
        self.start_rest()

    def start_outer(self):
        if self.free_sem is not None:
            self.line_each(lambda k, u: pl.semaphore_wait(self.free_sem.at[u], 1))
        if self.place.lines == 4:
            pl.when(self.ends())(lambda: self.outer().start())

    def start_rest(self):
        if self.place.lines == 4:
            self.line_each(lambda k, u: self.line_copy(k, u).start(), lambda u: ~self.later(u))
        else:
            self.line_each(lambda k, u: self.line_copy(k, u).start())

    def add(self, u, sources):
        p = self.place

        @pl.loop(0, self.size // 32)
        def _(i):
            at = pl.ds(pl.multiple_of(u * self.size + i * 32, 32), 32)
            total = self.grad[at, :].astype(F32)
            for slot in sources:
                here = pl.ds(pl.multiple_of(slot * self.size + i * 32, 32), 32)
                total = total + self.slots[here, :].astype(F32)
            self.grad[at, :] = total.astype(BF16)

    def combine(self):
        p = self.place
        if p.lines != 4:
            return

        @pl.when(~self.ends())
        def _():
            wait_bytes(self.chunk(self.slots, 0), self.recv_sem.at[2])
            self.add(jnp.where(p.u == 1, 3, 0), [p.u])
            self.line_each(lambda k, u: self.line_copy(k, u).start(), self.later)

    def group_copy(self, q):
        p = self.place
        j = (p.j + q) % TP
        block = self.grad.at[pl.ds((p.u * TP + j) * self.rows, self.rows)]
        return remote(block, self.out.at[p.j], self.send_sem.at[q], self.recv_sem.at[3], p.u * TP + j, p.t)

    def reduce(self):
        p = self.place
        if p.lines == 4:
            wait_bytes(self.slots.at[pl.ds(0, 2 * self.size)], self.recv_sem.at[0])
            pl.when(~self.ends())(lambda: wait_bytes(self.chunk(self.slots, 0), self.recv_sem.at[1]))
            pl.when(self.ends())(lambda: self.add(p.u, [1, 2]))
            pl.when(p.u == 1)(lambda: self.add(p.u, [0, 2, 3]))
            pl.when(p.u == 2)(lambda: self.add(p.u, [0, 1, 3]))
        else:
            wait_bytes(self.slots.at[pl.ds(0, (p.lines - 1) * self.size)], self.recv_sem.at[0])
            for k in range(1, p.lines):
                self.add(p.u, [(p.u + k) % p.lines])
        for q in (2, 3, 1):
            self.group_copy(q).start()
        own = self.grad.at[pl.ds(p.me * self.rows, self.rows)]
        pltpu.make_async_copy(own, self.out.at[p.j], self.recv_sem.at[3]).start()

    def finish(self):
        wait_bytes(self.out, self.recv_sem.at[3])
        for q in range(1, TP):
            self.group_copy(q).wait_send()
        self.line_each(lambda k, u: self.line_copy(k, u).wait_send())
        if self.place.lines == 4:
            pl.when(self.ends())(lambda: self.outer().wait_send())


def norm_stats(values):
    centre = values - jnp.mean(values, axis=-1, keepdims=True)
    inverse = lax.rsqrt(jnp.mean(centre * centre, axis=-1, keepdims=True) + 1e-05)
    return centre * inverse, inverse


def layer_kernel(
    count,
    small_src, aux_src, row_src, tok_src, cot_src, wq_src, wo_src, wga_src, wda_src, wgb_src, wdb_src,
    rs_q, rs_o, rs_ga, rs_da, rs_gb, rs_db, block_out, input_out, h1_out, norm_out, bias_out,
    wq, wo, wga, wda, wgb, wdb, cot, hh, qkv, att, hid, slopes, dga, dgb, gda, gga, gdb, ggb, go,
    slots_ga, slots_da, slots_db, slots_o,
    to_core, from_core, low, own, parts, grad, resid, gains, biases, norms,
    small, aux_all, row_all, small_all, bias_all, gains_t,
    w_send, w_recv, small_sem, aux_sem, row_sem, tok_sem, cot_sem, h1_sem,
    rs_send, rs_recv, free_g, free_q, core_sem, part_sem, free_sem, part2_sem, core2_sem, part3_sem, core3_sem,
    swap_sem, gain_sem, bias_sem, rank_sem, t_sem,
):
    p = Place(count)
    size = tok_src.shape[0]
    half = size // 2
    group = TP * size
    wide = att.shape[1]
    rows = wq_src.shape[1]
    first = wda.shape[1]
    second = hid.shape[1] - 128 - first
    greet(p)

    def rows_of(s):
        return pl.ds(pl.multiple_of(s * size, size), size)

    def columns(n, step):
        return pl.ds(pl.multiple_of(n * step, step), step)

    gathers = [
        WeightGather(p, i, src, dst, w_send, w_recv)
        for i, (src, dst) in enumerate(
            ((wq_src, wq), (wo_src, wo), (wga_src, wga), (wda_src, wda), (wgb_src, wgb), (wdb_src, wdb))
        )
    ]
    gather_q, gather_o, gather_ga, gather_da, gather_gb, gather_db = gathers
    tok = cot
    auxes = GroupPieces(p, aux_src, aux_all, aux_sem)
    rowses = GroupPieces(p, row_src, row_all, row_sem)
    tokens = GroupPieces(p, tok_src, tok, tok_sem, size)
    cots = GroupPieces(p, cot_src, cot, cot_sem, size)
    sums = GroupSum(p, to_core, from_core, low, own, parts, core_sem, part_sem, free_sem)
    spread_h = GroupGather(p, hh, size, part2_sem, core2_sem)
    spread_r = GroupGather(p, cot, size, part3_sem, core3_sem)
    gq = slopes.at[:D, : 3 * wide]
    scatters = [
        GradScatter(p, i, g, slots, out, rs_send, rs_recv, free)
        for i, (g, slots, out, free) in enumerate(
            (
                (gq, wga.at[:, : 3 * wide], rs_q, free_q),
                (go, slots_o, rs_o, None),
                (gga, slots_ga, rs_ga, None),
                (gda, slots_da, rs_da, None),
                (ggb, wgb, rs_gb, free_g),
                (gdb, slots_db, rs_db, None),
            )
        )
    ]
    scatter_q, scatter_o, scatter_ga, scatter_da, scatter_gb, scatter_db = scatters

    def small_copy(dest):
        return remote(small_src, small.at[p.me], small_sem.at[dest], small_sem.at[count], dest, p.t)

    pltpu.make_async_copy(small_src, small.at[p.me], small_sem.at[count]).start()
    each_dest(p, lambda dest, u, j: small_copy(dest).start())
    gather_q.start()
    auxes.start()
    rowses.start()
    gather_o.start()
    for part in gathers[2:4]:
        part.start()
    tokens.start()
    for part in gathers[4:]:
        part.start()
    for part in gathers[:4]:
        part.pass_on()
    auxes.pass_on()
    rowses.pass_on()
    tokens.pass_on()

    wait_bytes(small, small_sem.at[count])
    per_tile = 128 // rows
    for m in range(D // 128):
        tile = jnp.zeros((8, 128), F32)
        for i in range(per_tile):
            tile = tile + small[m * per_tile + i].astype(F32)[0:8]
        norms[0:8, m * 128 : (m + 1) * 128] = tile
    bias_rows = small.shape[1] - 16
    total = jnp.zeros((bias_rows, 128), F32)
    for d in range(count):
        total = total + small[d].astype(F32)[16:]
    for i in range(bias_rows):
        norms[8:9, i * 128 : (i + 1) * 128] = total[i : i + 1]
    auxes.arrive()
    rowses.arrive()
    gather_q.relay()
    tokens.arrive()

    @pl.loop(0, group // 32)
    def _(i):
        at = pl.ds(pl.multiple_of(i * 32, 32), 32)
        normed, _, _ = layer_norm(tok[at, :].astype(F32), norms[0:1, :D], norms[1:2, :D])
        hh[at, :] = normed.astype(BF16)

    tokens.finish()
    keep_h1 = pltpu.make_async_copy(hh, h1_out, h1_sem.at[0])
    keep_h1.start()
    gather_q.arrive()
    gather_gb.pass_on()
    gather_db.pass_on()
    gather_o.relay()
    head_wide = (bias_rows * 128) // 3

    @pl.loop(0, TP)
    def _(s):
        at = rows_of(s)
        proj = dot(hh[at, :], wq[...], 1, 0)
        tables = tables_of(aux_all[s], wide)

        def part(k):
            lanes = pl.ds(pl.multiple_of(k * head_wide + p.j * wide, 128), wide)
            return proj[:, k * wide : (k + 1) * wide] + norms[8:9, lanes]

        query = spin(part(0), *tables).astype(BF16)
        key = spin(part(1), *tables).astype(BF16)
        value = part(2).astype(BF16)
        qkv[at, :wide] = query
        qkv[at, wide : 2 * wide] = key
        qkv[at, 2 * wide :] = value
        allowed = mask_of(aux_all[s][:, ROT : ROT + 1], row_all[s, 0:1, :], size)
        att[at, :] = attend_values(query, key, value, allowed).astype(BF16)

    gather_o.arrive()
    keep_h1.wait()
    sums.start(lambda s, n, step: dot(att[rows_of(s), :], wo[columns(n, step), :], 1, 1))
    gather_ga.relay()
    sums.arrive()

    @pl.loop(0, half // 32)
    def _(i):
        at = pl.multiple_of(i * 32, 32)
        values = tok_src[pl.ds(pl.multiple_of(p.t * half + at, 32), 32), :].astype(F32)
        values = values + sums.total(at, 32)
        resid[pl.ds(at, 32), :] = values
        normed, _, _ = layer_norm(values, norms[2:3, :D], norms[3:4, :D])
        start = (p.j * 2 + p.t) * half + at
        hh[pl.ds(pl.multiple_of(start, 32), 32), :] = normed.astype(BF16)

    sums.release()
    spread_h.start()
    cots.start()
    spread_h.arrive()
    cots.pass_on()
    gather_da.relay()
    gather_gb.relay()
    gather_db.relay()
    step = min(256, D)

    def weight_grad(left, right, out):
        @pl.loop(0, D // step)
        def _(n):
            at = columns(n, step)
            out[at, :] = dot(left[:, at], right, 0, 0).astype(BF16)

    def late_rows(s):
        return pl.ds(pl.multiple_of(group + s * size, size), size)

    def hidden_part(weights, base, width, mixed):
        @pl.loop(0, TP)
        def _(s):
            at, late = rows_of(s), late_rows(s)
            rows_in = hh[at, :]
            lanes = slice(base, base + width)
            gate = dot(rows_in, weights[:, :width], 1, 0)
            up = dot(rows_in, weights[:, width : 2 * width], 1, 0)
            sig = jax.nn.sigmoid(gate)
            hid[at, lanes] = (gate * sig * up).astype(BF16)
            slopes[at, lanes] = (up * sig * (1.0 + gate * (1.0 - sig))).astype(BF16)
            slopes[late, lanes] = (gate * sig).astype(BF16)
            if mixed:
                gate = dot(rows_in, weights[:, 2 * width :], 1, 0)
                up = pltpu.roll(gate, 64, 1)
                sig = jax.nn.sigmoid(gate)
                left = lax.broadcasted_iota(jnp.int32, gate.shape, 1) < 64
                lanes = slice(base + width, base + width + 128)
                hid[at, lanes] = jnp.where(left, gate * sig * up, 0.0).astype(BF16)
                slopes[at, lanes] = jnp.where(left, up * sig * (1.0 + gate * (1.0 - sig)), 0.0).astype(BF16)
                slopes[late, lanes] = jnp.where(left, gate * sig, 0.0).astype(BF16)

    def gates_part(weights, base, width, mixed, out):
        @pl.loop(0, TP)
        def _(s):
            at, late = rows_of(s), late_rows(s)
            lanes = slice(base, base + weights.shape[1])
            dhid = dot(cot[at, :], weights[...], 1, 0)
            slope = dhid * slopes[at, lanes].astype(F32)
            gain = dhid * slopes[late, lanes].astype(F32)
            out[at, :width] = slope[:, :width].astype(BF16)
            out[at, width : 2 * width] = gain[:, :width].astype(BF16)
            if mixed:
                last = slope[:, width:] + pltpu.roll(gain[:, width:], 64, 1)
                out[at, 2 * width :] = last.astype(BF16)

    gather_ga.arrive()
    hidden_part(wga, 0, first, False)
    cots.arrive()
    weight_grad(cot, hid[:, :first], gda)
    scatter_da.start()
    gather_da.arrive()
    gates_part(wda, 0, first, False, dga)
    weight_grad(hh, dga[...], gga)
    scatter_ga.start()
    gather_gb.arrive()
    hidden_part(wgb, first, second, True)
    weight_grad(cot, hid[:, first:], gdb)
    scatter_db.start()
    gather_db.arrive()
    gates_part(wdb, first, second, True, dgb)

    cots.finish()
    sums.acquire()
    sums.start(
        lambda s, n, step: dot(dga[rows_of(s), :], wga[columns(n, step), :], 1, 1)
        + dot(dgb[rows_of(s), :], wgb[columns(n, step), :], 1, 1)
    )
    gather_gb.finish()
    gather_ga.finish()
    scatter_gb.allow()
    scatter_q.allow()
    weight_grad(hh, dgb[...], ggb)
    scatter_gb.start()
    spread_h.finish()
    load_h1 = pltpu.make_async_copy(h1_out, hh, h1_sem.at[1])
    load_h1.start()
    scatter_da.combine()
    scatter_ga.combine()
    sums.arrive()

    gains[...] = jnp.zeros_like(gains)

    @pl.loop(0, half // 32)
    def _(i):
        at = pl.multiple_of(i * 32, 32)
        scaled, inverse = norm_stats(resid[pl.ds(at, 32), :])
        part, gain, shift = norm_back(sums.total(at, 32), scaled, inverse, norms[2:3, :D])
        gains[2:3, :] += gain[None]
        gains[3:4, :] += shift[None]
        mine = pl.ds(pl.multiple_of((p.j * 2 + p.t) * half + at, 32), 32)
        total = cot[mine, :].astype(F32) + part
        grad[pl.ds(at, 32), :] = total
        cot[mine, :] = total.astype(BF16)

    sums.release()
    spread_r.start()
    spread_r.arrive()

    sums.acquire()
    sums.start(
        lambda s, n, step: dot(hid[rows_of(s), :first], wda[columns(n, step), :], 1, 1)
        + dot(hid[rows_of(s), first:], wdb[columns(n, step), :], 1, 1)
    )

    biases[...] = jnp.zeros_like(biases)

    @pl.loop(0, TP)
    def _(s):
        at = rows_of(s)
        grad_out = dot(cot[at, :], wo[...], 1, 0).astype(BF16)
        allowed = mask_of(aux_all[s][:, ROT : ROT + 1], row_all[s, 0:1, :], size)
        tables = tables_of(aux_all[s], wide)
        three = attend_back_values(
            qkv[at, :wide], qkv[at, wide : 2 * wide], qkv[at, 2 * wide :], grad_out, allowed, tables
        )
        for k, value in enumerate(three):
            lanes = slice(k * wide, (k + 1) * wide)
            qkv[at, lanes] = value
            biases[0:1, lanes] += jnp.sum(value.astype(F32), axis=0, keepdims=True)

    bias_all[p.u] = biases[...]

    def bias_copy(k):
        u = (p.u + k) % p.lines
        return remote(biases, bias_all.at[p.u], bias_sem.at[k], bias_sem.at[p.lines + k], u * TP + p.j, p.t)

    for k in range(1, p.lines):
        bias_copy(k).start()

    load_h1.wait()
    weight_grad(hh, qkv[...], gq)
    scatter_q.start_outer()
    weight_grad(cot, att[...], go)
    scatter_o.start_outer()
    scatter_q.start_rest()
    scatter_o.start_rest()
    scatter_db.combine()
    scatter_gb.combine()

    sums.arrive()

    @pl.loop(0, half // 32)
    def _(i):
        at = pl.multiple_of(i * 32, 32)
        resid[pl.ds(at, 32), :] += sums.total(at, 32)

    sums.release()
    mine = pl.ds(pl.multiple_of(p.t * half, half), half)

    def give(index, value, out):
        here = pltpu.make_async_copy(value, out.at[mine], swap_sem.at[index, 0])
        there = remote(value, out.at[mine], swap_sem.at[index, 1], swap_sem.at[index, 2], p.me, 1 - p.t)
        here.start()
        there.start()
        return here, there

    gives = [*give(1, resid, block_out)]

    sums.acquire()
    sums.start(lambda s, n, step: dot(qkv[rows_of(s), :], wq[columns(n, step), :], 1, 1))
    sums.arrive()

    @pl.loop(0, half // 32)
    def _(i):
        at = pl.multiple_of(i * 32, 32)
        values = tok_src[pl.ds(pl.multiple_of(p.t * half + at, 32), 32), :].astype(F32)
        scaled, inverse = norm_stats(values)
        part, gain, shift = norm_back(sums.total(at, 32), scaled, inverse, norms[0:1, :D])
        gains[0:1, :] += gain[None]
        gains[1:2, :] += shift[None]
        grad[pl.ds(at, 32), :] += part

    gives += give(0, grad, input_out)

    def tile_of(d):
        return pl.ds(pl.multiple_of(d * rows // 128 * 128, 128), 128)

    def gain_copy(dest):
        return remote(gains.at[:, tile_of(dest)], small_all.at[p.me], gain_sem.at[dest], gain_sem.at[count], dest, p.t)

    swap = remote(gains, gains_t, t_sem.at[0], t_sem.at[1], p.me, 1 - p.t)
    swap.start()
    swap.wait()
    gains[...] = gains[...] + gains_t[...]
    pltpu.make_async_copy(gains.at[:, tile_of(p.me)], small_all.at[p.me], gain_sem.at[count]).start()
    each_dest(p, lambda dest, u, j: gain_copy(dest).start())

    scatter_da.reduce()
    scatter_ga.reduce()
    scatter_db.reduce()
    scatter_gb.reduce()
    scatter_q.combine()
    scatter_o.combine()

    for k in range(1, p.lines):
        bias_copy(k).wait_recv()
    total = bias_all[0]
    for k in range(1, p.lines):
        total = total + bias_all[k]
    bias_out[p.j] = total

    def rank_copy(q):
        j = (p.j + q) % TP
        return remote(bias_out.at[p.j], bias_out.at[p.j], rank_sem.at[q], rank_sem.at[TP + q], p.u * TP + j, p.t)

    for q in range(1, TP):
        rank_copy(q).start()

    scatter_q.reduce()
    scatter_o.reduce()
    wait_bytes(small_all, gain_sem.at[count])
    total = small_all[0]
    for d in range(1, count):
        total = total + small_all[d]
    norm_out[...] = total
    for q in range(1, TP):
        rank_copy(q).wait()
    for k in range(1, p.lines):
        bias_copy(k).wait_send()
    each_dest(p, lambda dest, u, j: small_copy(dest).wait_send())
    each_dest(p, lambda dest, u, j: gain_copy(dest).wait_send())
    for copy in gives:
        copy.wait()
    for part in (auxes, rowses, sums, spread_r, gather_q, gather_o, gather_da, gather_db):
        part.finish()
    for scatter in scatters:
        scatter.finish()


def layer(count, small, aux, row, tokens, cot, *weights):
    size = tokens.shape[0]
    half = size // 2
    group = TP * size
    lines, rows = count // TP, weights[0].shape[1]
    _, wide, gates_a, hid_a, gates_b, hid_b = [w.shape[2] for w in weights]
    pad = hid_a + hid_b
    any_spec = pl.BlockSpec(memory_space=pl.ANY)
    vmem = pl.BlockSpec(memory_space=pltpu.VMEM)
    dma = pltpu.SemaphoreType.DMA
    regular = pltpu.SemaphoreType.REGULAR

    def out(*shape, dtype=BF16):
        return jax.ShapeDtypeStruct(shape, dtype)

    return pl.pallas_call(
        functools.partial(layer_kernel, count),
        in_specs=[vmem, vmem, vmem, vmem] + [any_spec] * 7,
        out_specs=[any_spec] * 9 + [vmem] * 2,
        out_shape=[
            *[out(TP, rows, w.shape[2]) for w in weights],
            out(size, D, dtype=F32),
            out(size, D, dtype=F32),
            out(group, D),
            out(8, 128, dtype=F32),
            out(TP, 8, 3 * wide, dtype=F32),
        ],
        scratch_shapes=[
            *[pltpu.VMEM((D, w.shape[2]), BF16) for w in weights],
            pltpu.VMEM((group, D), BF16),
            pltpu.VMEM((group, D), BF16),
            pltpu.VMEM((group, 3 * wide), BF16),
            pltpu.VMEM((group, wide), BF16),
            pltpu.VMEM((group, pad), BF16),
            pltpu.VMEM((max(2 * group, D), max(pad, 3 * wide)), BF16),
            pltpu.VMEM((group, gates_a), BF16),
            pltpu.VMEM((group, gates_b), BF16),
            pltpu.VMEM((D, hid_a), BF16),
            pltpu.VMEM((D, gates_a), BF16),
            pltpu.VMEM((D, hid_b), BF16),
            pltpu.VMEM((D, gates_b), BF16),
            pltpu.VMEM((D, wide), BF16),
            pltpu.VMEM((D, gates_a), BF16),
            pltpu.VMEM((D, hid_a), BF16),
            pltpu.VMEM((D, hid_b), BF16),
            pltpu.VMEM((D, wide), BF16),
            pltpu.VMEM((2, size, D), BF16),
            pltpu.VMEM((2, size, D), BF16),
            pltpu.VMEM((2, size, D), BF16),
            pltpu.VMEM((half, D), F32),
            pltpu.VMEM((3, half, D), BF16),
            pltpu.VMEM((half, D), F32),
            pltpu.VMEM((half, D), F32),
            pltpu.VMEM((8, D), F32),
            pltpu.VMEM((8, 3 * wide), F32),
            pltpu.VMEM((16, max(D, 128 * (small.shape[0] - 16))), F32),
            pltpu.VMEM((count,) + small.shape, BF16),
            pltpu.VMEM((TP, size, 128), F32),
            pltpu.VMEM((TP, 8, size), F32),
            pltpu.VMEM((count, 8, 128), F32),
            pltpu.VMEM((lines, 8, 3 * wide), F32),
            pltpu.VMEM((8, D), F32),
            dma((6, TP + lines)),
            dma((6, 4)),
            dma((count + 1,)),
            dma((2, 4)),
            dma((2, 4)),
            dma((2, 4)),
            dma((2, 4)),
            dma((2,)),
            dma((6, TP + lines)),
            dma((6, 4)),
            regular((lines,)),
            regular((lines,)),
            dma((2, 2)),
            dma((2, 4)),
            regular((4,)),
            dma((2, 4)),
            dma((2, 4)),
            dma((2, 4)),
            dma((2, 4)),
            dma((2, 3)),
            dma((count + 1,)),
            dma((2 * lines,)),
            dma((2 * TP,)),
            dma((2,)),
        ],
        compiler_params=pltpu.CompilerParams(
            collective_id=0, has_side_effects=True, vmem_limit_bytes=63 * 1024 * 1024
        ),
        cost_estimate=pl.CostEstimate(flops=40 * 10**9, bytes_accessed=60 * 10**6, transcendentals=10**7),
        name="layer",
    )(small, aux, row, tokens, cot, *weights)


def prepare_kernel(
    first, *refs,
):
    ins, outs = refs[:7], refs[7:16]
    held, made = refs[16:23], refs[23:32]
    lines, in_sem, out_sem = refs[32:]
    loads = [pltpu.make_async_copy(ref, here, in_sem.at[i]) for i, (ref, here) in enumerate(zip(ins, held))]
    stores = [pltpu.make_async_copy(here, ref, out_sem.at[i]) for i, (here, ref) in enumerate(zip(made, outs))]
    for copy in loads:
        copy.start()
    seg_ref, norm_ref, bias_ref, qkv_ref, out_ref, gates_ref, down_ref = held
    small, aux, row, wq, wo, wga, wda, wgb, wdb = made
    for copy in loads[:3]:
        copy.wait()
    size = seg_ref.shape[1]
    wide, second = wo.shape[2], (wgb.shape[2] - 128) // 2
    full = first + second
    me = lax.axis_index("dp")

    start = me * bias_ref.shape[1]
    wrapped = jnp.concatenate([bias_ref[...], jnp.zeros((1, 256 - bias_ref.shape[1]), F32)], axis=1)
    wrapped = pltpu.roll(jnp.broadcast_to(wrapped, (8, 256)), start % 128, 1)
    lines[...] = jnp.zeros_like(lines)
    lines[0:4, :] = norm_ref[...]
    lines[pl.ds(16 + start // 128, 1), :] = wrapped[0:1, :128]
    lines[pl.ds(17 + start // 128, 1), :] = wrapped[0:1, 128:]
    small[...] = lines[...].astype(BF16)

    seg = seg_ref[...].astype(F32)
    row[...] = jnp.broadcast_to(seg, row.shape)
    column = jnp.transpose(jnp.broadcast_to(seg, (128, size)))
    earlier = jnp.sum((seg < column[:, 0:1]).astype(F32), axis=1, keepdims=True)
    position = lax.broadcasted_iota(jnp.int32, (size, 128), 0).astype(F32) - earlier
    lane = lax.broadcasted_iota(jnp.int32, (size, 128), 1)
    half = ROT // 2
    frequency = jnp.zeros((size, 128), F32)
    for k in range(half):
        frequency = jnp.where(lane % half == k, 10000.0 ** (-2.0 * k / ROT), frequency)
    angles = position * frequency
    turned = jnp.where(lane < half, jnp.cos(angles), jnp.sin(angles))
    aux[...] = jnp.where(lane < ROT, turned, jnp.where(lane == ROT, column, 0.0))

    left = lax.broadcasted_iota(jnp.int32, (wq.shape[1], 128), 1) < 64
    for copy in stores[:3]:
        copy.start()
    loads[3].wait()
    for j in range(TP):
        for k in range(3):
            wq[j, :, k * wide : (k + 1) * wide] = qkv_ref[k, :, j * wide : (j + 1) * wide].astype(BF16)
    stores[3].start()
    loads[4].wait()
    for j in range(TP):
        wo[j] = jnp.transpose(out_ref[j * wide : (j + 1) * wide, :]).astype(BF16)
    stores[4].start()
    loads[5].wait()
    for j in range(TP):
        for k in range(2):
            begin = j * full
            wga[j, :, k * first : (k + 1) * first] = gates_ref[:, k, begin : begin + first].astype(BF16)
            wgb[j, :, k * second : (k + 1) * second] = gates_ref[:, k, begin + first : begin + full].astype(BF16)
        tile = slice(TP * full + j // 2 * 128, TP * full + j // 2 * 128 + 128)
        gate, up = gates_ref[:, 0, tile], gates_ref[:, 1, tile]
        if j % 2:
            gate = pltpu.roll(gate, 64, 1)
        else:
            up = pltpu.roll(up, 64, 1)
        wgb[j, :, 2 * second :] = jnp.where(left, gate, up).astype(BF16)
    stores[5].start()
    stores[7].start()
    loads[6].wait()
    for j in range(TP):
        wda[j] = jnp.transpose(down_ref[j * full : j * full + first, :]).astype(BF16)
        wdb[j, :, :second] = jnp.transpose(down_ref[j * full + first : (j + 1) * full, :]).astype(BF16)
        tile = slice(TP * full + j // 2 * 128, TP * full + j // 2 * 128 + 128)
        tail = jnp.transpose(down_ref[tile, :])
        if j % 2:
            tail = pltpu.roll(tail, 64, 1)
        wdb[j, :, second:] = jnp.where(left, tail, 0.0).astype(BF16)
    stores[6].start()
    stores[8].start()
    for copy in stores:
        copy.wait()


def prepare(first, seg, norm, bias, qkv, out, gates, down):
    rows, size = norm.shape[1], seg.shape[1]
    wide, hid = qkv.shape[2] // TP, down.shape[0] // TP
    second = hid // 128 * 128 - first
    lines = 16 + 3 * qkv.shape[2] // 128

    def shape(*dims, dtype=BF16):
        return jax.ShapeDtypeStruct(dims, dtype)

    given = (seg, norm, bias, qkv, out, gates, down)
    shapes = [
        shape(lines, 128),
        shape(size, 128, dtype=F32),
        shape(8, size, dtype=F32),
        shape(TP, rows, 3 * wide),
        shape(TP, rows, wide),
        shape(TP, rows, 2 * first),
        shape(TP, rows, first),
        shape(TP, rows, 2 * second + 128),
        shape(TP, rows, second + 128),
    ]
    return pl.pallas_call(
        functools.partial(prepare_kernel, first),
        in_specs=[pl.BlockSpec(memory_space=pl.ANY)] * 7,
        out_specs=[pl.BlockSpec(memory_space=pl.ANY)] * 9,
        out_shape=shapes,
        scratch_shapes=[pltpu.VMEM(x.shape, x.dtype) for x in (*given, *shapes)]
        + [pltpu.VMEM((lines, 128), F32), pltpu.SemaphoreType.DMA((7,)), pltpu.SemaphoreType.DMA((9,))],
        compiler_params=pltpu.CompilerParams(vmem_limit_bytes=60 * 1024 * 1024),
        name="prepare",
    )(*given)


def step_weights(weight, first, second, gradient, step_rate, decay_rate):
    first = 0.9 * first + 0.1 * gradient
    second = 0.95 * second + 0.05 * gradient * gradient
    corrected = first * (1.0 / (1.0 - 0.9**STEP)) / (jnp.sqrt(second * (1.0 / (1.0 - 0.95**STEP))) + 1e-08)
    return weight - step_rate * (corrected + decay_rate * weight), first, second


def update_kernel(*refs):
    ins, outs = refs[:18], refs[18:30]
    held = refs[30:48]
    in_sem, out_sem = refs[48:]
    loads = [pltpu.make_async_copy(ref, here, in_sem.at[i]) for i, (ref, here) in enumerate(zip(ins, held))]
    for copy in loads:
        copy.start()
    rs_q, rs_o, rs_ga, rs_gb, rs_da, rs_db = held[:6]
    states = [held[6 + 3 * i : 9 + 3 * i] for i in range(4)]
    stores = [
        pltpu.make_async_copy(here, ref, out_sem.at[i]) for i, (here, ref) in enumerate(zip(held[6:], outs))
    ]

    def ready(index, *gradients):
        for i in (*gradients, *range(6 + 3 * index, 9 + 3 * index)):
            loads[i].wait()

    def done(index):
        for copy in stores[3 * index : 3 * index + 3]:
            copy.start()

    def change(index, at, gradient, rate):
        new = step_weights(*(ref[at] for ref in states[index]), gradient, rate, 0.1)
        for ref, value in zip(states[index], new):
            ref[at] = value

    every = slice(None)
    wide = rs_o.shape[2]
    first, second = rs_da.shape[2], rs_db.shape[2] - 128
    full = first + second
    left = lax.broadcasted_iota(jnp.int32, (rs_gb.shape[1], 128), 1) < 64

    ready(0, 0)
    for k in range(3):
        for j in range(TP):
            gradient = rs_q[j, :, k * wide : (k + 1) * wide].astype(F32)
            change(0, (k, every, slice(j * wide, (j + 1) * wide)), gradient, D ** (-0.5))
    done(0)
    ready(2, 2, 3)
    for j in range(TP):
        for k in range(2):
            begin = j * full
            gradient = rs_ga[j, :, k * first : (k + 1) * first].astype(F32)
            change(2, (every, k, slice(begin, begin + first)), gradient, D ** (-0.5))
            gradient = rs_gb[j, :, k * second : (k + 1) * second].astype(F32)
            change(2, (every, k, slice(begin + first, begin + full)), gradient, D ** (-0.5))
    for i in range(TP // 2):
        even = rs_gb[2 * i, :, 2 * second :].astype(F32)
        odd = rs_gb[2 * i + 1, :, 2 * second :].astype(F32)
        tile = slice(TP * full + i * 128, TP * full + (i + 1) * 128)
        change(2, (every, 0, tile), jnp.where(left, even, pltpu.roll(odd, 64, 1)), D ** (-0.5))
        change(2, (every, 1, tile), jnp.where(left, pltpu.roll(even, 64, 1), odd), D ** (-0.5))
    done(2)
    ready(3, 4, 5)
    for j in range(TP):
        begin = j * full
        gradient = jnp.transpose(rs_da[j].astype(F32))
        change(3, (slice(begin, begin + first), every), gradient, FF ** (-0.5))
        gradient = jnp.transpose(rs_db[j].astype(F32))
        change(3, (slice(begin + first, begin + full), every), gradient[:second], FF ** (-0.5))
        begin = TP * full + j * 64
        change(3, (slice(begin, begin + 64), every), gradient[second : second + 64], FF ** (-0.5))
    done(3)
    ready(1, 1)
    for j in range(TP):
        gradient = jnp.transpose(rs_o[j].astype(F32))
        change(1, (slice(j * wide, (j + 1) * wide), every), gradient, (H * HD // 16) ** (-0.5))
    done(1)
    for copy in stores:
        copy.wait()


def update(gradients, states):
    given = (*gradients, *states)
    any_spec = pl.BlockSpec(memory_space=pl.ANY)
    return pl.pallas_call(
        update_kernel,
        in_specs=[any_spec] * 18,
        out_specs=[any_spec] * 12,
        out_shape=[jax.ShapeDtypeStruct(x.shape, x.dtype) for x in states],
        scratch_shapes=[pltpu.VMEM(x.shape, x.dtype) for x in given]
        + [pltpu.SemaphoreType.DMA((18,)), pltpu.SemaphoreType.DMA((12,))],
        compiler_params=pltpu.CompilerParams(vmem_limit_bytes=60 * 1024 * 1024),
        name="update",
    )(*given)


def laid_out(values):
    return with_layout_constraint(values, Layout(tuple(range(values.ndim))))


def per_device(
    count,
    tokens_in,
    segment_ids,
    d_out,
    qkv_weight,
    qkv_bias,
    out_weight,
    gating_weight,
    down_weight,
    norm_params,
    qkv_first,
    qkv_second,
    bias_first,
    bias_second,
    out_first,
    out_second,
    gating_first,
    gating_second,
    down_first,
    down_second,
    norm_first,
    norm_second,
):
    place = lax.axis_index("dp")
    rows = norm_params.shape[1]
    seq_len = tokens_in.shape[1]
    head_local = qkv_weight.shape[2]
    hidden_local = gating_weight.shape[2]
    wide = head_local // TP
    hid = hidden_local // TP
    full = hid // 128 * 128

    first = -(-(full // 2) // 128) * 128
    spare = hid - full
    bias_here = qkv_bias.shape[1]
    if rows % 128 == 0 and spare == 64 and bias_here <= 192:
        small, aux, row, *weights = prepare(
            first, segment_ids, norm_params, qkv_bias, qkv_weight.transpose(1, 0, 2), out_weight, gating_weight, down_weight
        )
    else:
        low_gates = laid_out(gating_weight.astype(BF16))

        def gate_cut(k, start, width):
            return [low_gates[:, k, j * width + start : (j + 1) * width + start] for j in range(TP)]

        def ranks(parts):
            return jnp.stack([jnp.concatenate(one, axis=1) for one in zip(*parts, strict=True)])

        low_down = down_weight.astype(BF16)
        down_full = low_down[: TP * full].reshape(TP, full, rows)
        gate_full = [[low_gates[:, k, j * full : (j + 1) * full] for j in range(TP)] for k in range(2)]
        weights = (
            ranks([[qkv_weight[:, k, j * wide : (j + 1) * wide] for j in range(TP)] for k in range(3)]).astype(BF16),
            out_weight.astype(BF16).reshape(TP, wide, rows).transpose(0, 2, 1),
            ranks([[part[:, :first] for part in gate_full[k]] for k in range(2)]),
            down_full[:, :first].transpose(0, 2, 1),
            ranks([[part[:, first:] for part in gate_full[k]] for k in range(2)] + [gate_cut(k, TP * full, spare) for k in range(2)]),
            jnp.concatenate(
                [
                    down_full[:, first:],
                    low_down[TP * full :].reshape(TP, spare, rows),
                    jnp.zeros((TP, -hid % 128, rows), BF16),
                ],
                axis=1,
            ).transpose(0, 2, 1),
        )
        small_norm = lax.dynamic_update_slice(jnp.zeros((16, 128), F32), norm_params, (0, (place * rows) % 128))
        small_bias = lax.dynamic_update_slice(jnp.zeros((3 * head_local,), F32), qkv_bias[0], (place * bias_here,))
        small = jnp.concatenate([small_norm, small_bias.reshape(-1, 128)]).astype(BF16)
        segments = segment_ids[0]
        earlier = jnp.sum((segments[None, :] < segments[:, None]).astype(jnp.int32), axis=1)
        positions = (jnp.arange(seq_len, dtype=jnp.int32) - earlier).astype(F32)
        frequency = 10000.0 ** (-2.0 * jnp.arange(ROT // 2, dtype=F32) / ROT)
        angles = positions[:, None] * frequency[None, :]
        aux = jnp.concatenate([jnp.cos(angles), jnp.sin(angles), segments[:, None].astype(F32)], axis=1)
        aux = jnp.pad(aux, ((0, 0), (0, 128 - aux.shape[1])))
        row = jnp.broadcast_to(segments.astype(F32)[None], (8, seq_len))

    rs_q, rs_o, rs_ga, rs_da, rs_gb, rs_db, block_out, input_grad, _, norm_sum, bias_sum = layer(
        count, small, aux, row, tokens_in[0], d_out[0], *weights
    )

    norm_grad = lax.dynamic_slice_in_dim(norm_sum[:4], (place * rows) % 128, rows, 1)
    bias_grad = bias_sum[:, 0].reshape(TP, 3, wide).transpose(1, 0, 2).reshape(1, 3 * head_local)
    bias_grad = lax.dynamic_slice_in_dim(bias_grad, place * bias_here, bias_here, 1)
    if rows % 128 == 0 and spare == 64 and bias_here <= 192:
        planes = [x.transpose(1, 0, 2) for x in (qkv_weight, qkv_first, qkv_second)]
        new = update(
            (rs_q, rs_o, rs_ga, rs_gb, rs_da, rs_db),
            (*planes, out_weight, out_first, out_second, gating_weight, gating_first, gating_second)
            + (down_weight, down_first, down_second),
        )
        new_qkv, new_out, new_gating, new_down = [x.transpose(1, 0, 2) for x in new[:3]], new[3:6], new[6:9], new[9:]
    else:
        second = full - first
        gate_parts = [
            jnp.concatenate(
                [
                    part
                    for j in range(TP)
                    for part in (
                        rs_ga[j, :, k * first : (k + 1) * first],
                        rs_gb[j, :, k * second : (k + 1) * second],
                    )
                ]
                + [rs_gb[j, :, 2 * second + k * spare : 2 * second + (k + 1) * spare] for j in range(TP)],
                axis=1,
            )
            for k in range(2)
        ]
        gating_shard = lax.optimization_barrier(laid_out(jnp.stack(gate_parts, axis=1))).astype(F32)
        qkv_shard = jnp.stack(
            [
                jnp.concatenate([rs_q[j, :, k * wide : (k + 1) * wide] for j in range(TP)], axis=1)
                for k in range(3)
            ],
            axis=1,
        ).astype(F32)
        out_shard = laid_out(rs_o.transpose(0, 2, 1).reshape(head_local, rows)).astype(F32)
        down_parts = jnp.concatenate([rs_da, rs_db], axis=2).transpose(0, 2, 1)
        down_shard = laid_out(
            jnp.concatenate(
                [down_parts[:, :full].reshape(TP * full, rows), down_parts[:, full:hid].reshape(TP * spare, rows)]
            )
        ).astype(F32)
        new_qkv = adamw_update(qkv_weight, qkv_shard, qkv_first, qkv_second, D ** (-0.5), 0.1)
        new_out = adamw_update(out_weight, out_shard, out_first, out_second, (H * HD // 16) ** (-0.5), 0.1)
        new_gating = adamw_update(gating_weight, gating_shard, gating_first, gating_second, D ** (-0.5), 0.1)
        new_down = adamw_update(down_weight, down_shard, down_first, down_second, FF ** (-0.5), 0.1)
    return (
        block_out[None],
        input_grad[None],
        *new_qkv,
        *adamw_update(qkv_bias, bias_grad, bias_first, bias_second, 0.3, 0.0),
        *new_out,
        *new_gating,
        *new_down,
        *adamw_update(norm_params, norm_grad, norm_first, norm_second, 0.25, 0.0),
    )


def solution(mesh):
    tokens = P("dp", None, None)
    qkv = P("dp", None, "tensor")
    rest = P("tensor", "dp")
    norm = P(None, "dp")
    weights = (qkv, rest, rest, qkv, rest, norm)
    states = (qkv, qkv, rest, rest, rest, rest, qkv, qkv, rest, rest, norm, norm)
    return jax.shard_map(
        functools.partial(per_device, mesh.shape["dp"]),
        mesh=mesh,
        in_specs=(tokens, P("dp", None), tokens, *weights, *states),
        out_specs=(tokens, tokens, *(spec for spec in weights for _ in range(3))),
        check_vma=False,
    )
```

```python
import functools

import jax
import jax.numpy as jnp
from jax import lax
from jax.experimental import pallas as pl
from jax.experimental.layout import Layout, with_layout_constraint
from jax.experimental.pallas import tpu as pltpu
from jax.sharding import PartitionSpec as P

D = 2048
H = 32
HD = 64
ROT = 16
FF = 5632
STEP = 10
TP = 4

F32 = jnp.float32
BF16 = jnp.bfloat16


def layer_norm(values, scale_row, shift_row):
    centre = values - jnp.mean(values, axis=-1, keepdims=True)
    spread = jnp.mean(centre * centre, axis=-1, keepdims=True)
    inverse = lax.rsqrt(spread + 1e-05)
    scaled = centre * inverse
    return (scaled * scale_row + shift_row, scaled, inverse)


def norm_back(grad_in, scaled, inverse, scale_row):
    grad_scaled = grad_in * scale_row
    mean_first = jnp.mean(grad_scaled, axis=-1, keepdims=True)
    mean_second = jnp.mean(grad_scaled * scaled, axis=-1, keepdims=True)
    grad_values = inverse * (grad_scaled - mean_first - scaled * mean_second)
    return (grad_values, jnp.sum(grad_in * scaled, axis=0), jnp.sum(grad_in, axis=0))


def adamw_update(weight_old, gradient, first_old, second_old, step_rate, decay_rate):
    first_new = 0.9 * first_old + 0.1 * gradient
    second_new = 0.95 * second_old + 0.05 * gradient * gradient
    corrected = first_new / (1.0 - 0.9**STEP) / (jnp.sqrt(second_new / (1.0 - 0.95**STEP)) + 1e-08)
    return (weight_old - step_rate * (corrected + decay_rate * weight_old), first_new, second_new)


def dot(a, b, ca, cb):
    return lax.dot_general(a, b, (((ca,), (cb,)), ((), ())), preferred_element_type=F32)


def spin(values, cos_t, lower_t, upper_t):
    wide = values.shape[1]
    return (
        values * cos_t
        + pltpu.roll(values, wide - ROT // 2, 1) * lower_t
        + pltpu.roll(values, ROT // 2, 1) * upper_t
    )


def spin_back(values, cos_t, lower_t, upper_t):
    wide = values.shape[1]
    return (
        values * cos_t
        + pltpu.roll(values * lower_t, ROT // 2, 1)
        + pltpu.roll(values * upper_t, wide - ROT // 2, 1)
    )


def mask_of(seg_col, seg_row, size):
    rows = lax.broadcasted_iota(jnp.int32, (size, size), 0)
    cols = lax.broadcasted_iota(jnp.int32, (size, size), 1)
    return (seg_col == seg_row) & (cols <= rows)


def attend_back_values(query, key, value, grad, allowed, tables):
    head_of = lax.broadcasted_iota(jnp.int32, query.shape, 1) // HD
    zero = jnp.zeros_like(query)
    dq = jnp.zeros(query.shape, F32)
    dk = jnp.zeros(query.shape, F32)
    dv = jnp.zeros(query.shape, F32)
    for head in range(query.shape[1] // HD):
        mine = head_of == head
        query_h = jnp.where(mine, query, zero)
        grad_h = jnp.where(mine, grad, zero)
        scores = dot(query_h, key, 1, 1) * HD ** (-0.5)
        scores = jnp.where(allowed, scores, -1e30)
        weights = jnp.exp(scores - jnp.max(scores, axis=1, keepdims=True))
        prob = weights / jnp.sum(weights, axis=1, keepdims=True)
        dv = dv + dot(prob.astype(BF16), grad_h, 0, 0)
        dprob = dot(grad_h, value, 1, 1)
        delta = jnp.sum(prob * dprob, axis=1, keepdims=True)
        dscore = (prob * (dprob - delta)).astype(BF16)
        dq = jnp.where(mine, dot(dscore, key, 1, 0), dq)
        dk = dk + dot(dscore, query_h, 0, 0)
    dq = spin_back(dq * HD ** (-0.5), *tables).astype(BF16)
    dk = spin_back(dk * HD ** (-0.5), *tables).astype(BF16)
    return dq, dk, dv.astype(BF16)


class Place:
    def __init__(self, count):
        self.count = count
        self.lines = count // TP
        self.me = lax.axis_index("dp")
        self.t = lax.axis_index("tensor")
        self.u = self.me // TP
        self.j = self.me % TP
        self.x = self.j // 2
        self.c = self.j % 2
        self.core_peer = self.me + 1 - 2 * self.c
        self.x_peer = self.me + 2 - 4 * self.x

    def group(self, k):
        x = (self.x + k // 2) % 2
        return self.u * TP + x * 2 + self.c, (self.t + k % 2) % 2, x


def remote(src, dst, send_sem, recv_sem, dp, t):
    return pltpu.make_async_remote_copy(
        src_ref=src,
        dst_ref=dst,
        send_sem=send_sem,
        recv_sem=recv_sem,
        device_id=(dp, t),
        device_id_type=pl.DeviceIdType.MESH,
    )


def wait_bytes(ref, sem):
    pltpu.make_async_copy(ref, ref, sem).wait()


def greet(place):
    barrier = pltpu.get_barrier_semaphore()

    @pl.loop(1, place.count)
    def _(k):
        pl.semaphore_signal(
            barrier,
            inc=1,
            device_id=((place.me + k) % place.count, place.t),
            device_id_type=pl.DeviceIdType.MESH,
        )

    for k in (1, 3):
        dp, t, _ = place.group(k)
        pl.semaphore_signal(barrier, inc=1, device_id=(dp, t), device_id_type=pl.DeviceIdType.MESH)
    pl.semaphore_wait(barrier, place.count + 1)


def each_dest(place, act):
    if place.lines == 4:

        @pl.loop(1, TP)
        def _(q):
            j = (place.j + q) % TP
            act(place.u * TP + j, place.u, j)

        @pl.loop(0, TP)
        def _(q):
            j = (place.j + q) % TP
            for dz in (2, 1, 3):
                u = (place.u + dz) % 4
                act(u * TP + j, u, j)

    else:

        @pl.loop(1, place.count)
        def _(k):
            dest = (place.me + k) % place.count
            act(dest, dest // TP, dest % TP)


class WeightGather:
    def __init__(self, place, index, src, dst, send_sem, recv_sem):
        self.place, self.src, self.dst = place, src, dst
        self.send_sem, self.recv_sem = send_sem.at[index], recv_sem.at[index]
        self.rows = src.shape[1]

    def group_copy(self, q):
        p = self.place
        j = (p.j + q) % TP
        mine = self.dst.at[pl.ds(p.me * self.rows, self.rows)]
        return remote(self.src.at[j], mine, self.send_sem.at[q], self.recv_sem.at[2], p.u * TP + j, p.t)

    def chunk(self, u):
        size = TP * self.rows
        return self.dst.at[pl.ds(u * size, size)]

    def line_copy(self, k):
        p = self.place
        u = (p.u + k) % p.lines
        sem = 0
        if p.lines == 4:
            sem = jnp.where(self.middle(), jnp.where(p.u + u == 3, 3, 0), jnp.where(jnp.abs(p.u - u) == 2, 1, 0))
        mine = self.chunk(p.u)
        return remote(mine, mine, self.send_sem.at[TP + k], self.recv_sem.at[sem], u * TP + p.j, p.t)

    def line_each(self, act):
        p = self.place
        if p.lines == 4:
            for k in (2, 1, 3):
                gap = jnp.abs(p.u - (p.u + k) % 4)
                pl.when((gap == 1) | ((gap == 2) & ~self.middle()))(lambda k=k: act(k))
        else:
            for k in range(1, p.lines):
                act(k)

    def start(self):
        p = self.place
        for q in (2, 3, 1):
            self.group_copy(q).start()
        mine = self.dst.at[pl.ds(p.me * self.rows, self.rows)]
        pltpu.make_async_copy(self.src.at[p.j], mine, self.recv_sem.at[2]).start()

    def pass_on(self):
        wait_bytes(self.chunk(0), self.recv_sem.at[2])
        self.line_each(lambda k: self.line_copy(k).start())

    def middle(self):
        return (self.place.u == 1) | (self.place.u == 2)

    def forward(self, which):
        p = self.place
        up = p.u == 2
        chunk = self.chunk(jnp.where(up, which, 3 - which))
        sem = self.send_sem.at[TP + 2 * which]
        return remote(chunk, chunk, sem, self.recv_sem.at[1], p.me + jnp.where(up, TP, -TP), p.t)

    def relay(self):
        if self.place.lines == 4:

            @pl.when(self.middle())
            def _():
                wait_bytes(self.chunk(0), self.recv_sem.at[3])
                self.forward(1).start()
                wait_bytes(self.chunk(0), self.recv_sem.at[1])
                self.forward(0).start()

    def arrive(self):
        p = self.place
        size = TP * self.rows
        if p.lines == 4:
            wait_bytes(self.chunk(0), self.recv_sem.at[0])
            pl.when(~self.middle())(lambda: wait_bytes(self.dst.at[pl.ds(0, 2 * size)], self.recv_sem.at[1]))
        else:
            wait_bytes(self.dst.at[pl.ds(0, size * (p.lines - 1))], self.recv_sem.at[0])

    def finish(self):
        for q in range(1, TP):
            self.group_copy(q).wait_send()
        self.line_each(lambda k: self.line_copy(k).wait_send())
        if self.place.lines == 4:

            @pl.when(self.middle())
            def _():
                self.forward(1).wait_send()
                self.forward(0).wait_send()


class GroupSum:
    def __init__(self, place, to_core, from_core, low, own, parts, core_sem, part_sem, free_sem=None):
        self.place = place
        self.to_core, self.from_core, self.low, self.own, self.parts = to_core, from_core, low, own, parts
        self.core_sem, self.part_sem, self.free_sem = core_sem, part_sem, free_sem

    def core_copy(self, i):
        p = self.place
        return remote(
            self.to_core.at[i], self.from_core.at[i], self.core_sem.at[0, i], self.core_sem.at[1, i], p.core_peer, p.t
        )

    def part_copy(self, k):
        p = self.place
        half = self.parts.shape[1]
        dp, t, _ = p.group(k)
        block = self.low.at[0 if k >= 2 else 1, pl.ds(pl.multiple_of(t * half, half), half)]
        return remote(block, self.parts.at[k - 1], self.part_sem.at[0, k], self.part_sem.at[1, k], dp, t)

    def start(self, product):
        p = self.place
        step = min(512, D)
        other = [(p.x + 1) % 2, p.x]
        for i in range(2):

            @pl.loop(0, D // step)
            def _(n):
                at = pl.ds(pl.multiple_of(n * step, step), step)
                self.to_core[i, :, at] = product(other[i] * 2 + 1 - p.c, n, step).astype(BF16)

            self.core_copy(i).start()
        for i in range(2):
            self.core_copy(i).wait_recv()

            @pl.loop(0, D // step)
            def _(n):
                at = pl.ds(pl.multiple_of(n * step, step), step)
                total = product(other[i] * 2 + p.c, n, step) + self.from_core[i, :, at].astype(F32)
                self.low[i, :, at] = total.astype(BF16)
                if i == 1:
                    half = self.own.shape[0]

                    @pl.when(p.t == 0)
                    def _():
                        self.own[:, at] = total[:half]

                    @pl.when(p.t == 1)
                    def _():
                        self.own[:, at] = total[half:]

            for k in (3, 2) if i == 0 else (1,):
                self.part_copy(k).start()

    def arrive(self):
        for k in (3, 2, 1):
            self.part_copy(k).wait_recv()

    def total(self, at, rows):
        value = self.own[pl.ds(pl.multiple_of(at, 32), rows), :]
        for k in range(3):
            value = value + self.parts[k, pl.ds(pl.multiple_of(at, 32), rows), :].astype(F32)
        return value

    def finish(self):
        for i in range(2):
            self.core_copy(i).wait_send()
        for k in (1, 2, 3):
            self.part_copy(k).wait_send()

    def release(self):
        p = self.place
        pl.semaphore_signal(
            self.free_sem.at[0], inc=1, device_id=(p.core_peer, p.t), device_id_type=pl.DeviceIdType.MESH
        )
        for k in (1, 2, 3):
            dp, t, _ = p.group(k)
            pl.semaphore_signal(
                self.free_sem.at[k], inc=1, device_id=(dp, t), device_id_type=pl.DeviceIdType.MESH
            )

    def acquire(self):
        self.finish()
        for k in range(4):
            pl.semaphore_wait(self.free_sem.at[k], 1)


class GroupGather:
    def __init__(self, place, out, size, part_sem, core_sem):
        self.place, self.out, self.half = place, out, size // 2
        self.part_sem, self.core_sem = part_sem, core_sem

    def block(self, x, t):
        p = self.place
        start = ((x * 2 + p.c) * 2 + t) * self.half
        return self.out.at[pl.ds(pl.multiple_of(start, self.half), self.half)]

    def part_copy(self, k):
        p = self.place
        dp, t, _ = p.group(k)
        mine = self.block(p.x, p.t)
        return remote(mine, mine, self.part_sem.at[0, k], self.part_sem.at[1, k], dp, t)

    def core_copy(self, k):
        p = self.place
        _, t, x = p.group(k)
        block = self.block(x, t)
        return remote(block, block, self.core_sem.at[0, k], self.core_sem.at[1, k], p.core_peer, p.t)

    def start(self):
        for k in (3, 2, 1):
            self.part_copy(k).start()
        self.core_copy(0).start()

    def arrive(self):
        for k in (1, 2, 3):
            self.part_copy(k).wait_recv()
            self.core_copy(k).start()
        for k in range(4):
            self.core_copy(k).wait_recv()

    def finish(self):
        for k in (1, 2, 3):
            self.part_copy(k).wait_send()
        for k in range(4):
            self.core_copy(k).wait_send()


class GroupPieces:
    def __init__(self, place, src, out, sem, size=0):
        self.place, self.src, self.out, self.sem, self.size = place, src, out, sem, size

    def at(self, j):
        if self.size:
            return self.out.at[pl.ds(pl.multiple_of(j * self.size, self.size), self.size)]
        return self.out.at[j]

    def own(self):
        return pltpu.make_async_copy(self.src, self.at(self.place.j), self.sem.at[0, 0])

    def near(self, k):
        p = self.place
        dest = p.core_peer if k == 1 else p.x_peer
        return remote(self.src, self.at(p.j), self.sem.at[0, k], self.sem.at[1, k], dest, p.t)

    def relay(self):
        p = self.place
        block = self.at((p.j + 2) % TP)
        return remote(block, block, self.sem.at[0, 3], self.sem.at[1, 3], p.core_peer, p.t)

    def start(self):
        self.near(2).start()
        self.near(1).start()
        self.own().start()

    def pass_on(self):
        self.near(2).wait_recv()
        self.relay().start()

    def arrive(self):
        self.near(1).wait_recv()
        self.relay().wait_recv()
        self.own().wait()

    def finish(self):
        self.near(1).wait_send()
        self.near(2).wait_send()
        self.relay().wait_send()


def tables_of(aux, wide):
    half = ROT // 2
    line = lax.broadcasted_iota(jnp.int32, (aux.shape[1], wide), 0)
    lane = lax.broadcasted_iota(jnp.int32, (aux.shape[1], wide), 1) % HD
    first = lane < half
    second = (lane >= half) & (lane < ROT)

    def spread(pick, sign):
        table = jnp.where(pick, sign, 0.0).astype(F32)
        return lax.dot_general(
            aux, table, (((1,), (0,)), ((), ())), precision=lax.Precision.HIGHEST, preferred_element_type=F32
        )

    rest = lax.broadcasted_iota(jnp.int32, (aux.shape[0], wide), 1) % HD >= ROT
    cos_t = spread((line == lane % half) & (first | second), 1.0) + jnp.where(rest, 1.0, 0.0)
    low_t = spread((line == lane + half) & first, -1.0)
    upp_t = spread((line == lane) & second, 1.0)
    return cos_t, low_t, upp_t


def attend_values(query, key, value, allowed):
    head_of = lax.broadcasted_iota(jnp.int32, query.shape, 1) // HD
    total = jnp.zeros(query.shape, F32)
    for head in range(query.shape[1] // HD):
        mine = head_of == head
        scores = dot(jnp.where(mine, query, jnp.zeros_like(query)), key, 1, 1) * HD ** (-0.5)
        scores = jnp.where(allowed, scores, -1e30)
        weights = jnp.exp(scores - jnp.max(scores, axis=1, keepdims=True))
        prob = weights / jnp.sum(weights, axis=1, keepdims=True)
        total = jnp.where(mine, dot(prob.astype(BF16), value, 1, 0), total)
    return total


class GradScatter:
    def __init__(self, place, index, grad, slots, out, send_sem, recv_sem, free_sem=None):
        self.place, self.grad, self.slots, self.out = place, grad, slots, out
        self.send_sem, self.recv_sem, self.free_sem = send_sem.at[index], recv_sem.at[index], free_sem
        self.rows = out.shape[1]
        self.size = TP * self.rows

    def chunk(self, ref, u):
        return ref.at[pl.ds(u * self.size, self.size)]

    def near(self, u):
        return jnp.abs(self.place.u - u) < 3 if self.place.lines == 4 else None

    def line_each(self, act, picked=lambda u: True):
        p = self.place
        for k in (2, 1, 3) if p.lines == 4 else range(1, p.lines):
            u = (p.u + k) % p.lines
            if p.lines == 4:
                pl.when(self.near(u) & picked(u))(lambda k=k, u=u: act(k, u))
            else:
                act(k, u)

    def line_copy(self, k, u):
        p = self.place
        far = 0
        if p.lines == 4:
            far = (((p.u == 0) & (u == 2)) | ((p.u == 3) & (u == 1))).astype(jnp.int32)
        return remote(
            self.chunk(self.grad, u), self.chunk(self.slots, p.u), self.send_sem.at[TP + k], self.recv_sem.at[far],
            u * TP + p.j, p.t,
        )

    def outer(self):
        p = self.place
        first = p.u == 0
        src, dst = self.chunk(self.grad, jnp.where(first, 3, 0)), self.chunk(self.slots, jnp.where(first, 1, 2))
        return remote(src, dst, self.send_sem.at[TP], self.recv_sem.at[2], p.me + jnp.where(first, TP, -TP), p.t)

    def ends(self):
        return (self.place.u == 0) | (self.place.u == 3)

    def later(self, u):
        p = self.place
        return ((p.u == 1) & (u == 3)) | ((p.u == 2) & (u == 0))

    def allow(self):
        p = self.place
        self.line_each(
            lambda k, u: pl.semaphore_signal(
                self.free_sem.at[p.u], inc=1, device_id=(u * TP + p.j, p.t), device_id_type=pl.DeviceIdType.MESH
            )
        )

    def start(self):
        self.start_outer()
        self.start_rest()

    def start_outer(self):
        if self.free_sem is not None:
            self.line_each(lambda k, u: pl.semaphore_wait(self.free_sem.at[u], 1))
        if self.place.lines == 4:
            pl.when(self.ends())(lambda: self.outer().start())

    def start_rest(self):
        if self.place.lines == 4:
            self.line_each(lambda k, u: self.line_copy(k, u).start(), lambda u: ~self.later(u))
        else:
            self.line_each(lambda k, u: self.line_copy(k, u).start())

    def add(self, u, sources):
        p = self.place

        @pl.loop(0, self.size // 32)
        def _(i):
            at = pl.ds(pl.multiple_of(u * self.size + i * 32, 32), 32)
            total = self.grad[at, :].astype(F32)
            for slot in sources:
                here = pl.ds(pl.multiple_of(slot * self.size + i * 32, 32), 32)
                total = total + self.slots[here, :].astype(F32)
            self.grad[at, :] = total.astype(BF16)

    def combine(self):
        p = self.place
        if p.lines != 4:
            return

        @pl.when(~self.ends())
        def _():
            wait_bytes(self.chunk(self.slots, 0), self.recv_sem.at[2])
            self.add(jnp.where(p.u == 1, 3, 0), [p.u])
            self.line_each(lambda k, u: self.line_copy(k, u).start(), self.later)

    def group_copy(self, q):
        p = self.place
        j = (p.j + q) % TP
        block = self.grad.at[pl.ds((p.u * TP + j) * self.rows, self.rows)]
        return remote(block, self.out.at[p.j], self.send_sem.at[q], self.recv_sem.at[3], p.u * TP + j, p.t)

    def reduce(self):
        p = self.place
        if p.lines == 4:
            wait_bytes(self.slots.at[pl.ds(0, 2 * self.size)], self.recv_sem.at[0])
            pl.when(~self.ends())(lambda: wait_bytes(self.chunk(self.slots, 0), self.recv_sem.at[1]))
            pl.when(self.ends())(lambda: self.add(p.u, [1, 2]))
            pl.when(p.u == 1)(lambda: self.add(p.u, [0, 2, 3]))
            pl.when(p.u == 2)(lambda: self.add(p.u, [0, 1, 3]))
        else:
            wait_bytes(self.slots.at[pl.ds(0, (p.lines - 1) * self.size)], self.recv_sem.at[0])
            for k in range(1, p.lines):
                self.add(p.u, [(p.u + k) % p.lines])
        for q in (2, 3, 1):
            self.group_copy(q).start()
        own = self.grad.at[pl.ds(p.me * self.rows, self.rows)]
        pltpu.make_async_copy(own, self.out.at[p.j], self.recv_sem.at[3]).start()

    def finish(self):
        wait_bytes(self.out, self.recv_sem.at[3])
        for q in range(1, TP):
            self.group_copy(q).wait_send()
        self.line_each(lambda k, u: self.line_copy(k, u).wait_send())
        if self.place.lines == 4:
            pl.when(self.ends())(lambda: self.outer().wait_send())


def norm_stats(values):
    centre = values - jnp.mean(values, axis=-1, keepdims=True)
    inverse = lax.rsqrt(jnp.mean(centre * centre, axis=-1, keepdims=True) + 1e-05)
    return centre * inverse, inverse


def layer_kernel(
    count,
    small_src, aux_src, row_src, tok_src, cot_src, wq_src, wo_src, wga_src, wda_src, wgb_src, wdb_src,
    rs_q, rs_o, rs_ga, rs_da, rs_gb, rs_db, block_out, input_out, h1_out, norm_out, bias_out,
    wq, wo, wga, wda, wgb, wdb, cot, hh, qkv, att, hid, slopes, dga, dgb, gda, gga, gdb, ggb, go,
    slots_ga, slots_da, slots_db, slots_o,
    to_core, from_core, low, own, parts, grad, resid, gains, biases, norms,
    small, aux_all, row_all, small_all, bias_all, gains_t,
    w_send, w_recv, small_sem, aux_sem, row_sem, tok_sem, cot_sem, h1_sem,
    rs_send, rs_recv, free_g, free_q, core_sem, part_sem, free_sem, part2_sem, core2_sem, part3_sem, core3_sem,
    swap_sem, gain_sem, bias_sem, rank_sem, t_sem,
):
    p = Place(count)
    size = tok_src.shape[0]
    half = size // 2
    group = TP * size
    wide = att.shape[1]
    rows = wq_src.shape[1]
    first = wda.shape[1]
    second = hid.shape[1] - 128 - first
    greet(p)

    def rows_of(s):
        return pl.ds(pl.multiple_of(s * size, size), size)

    def columns(n, step):
        return pl.ds(pl.multiple_of(n * step, step), step)

    gathers = [
        WeightGather(p, i, src, dst, w_send, w_recv)
        for i, (src, dst) in enumerate(
            ((wq_src, wq), (wo_src, wo), (wga_src, wga), (wda_src, wda), (wgb_src, wgb), (wdb_src, wdb))
        )
    ]
    gather_q, gather_o, gather_ga, gather_da, gather_gb, gather_db = gathers
    tok = cot
    auxes = GroupPieces(p, aux_src, aux_all, aux_sem)
    rowses = GroupPieces(p, row_src, row_all, row_sem)
    tokens = GroupPieces(p, tok_src, tok, tok_sem, size)
    cots = GroupPieces(p, cot_src, cot, cot_sem, size)
    sums = GroupSum(p, to_core, from_core, low, own, parts, core_sem, part_sem, free_sem)
    spread_h = GroupGather(p, hh, size, part2_sem, core2_sem)
    spread_r = GroupGather(p, cot, size, part3_sem, core3_sem)
    gq = slopes.at[:D, : 3 * wide]
    scatters = [
        GradScatter(p, i, g, slots, out, rs_send, rs_recv, free)
        for i, (g, slots, out, free) in enumerate(
            (
                (gq, wga.at[:, : 3 * wide], rs_q, free_q),
                (go, slots_o, rs_o, None),
                (gga, slots_ga, rs_ga, None),
                (gda, slots_da, rs_da, None),
                (ggb, wgb, rs_gb, free_g),
                (gdb, slots_db, rs_db, None),
            )
        )
    ]
    scatter_q, scatter_o, scatter_ga, scatter_da, scatter_gb, scatter_db = scatters

    def small_copy(dest):
        return remote(small_src, small.at[p.me], small_sem.at[dest], small_sem.at[count], dest, p.t)

    pltpu.make_async_copy(small_src, small.at[p.me], small_sem.at[count]).start()
    each_dest(p, lambda dest, u, j: small_copy(dest).start())
    gather_q.start()
    auxes.start()
    rowses.start()
    gather_o.start()
    for part in gathers[2:4]:
        part.start()
    tokens.start()
    for part in gathers[4:]:
        part.start()
    for part in gathers[:4]:
        part.pass_on()
    auxes.pass_on()
    rowses.pass_on()
    tokens.pass_on()

    wait_bytes(small, small_sem.at[count])
    per_tile = 128 // rows
    for m in range(D // 128):
        tile = jnp.zeros((8, 128), F32)
        for i in range(per_tile):
            tile = tile + small[m * per_tile + i].astype(F32)[0:8]
        norms[0:8, m * 128 : (m + 1) * 128] = tile
    bias_rows = small.shape[1] - 16
    total = jnp.zeros((bias_rows, 128), F32)
    for d in range(count):
        total = total + small[d].astype(F32)[16:]
    for i in range(bias_rows):
        norms[8:9, i * 128 : (i + 1) * 128] = total[i : i + 1]
    auxes.arrive()
    rowses.arrive()
    gather_q.relay()
    tokens.arrive()

    @pl.loop(0, group // 32)
    def _(i):
        at = pl.ds(pl.multiple_of(i * 32, 32), 32)
        normed, _, _ = layer_norm(tok[at, :].astype(F32), norms[0:1, :D], norms[1:2, :D])
        hh[at, :] = normed.astype(BF16)

    tokens.finish()
    keep_h1 = pltpu.make_async_copy(hh, h1_out, h1_sem.at[0])
    keep_h1.start()
    gather_q.arrive()
    gather_gb.pass_on()
    gather_db.pass_on()
    gather_o.relay()
    head_wide = (bias_rows * 128) // 3

    @pl.loop(0, TP)
    def _(s):
        at = rows_of(s)
        proj = dot(hh[at, :], wq[...], 1, 0)
        tables = tables_of(aux_all[s], wide)

        def part(k):
            lanes = pl.ds(pl.multiple_of(k * head_wide + p.j * wide, 128), wide)
            return proj[:, k * wide : (k + 1) * wide] + norms[8:9, lanes]

        query = spin(part(0), *tables).astype(BF16)
        key = spin(part(1), *tables).astype(BF16)
        value = part(2).astype(BF16)
        qkv[at, :wide] = query
        qkv[at, wide : 2 * wide] = key
        qkv[at, 2 * wide :] = value
        allowed = mask_of(aux_all[s][:, ROT : ROT + 1], row_all[s, 0:1, :], size)
        att[at, :] = attend_values(query, key, value, allowed).astype(BF16)

    gather_o.arrive()
    keep_h1.wait()
    sums.start(lambda s, n, step: dot(att[rows_of(s), :], wo[columns(n, step), :], 1, 1))
    gather_ga.relay()
    sums.arrive()

    @pl.loop(0, half // 32)
    def _(i):
        at = pl.multiple_of(i * 32, 32)
        values = tok_src[pl.ds(pl.multiple_of(p.t * half + at, 32), 32), :].astype(F32)
        values = values + sums.total(at, 32)
        resid[pl.ds(at, 32), :] = values
        normed, _, _ = layer_norm(values, norms[2:3, :D], norms[3:4, :D])
        start = (p.j * 2 + p.t) * half + at
        hh[pl.ds(pl.multiple_of(start, 32), 32), :] = normed.astype(BF16)

    sums.release()
    spread_h.start()
    cots.start()
    spread_h.arrive()
    cots.pass_on()
    gather_da.relay()
    gather_gb.relay()
    gather_db.relay()
    step = min(256, D)

    def weight_grad(left, right, out):
        @pl.loop(0, D // step)
        def _(n):
            at = columns(n, step)
            out[at, :] = dot(left[:, at], right, 0, 0).astype(BF16)

    def late_rows(s):
        return pl.ds(pl.multiple_of(group + s * size, size), size)

    def hidden_part(weights, base, width, mixed):
        @pl.loop(0, TP)
        def _(s):
            at, late = rows_of(s), late_rows(s)
            rows_in = hh[at, :]
            lanes = slice(base, base + width)
            gate = dot(rows_in, weights[:, :width], 1, 0)
            up = dot(rows_in, weights[:, width : 2 * width], 1, 0)
            sig = jax.nn.sigmoid(gate)
            hid[at, lanes] = (gate * sig * up).astype(BF16)
            slopes[at, lanes] = (up * sig * (1.0 + gate * (1.0 - sig))).astype(BF16)
            slopes[late, lanes] = (gate * sig).astype(BF16)
            if mixed:
                gate = dot(rows_in, weights[:, 2 * width :], 1, 0)
                up = pltpu.roll(gate, 64, 1)
                sig = jax.nn.sigmoid(gate)
                left = lax.broadcasted_iota(jnp.int32, gate.shape, 1) < 64
                lanes = slice(base + width, base + width + 128)
                hid[at, lanes] = jnp.where(left, gate * sig * up, 0.0).astype(BF16)
                slopes[at, lanes] = jnp.where(left, up * sig * (1.0 + gate * (1.0 - sig)), 0.0).astype(BF16)
                slopes[late, lanes] = jnp.where(left, gate * sig, 0.0).astype(BF16)

    def gates_part(weights, base, width, mixed, out):
        @pl.loop(0, TP)
        def _(s):
            at, late = rows_of(s), late_rows(s)
            lanes = slice(base, base + weights.shape[1])
            dhid = dot(cot[at, :], weights[...], 1, 0)
            slope = dhid * slopes[at, lanes].astype(F32)
            gain = dhid * slopes[late, lanes].astype(F32)
            out[at, :width] = slope[:, :width].astype(BF16)
            out[at, width : 2 * width] = gain[:, :width].astype(BF16)
            if mixed:
                last = slope[:, width:] + pltpu.roll(gain[:, width:], 64, 1)
                out[at, 2 * width :] = last.astype(BF16)

    gather_ga.arrive()
    hidden_part(wga, 0, first, False)
    cots.arrive()
    weight_grad(cot, hid[:, :first], gda)
    scatter_da.start()
    gather_da.arrive()
    gates_part(wda, 0, first, False, dga)
    weight_grad(hh, dga[...], gga)
    scatter_ga.start()
    gather_gb.arrive()
    hidden_part(wgb, first, second, True)
    weight_grad(cot, hid[:, first:], gdb)
    scatter_db.start()
    gather_db.arrive()
    gates_part(wdb, first, second, True, dgb)

    cots.finish()
    sums.acquire()
    sums.start(
        lambda s, n, step: dot(dga[rows_of(s), :], wga[columns(n, step), :], 1, 1)
        + dot(dgb[rows_of(s), :], wgb[columns(n, step), :], 1, 1)
    )
    gather_gb.finish()
    gather_ga.finish()
    scatter_gb.allow()
    scatter_q.allow()
    weight_grad(hh, dgb[...], ggb)
    scatter_gb.start()
    spread_h.finish()
    load_h1 = pltpu.make_async_copy(h1_out, hh, h1_sem.at[1])
    load_h1.start()
    scatter_da.combine()
    scatter_ga.combine()
    sums.arrive()

    gains[...] = jnp.zeros_like(gains)

    @pl.loop(0, half // 32)
    def _(i):
        at = pl.multiple_of(i * 32, 32)
        scaled, inverse = norm_stats(resid[pl.ds(at, 32), :])
        part, gain, shift = norm_back(sums.total(at, 32), scaled, inverse, norms[2:3, :D])
        gains[2:3, :] += gain[None]
        gains[3:4, :] += shift[None]
        mine = pl.ds(pl.multiple_of((p.j * 2 + p.t) * half + at, 32), 32)
        total = cot[mine, :].astype(F32) + part
        grad[pl.ds(at, 32), :] = total
        cot[mine, :] = total.astype(BF16)

    sums.release()
    spread_r.start()
    spread_r.arrive()

    sums.acquire()
    sums.start(
        lambda s, n, step: dot(hid[rows_of(s), :first], wda[columns(n, step), :], 1, 1)
        + dot(hid[rows_of(s), first:], wdb[columns(n, step), :], 1, 1)
    )

    biases[...] = jnp.zeros_like(biases)

    @pl.loop(0, TP)
    def _(s):
        at = rows_of(s)
        grad_out = dot(cot[at, :], wo[...], 1, 0).astype(BF16)
        allowed = mask_of(aux_all[s][:, ROT : ROT + 1], row_all[s, 0:1, :], size)
        tables = tables_of(aux_all[s], wide)
        three = attend_back_values(
            qkv[at, :wide], qkv[at, wide : 2 * wide], qkv[at, 2 * wide :], grad_out, allowed, tables
        )
        for k, value in enumerate(three):
            lanes = slice(k * wide, (k + 1) * wide)
            qkv[at, lanes] = value
            biases[0:1, lanes] += jnp.sum(value.astype(F32), axis=0, keepdims=True)

    bias_all[p.u] = biases[...]

    def bias_copy(k):
        u = (p.u + k) % p.lines
        return remote(biases, bias_all.at[p.u], bias_sem.at[k], bias_sem.at[p.lines + k], u * TP + p.j, p.t)

    for k in range(1, p.lines):
        bias_copy(k).start()

    load_h1.wait()
    weight_grad(hh, qkv[...], gq)
    scatter_q.start_outer()
    weight_grad(cot, att[...], go)
    scatter_o.start_outer()
    scatter_q.start_rest()
    scatter_o.start_rest()
    scatter_db.combine()
    scatter_gb.combine()

    sums.arrive()

    @pl.loop(0, half // 32)
    def _(i):
        at = pl.multiple_of(i * 32, 32)
        resid[pl.ds(at, 32), :] += sums.total(at, 32)

    sums.release()
    mine = pl.ds(pl.multiple_of(p.t * half, half), half)

    def give(index, value, out):
        here = pltpu.make_async_copy(value, out.at[mine], swap_sem.at[index, 0])
        there = remote(value, out.at[mine], swap_sem.at[index, 1], swap_sem.at[index, 2], p.me, 1 - p.t)
        here.start()
        there.start()
        return here, there

    gives = [*give(1, resid, block_out)]

    sums.acquire()
    sums.start(lambda s, n, step: dot(qkv[rows_of(s), :], wq[columns(n, step), :], 1, 1))
    sums.arrive()

    @pl.loop(0, half // 32)
    def _(i):
        at = pl.multiple_of(i * 32, 32)
        values = tok_src[pl.ds(pl.multiple_of(p.t * half + at, 32), 32), :].astype(F32)
        scaled, inverse = norm_stats(values)
        part, gain, shift = norm_back(sums.total(at, 32), scaled, inverse, norms[0:1, :D])
        gains[0:1, :] += gain[None]
        gains[1:2, :] += shift[None]
        grad[pl.ds(at, 32), :] += part

    gives += give(0, grad, input_out)

    def tile_of(d):
        return pl.ds(pl.multiple_of(d * rows // 128 * 128, 128), 128)

    def gain_copy(dest):
        return remote(gains.at[:, tile_of(dest)], small_all.at[p.me], gain_sem.at[dest], gain_sem.at[count], dest, p.t)

    swap = remote(gains, gains_t, t_sem.at[0], t_sem.at[1], p.me, 1 - p.t)
    swap.start()
    swap.wait()
    gains[...] = gains[...] + gains_t[...]
    pltpu.make_async_copy(gains.at[:, tile_of(p.me)], small_all.at[p.me], gain_sem.at[count]).start()
    each_dest(p, lambda dest, u, j: gain_copy(dest).start())

    scatter_da.reduce()
    scatter_ga.reduce()
    scatter_q.combine()
    scatter_o.combine()
    scatter_db.reduce()
    scatter_gb.reduce()

    for k in range(1, p.lines):
        bias_copy(k).wait_recv()
    total = bias_all[0]
    for k in range(1, p.lines):
        total = total + bias_all[k]
    bias_out[p.j] = total

    def rank_copy(q):
        j = (p.j + q) % TP
        return remote(bias_out.at[p.j], bias_out.at[p.j], rank_sem.at[q], rank_sem.at[TP + q], p.u * TP + j, p.t)

    for q in range(1, TP):
        rank_copy(q).start()

    scatter_q.reduce()
    scatter_o.reduce()
    wait_bytes(small_all, gain_sem.at[count])
    total = small_all[0]
    for d in range(1, count):
        total = total + small_all[d]
    norm_out[...] = total
    for q in range(1, TP):
        rank_copy(q).wait()
    for k in range(1, p.lines):
        bias_copy(k).wait_send()
    each_dest(p, lambda dest, u, j: small_copy(dest).wait_send())
    each_dest(p, lambda dest, u, j: gain_copy(dest).wait_send())
    for copy in gives:
        copy.wait()
    for part in (auxes, rowses, sums, spread_r, gather_q, gather_o, gather_da, gather_db):
        part.finish()
    for scatter in scatters:
        scatter.finish()


def layer(count, small, aux, row, tokens, cot, *weights):
    size = tokens.shape[0]
    half = size // 2
    group = TP * size
    lines, rows = count // TP, weights[0].shape[1]
    _, wide, gates_a, hid_a, gates_b, hid_b = [w.shape[2] for w in weights]
    pad = hid_a + hid_b
    any_spec = pl.BlockSpec(memory_space=pl.ANY)
    vmem = pl.BlockSpec(memory_space=pltpu.VMEM)
    dma = pltpu.SemaphoreType.DMA
    regular = pltpu.SemaphoreType.REGULAR

    def out(*shape, dtype=BF16):
        return jax.ShapeDtypeStruct(shape, dtype)

    return pl.pallas_call(
        functools.partial(layer_kernel, count),
        in_specs=[vmem, vmem, vmem, vmem] + [any_spec] * 7,
        out_specs=[any_spec] * 9 + [vmem] * 2,
        out_shape=[
            *[out(TP, rows, w.shape[2]) for w in weights],
            out(size, D, dtype=F32),
            out(size, D, dtype=F32),
            out(group, D),
            out(8, 128, dtype=F32),
            out(TP, 8, 3 * wide, dtype=F32),
        ],
        scratch_shapes=[
            *[pltpu.VMEM((D, w.shape[2]), BF16) for w in weights],
            pltpu.VMEM((group, D), BF16),
            pltpu.VMEM((group, D), BF16),
            pltpu.VMEM((group, 3 * wide), BF16),
            pltpu.VMEM((group, wide), BF16),
            pltpu.VMEM((group, pad), BF16),
            pltpu.VMEM((max(2 * group, D), max(pad, 3 * wide)), BF16),
            pltpu.VMEM((group, gates_a), BF16),
            pltpu.VMEM((group, gates_b), BF16),
            pltpu.VMEM((D, hid_a), BF16),
            pltpu.VMEM((D, gates_a), BF16),
            pltpu.VMEM((D, hid_b), BF16),
            pltpu.VMEM((D, gates_b), BF16),
            pltpu.VMEM((D, wide), BF16),
            pltpu.VMEM((D, gates_a), BF16),
            pltpu.VMEM((D, hid_a), BF16),
            pltpu.VMEM((D, hid_b), BF16),
            pltpu.VMEM((D, wide), BF16),
            pltpu.VMEM((2, size, D), BF16),
            pltpu.VMEM((2, size, D), BF16),
            pltpu.VMEM((2, size, D), BF16),
            pltpu.VMEM((half, D), F32),
            pltpu.VMEM((3, half, D), BF16),
            pltpu.VMEM((half, D), F32),
            pltpu.VMEM((half, D), F32),
            pltpu.VMEM((8, D), F32),
            pltpu.VMEM((8, 3 * wide), F32),
            pltpu.VMEM((16, max(D, 128 * (small.shape[0] - 16))), F32),
            pltpu.VMEM((count,) + small.shape, BF16),
            pltpu.VMEM((TP, size, 128), F32),
            pltpu.VMEM((TP, 8, size), F32),
            pltpu.VMEM((count, 8, 128), F32),
            pltpu.VMEM((lines, 8, 3 * wide), F32),
            pltpu.VMEM((8, D), F32),
            dma((6, TP + lines)),
            dma((6, 4)),
            dma((count + 1,)),
            dma((2, 4)),
            dma((2, 4)),
            dma((2, 4)),
            dma((2, 4)),
            dma((2,)),
            dma((6, TP + lines)),
            dma((6, 4)),
            regular((lines,)),
            regular((lines,)),
            dma((2, 2)),
            dma((2, 4)),
            regular((4,)),
            dma((2, 4)),
            dma((2, 4)),
            dma((2, 4)),
            dma((2, 4)),
            dma((2, 3)),
            dma((count + 1,)),
            dma((2 * lines,)),
            dma((2 * TP,)),
            dma((2,)),
        ],
        compiler_params=pltpu.CompilerParams(
            collective_id=0, has_side_effects=True, vmem_limit_bytes=63 * 1024 * 1024
        ),
        cost_estimate=pl.CostEstimate(flops=40 * 10**9, bytes_accessed=60 * 10**6, transcendentals=10**7),
        name="layer",
    )(small, aux, row, tokens, cot, *weights)


def prepare_kernel(
    first, *refs,
):
    ins, outs = refs[:7], refs[7:16]
    held, made = refs[16:23], refs[23:32]
    lines, in_sem, out_sem = refs[32:]
    loads = [pltpu.make_async_copy(ref, here, in_sem.at[i]) for i, (ref, here) in enumerate(zip(ins, held))]
    stores = [pltpu.make_async_copy(here, ref, out_sem.at[i]) for i, (here, ref) in enumerate(zip(made, outs))]
    for copy in loads:
        copy.start()
    seg_ref, norm_ref, bias_ref, qkv_ref, out_ref, gates_ref, down_ref = held
    small, aux, row, wq, wo, wga, wda, wgb, wdb = made
    for copy in loads[:3]:
        copy.wait()
    size = seg_ref.shape[1]
    wide, second = wo.shape[2], (wgb.shape[2] - 128) // 2
    full = first + second
    me = lax.axis_index("dp")

    start = me * bias_ref.shape[1]
    wrapped = jnp.concatenate([bias_ref[...], jnp.zeros((1, 256 - bias_ref.shape[1]), F32)], axis=1)
    wrapped = pltpu.roll(jnp.broadcast_to(wrapped, (8, 256)), start % 128, 1)
    lines[...] = jnp.zeros_like(lines)
    lines[0:4, :] = norm_ref[...]
    lines[pl.ds(16 + start // 128, 1), :] = wrapped[0:1, :128]
    lines[pl.ds(17 + start // 128, 1), :] = wrapped[0:1, 128:]
    small[...] = lines[...].astype(BF16)

    seg = seg_ref[...].astype(F32)
    row[...] = jnp.broadcast_to(seg, row.shape)
    column = jnp.transpose(jnp.broadcast_to(seg, (128, size)))
    earlier = jnp.sum((seg < column[:, 0:1]).astype(F32), axis=1, keepdims=True)
    position = lax.broadcasted_iota(jnp.int32, (size, 128), 0).astype(F32) - earlier
    lane = lax.broadcasted_iota(jnp.int32, (size, 128), 1)
    half = ROT // 2
    frequency = jnp.zeros((size, 128), F32)
    for k in range(half):
        frequency = jnp.where(lane % half == k, 10000.0 ** (-2.0 * k / ROT), frequency)
    angles = position * frequency
    turned = jnp.where(lane < half, jnp.cos(angles), jnp.sin(angles))
    aux[...] = jnp.where(lane < ROT, turned, jnp.where(lane == ROT, column, 0.0))

    left = lax.broadcasted_iota(jnp.int32, (wq.shape[1], 128), 1) < 64
    for copy in stores[:3]:
        copy.start()
    loads[3].wait()
    for j in range(TP):
        for k in range(3):
            wq[j, :, k * wide : (k + 1) * wide] = qkv_ref[k, :, j * wide : (j + 1) * wide].astype(BF16)
    stores[3].start()
    loads[4].wait()
    for j in range(TP):
        wo[j] = jnp.transpose(out_ref[j * wide : (j + 1) * wide, :]).astype(BF16)
    stores[4].start()
    loads[5].wait()
    for j in range(TP):
        for k in range(2):
            begin = j * full
            wga[j, :, k * first : (k + 1) * first] = gates_ref[:, k, begin : begin + first].astype(BF16)
            wgb[j, :, k * second : (k + 1) * second] = gates_ref[:, k, begin + first : begin + full].astype(BF16)
        tile = slice(TP * full + j // 2 * 128, TP * full + j // 2 * 128 + 128)
        gate, up = gates_ref[:, 0, tile], gates_ref[:, 1, tile]
        if j % 2:
            gate = pltpu.roll(gate, 64, 1)
        else:
            up = pltpu.roll(up, 64, 1)
        wgb[j, :, 2 * second :] = jnp.where(left, gate, up).astype(BF16)
    stores[5].start()
    stores[7].start()
    loads[6].wait()
    for j in range(TP):
        wda[j] = jnp.transpose(down_ref[j * full : j * full + first, :]).astype(BF16)
        wdb[j, :, :second] = jnp.transpose(down_ref[j * full + first : (j + 1) * full, :]).astype(BF16)
        tile = slice(TP * full + j // 2 * 128, TP * full + j // 2 * 128 + 128)
        tail = jnp.transpose(down_ref[tile, :])
        if j % 2:
            tail = pltpu.roll(tail, 64, 1)
        wdb[j, :, second:] = jnp.where(left, tail, 0.0).astype(BF16)
    stores[6].start()
    stores[8].start()
    for copy in stores:
        copy.wait()


def prepare(first, seg, norm, bias, qkv, out, gates, down):
    rows, size = norm.shape[1], seg.shape[1]
    wide, hid = qkv.shape[2] // TP, down.shape[0] // TP
    second = hid // 128 * 128 - first
    lines = 16 + 3 * qkv.shape[2] // 128

    def shape(*dims, dtype=BF16):
        return jax.ShapeDtypeStruct(dims, dtype)

    given = (seg, norm, bias, qkv, out, gates, down)
    shapes = [
        shape(lines, 128),
        shape(size, 128, dtype=F32),
        shape(8, size, dtype=F32),
        shape(TP, rows, 3 * wide),
        shape(TP, rows, wide),
        shape(TP, rows, 2 * first),
        shape(TP, rows, first),
        shape(TP, rows, 2 * second + 128),
        shape(TP, rows, second + 128),
    ]
    return pl.pallas_call(
        functools.partial(prepare_kernel, first),
        in_specs=[pl.BlockSpec(memory_space=pl.ANY)] * 7,
        out_specs=[pl.BlockSpec(memory_space=pl.ANY)] * 9,
        out_shape=shapes,
        scratch_shapes=[pltpu.VMEM(x.shape, x.dtype) for x in (*given, *shapes)]
        + [pltpu.VMEM((lines, 128), F32), pltpu.SemaphoreType.DMA((7,)), pltpu.SemaphoreType.DMA((9,))],
        compiler_params=pltpu.CompilerParams(vmem_limit_bytes=60 * 1024 * 1024),
        name="prepare",
    )(*given)


def step_weights(weight, first, second, gradient, step_rate, decay_rate):
    first = 0.9 * first + 0.1 * gradient
    second = 0.95 * second + 0.05 * gradient * gradient
    corrected = first * (1.0 / (1.0 - 0.9**STEP)) / (jnp.sqrt(second * (1.0 / (1.0 - 0.95**STEP))) + 1e-08)
    return weight - step_rate * (corrected + decay_rate * weight), first, second


def update_kernel(*refs):
    ins, outs = refs[:18], refs[18:30]
    held = refs[30:48]
    in_sem, out_sem = refs[48:]
    loads = [pltpu.make_async_copy(ref, here, in_sem.at[i]) for i, (ref, here) in enumerate(zip(ins, held))]
    for copy in loads:
        copy.start()
    rs_q, rs_o, rs_ga, rs_gb, rs_da, rs_db = held[:6]
    states = [held[6 + 3 * i : 9 + 3 * i] for i in range(4)]
    stores = [
        pltpu.make_async_copy(here, ref, out_sem.at[i]) for i, (here, ref) in enumerate(zip(held[6:], outs))
    ]

    def ready(index, *gradients):
        for i in (*gradients, *range(6 + 3 * index, 9 + 3 * index)):
            loads[i].wait()

    def done(index):
        for copy in stores[3 * index : 3 * index + 3]:
            copy.start()

    def change(index, at, gradient, rate):
        new = step_weights(*(ref[at] for ref in states[index]), gradient, rate, 0.1)
        for ref, value in zip(states[index], new):
            ref[at] = value

    every = slice(None)
    wide = rs_o.shape[2]
    first, second = rs_da.shape[2], rs_db.shape[2] - 128
    full = first + second
    left = lax.broadcasted_iota(jnp.int32, (rs_gb.shape[1], 128), 1) < 64

    ready(0, 0)
    for k in range(3):
        for j in range(TP):
            gradient = rs_q[j, :, k * wide : (k + 1) * wide].astype(F32)
            change(0, (k, every, slice(j * wide, (j + 1) * wide)), gradient, D ** (-0.5))
    done(0)
    ready(2, 2, 3)
    for j in range(TP):
        for k in range(2):
            begin = j * full
            gradient = rs_ga[j, :, k * first : (k + 1) * first].astype(F32)
            change(2, (every, k, slice(begin, begin + first)), gradient, D ** (-0.5))
            gradient = rs_gb[j, :, k * second : (k + 1) * second].astype(F32)
            change(2, (every, k, slice(begin + first, begin + full)), gradient, D ** (-0.5))
    for i in range(TP // 2):
        even = rs_gb[2 * i, :, 2 * second :].astype(F32)
        odd = rs_gb[2 * i + 1, :, 2 * second :].astype(F32)
        tile = slice(TP * full + i * 128, TP * full + (i + 1) * 128)
        change(2, (every, 0, tile), jnp.where(left, even, pltpu.roll(odd, 64, 1)), D ** (-0.5))
        change(2, (every, 1, tile), jnp.where(left, pltpu.roll(even, 64, 1), odd), D ** (-0.5))
    done(2)
    ready(3, 4, 5)
    for j in range(TP):
        begin = j * full
        gradient = jnp.transpose(rs_da[j].astype(F32))
        change(3, (slice(begin, begin + first), every), gradient, FF ** (-0.5))
        gradient = jnp.transpose(rs_db[j].astype(F32))
        change(3, (slice(begin + first, begin + full), every), gradient[:second], FF ** (-0.5))
        begin = TP * full + j * 64
        change(3, (slice(begin, begin + 64), every), gradient[second : second + 64], FF ** (-0.5))
    done(3)
    ready(1, 1)
    for j in range(TP):
        gradient = jnp.transpose(rs_o[j].astype(F32))
        change(1, (slice(j * wide, (j + 1) * wide), every), gradient, (H * HD // 16) ** (-0.5))
    done(1)
    for copy in stores:
        copy.wait()


def update(gradients, states):
    given = (*gradients, *states)
    any_spec = pl.BlockSpec(memory_space=pl.ANY)
    return pl.pallas_call(
        update_kernel,
        in_specs=[any_spec] * 18,
        out_specs=[any_spec] * 12,
        out_shape=[jax.ShapeDtypeStruct(x.shape, x.dtype) for x in states],
        scratch_shapes=[pltpu.VMEM(x.shape, x.dtype) for x in given]
        + [pltpu.SemaphoreType.DMA((18,)), pltpu.SemaphoreType.DMA((12,))],
        compiler_params=pltpu.CompilerParams(vmem_limit_bytes=60 * 1024 * 1024),
        name="update",
    )(*given)


def laid_out(values):
    return with_layout_constraint(values, Layout(tuple(range(values.ndim))))


def per_device(
    count,
    tokens_in,
    segment_ids,
    d_out,
    qkv_weight,
    qkv_bias,
    out_weight,
    gating_weight,
    down_weight,
    norm_params,
    qkv_first,
    qkv_second,
    bias_first,
    bias_second,
    out_first,
    out_second,
    gating_first,
    gating_second,
    down_first,
    down_second,
    norm_first,
    norm_second,
):
    place = lax.axis_index("dp")
    rows = norm_params.shape[1]
    seq_len = tokens_in.shape[1]
    head_local = qkv_weight.shape[2]
    hidden_local = gating_weight.shape[2]
    wide = head_local // TP
    hid = hidden_local // TP
    full = hid // 128 * 128

    first = -(-(full // 2) // 128) * 128
    spare = hid - full
    bias_here = qkv_bias.shape[1]
    if rows % 128 == 0 and spare == 64 and bias_here <= 192:
        small, aux, row, *weights = prepare(
            first, segment_ids, norm_params, qkv_bias, qkv_weight.transpose(1, 0, 2), out_weight, gating_weight, down_weight
        )
    else:
        low_gates = laid_out(gating_weight.astype(BF16))

        def gate_cut(k, start, width):
            return [low_gates[:, k, j * width + start : (j + 1) * width + start] for j in range(TP)]

        def ranks(parts):
            return jnp.stack([jnp.concatenate(one, axis=1) for one in zip(*parts, strict=True)])

        low_down = down_weight.astype(BF16)
        down_full = low_down[: TP * full].reshape(TP, full, rows)
        gate_full = [[low_gates[:, k, j * full : (j + 1) * full] for j in range(TP)] for k in range(2)]
        weights = (
            ranks([[qkv_weight[:, k, j * wide : (j + 1) * wide] for j in range(TP)] for k in range(3)]).astype(BF16),
            out_weight.astype(BF16).reshape(TP, wide, rows).transpose(0, 2, 1),
            ranks([[part[:, :first] for part in gate_full[k]] for k in range(2)]),
            down_full[:, :first].transpose(0, 2, 1),
            ranks([[part[:, first:] for part in gate_full[k]] for k in range(2)] + [gate_cut(k, TP * full, spare) for k in range(2)]),
            jnp.concatenate(
                [
                    down_full[:, first:],
                    low_down[TP * full :].reshape(TP, spare, rows),
                    jnp.zeros((TP, -hid % 128, rows), BF16),
                ],
                axis=1,
            ).transpose(0, 2, 1),
        )
        small_norm = lax.dynamic_update_slice(jnp.zeros((16, 128), F32), norm_params, (0, (place * rows) % 128))
        small_bias = lax.dynamic_update_slice(jnp.zeros((3 * head_local,), F32), qkv_bias[0], (place * bias_here,))
        small = jnp.concatenate([small_norm, small_bias.reshape(-1, 128)]).astype(BF16)
        segments = segment_ids[0]
        earlier = jnp.sum((segments[None, :] < segments[:, None]).astype(jnp.int32), axis=1)
        positions = (jnp.arange(seq_len, dtype=jnp.int32) - earlier).astype(F32)
        frequency = 10000.0 ** (-2.0 * jnp.arange(ROT // 2, dtype=F32) / ROT)
        angles = positions[:, None] * frequency[None, :]
        aux = jnp.concatenate([jnp.cos(angles), jnp.sin(angles), segments[:, None].astype(F32)], axis=1)
        aux = jnp.pad(aux, ((0, 0), (0, 128 - aux.shape[1])))
        row = jnp.broadcast_to(segments.astype(F32)[None], (8, seq_len))

    rs_q, rs_o, rs_ga, rs_da, rs_gb, rs_db, block_out, input_grad, _, norm_sum, bias_sum = layer(
        count, small, aux, row, tokens_in[0], d_out[0], *weights
    )

    norm_grad = lax.dynamic_slice_in_dim(norm_sum[:4], (place * rows) % 128, rows, 1)
    bias_grad = bias_sum[:, 0].reshape(TP, 3, wide).transpose(1, 0, 2).reshape(1, 3 * head_local)
    bias_grad = lax.dynamic_slice_in_dim(bias_grad, place * bias_here, bias_here, 1)
    if rows % 128 == 0 and spare == 64 and bias_here <= 192:
        planes = [x.transpose(1, 0, 2) for x in (qkv_weight, qkv_first, qkv_second)]
        new = update(
            (rs_q, rs_o, rs_ga, rs_gb, rs_da, rs_db),
            (*planes, out_weight, out_first, out_second, gating_weight, gating_first, gating_second)
            + (down_weight, down_first, down_second),
        )
        new_qkv, new_out, new_gating, new_down = [x.transpose(1, 0, 2) for x in new[:3]], new[3:6], new[6:9], new[9:]
    else:
        second = full - first
        gate_parts = [
            jnp.concatenate(
                [
                    part
                    for j in range(TP)
                    for part in (
                        rs_ga[j, :, k * first : (k + 1) * first],
                        rs_gb[j, :, k * second : (k + 1) * second],
                    )
                ]
                + [rs_gb[j, :, 2 * second + k * spare : 2 * second + (k + 1) * spare] for j in range(TP)],
                axis=1,
            )
            for k in range(2)
        ]
        gating_shard = lax.optimization_barrier(laid_out(jnp.stack(gate_parts, axis=1))).astype(F32)
        qkv_shard = jnp.stack(
            [
                jnp.concatenate([rs_q[j, :, k * wide : (k + 1) * wide] for j in range(TP)], axis=1)
                for k in range(3)
            ],
            axis=1,
        ).astype(F32)
        out_shard = laid_out(rs_o.transpose(0, 2, 1).reshape(head_local, rows)).astype(F32)
        down_parts = jnp.concatenate([rs_da, rs_db], axis=2).transpose(0, 2, 1)
        down_shard = laid_out(
            jnp.concatenate(
                [down_parts[:, :full].reshape(TP * full, rows), down_parts[:, full:hid].reshape(TP * spare, rows)]
            )
        ).astype(F32)
        new_qkv = adamw_update(qkv_weight, qkv_shard, qkv_first, qkv_second, D ** (-0.5), 0.1)
        new_out = adamw_update(out_weight, out_shard, out_first, out_second, (H * HD // 16) ** (-0.5), 0.1)
        new_gating = adamw_update(gating_weight, gating_shard, gating_first, gating_second, D ** (-0.5), 0.1)
        new_down = adamw_update(down_weight, down_shard, down_first, down_second, FF ** (-0.5), 0.1)
    return (
        block_out[None],
        input_grad[None],
        *new_qkv,
        *adamw_update(qkv_bias, bias_grad, bias_first, bias_second, 0.3, 0.0),
        *new_out,
        *new_gating,
        *new_down,
        *adamw_update(norm_params, norm_grad, norm_first, norm_second, 0.25, 0.0),
    )


def solution(mesh):
    tokens = P("dp", None, None)
    qkv = P("dp", None, "tensor")
    rest = P("tensor", "dp")
    norm = P(None, "dp")
    weights = (qkv, rest, rest, qkv, rest, norm)
    states = (qkv, qkv, rest, rest, rest, rest, qkv, qkv, rest, rest, norm, norm)
    return jax.shard_map(
        functools.partial(per_device, mesh.shape["dp"]),
        mesh=mesh,
        in_specs=(tokens, P("dp", None), tokens, *weights, *states),
        out_specs=(tokens, tokens, *(spec for spec in weights for _ in range(3))),
        check_vma=False,
    )
```
